32 devices in a mesh: gx: 8 (over z, core), gy: 4 (over y, x).
Axes of the slice: x: 2, y: 2, z: 4, core: 2. Of those that a mesh axis runs over, the one named last changes fastest.
Arguments:
- u_field: float32 [256, 1024], P('gx', 'gy'), may hold values from -6 to 6
- v_field: float32 [256, 1024], P('gx', 'gy'), may hold values from -6 to 6
- w_first: bfloat16 [9, 64, 2], replicated, may hold values from -1.5 to 1.5
- b_first: float32 [64], replicated, may hold values from -3 to 3
- w_second: bfloat16 [9, 64, 64], replicated, may hold values from -0.25 to 0.25
- b_second: float32 [64], replicated, may hold values from -3 to 3
- w_third: bfloat16 [9, 16, 64], replicated, may hold values from -0.25 to 0.25
- b_third: float32 [16], replicated, may hold values from -3 to 3
Outputs:
- u_next: float32 [256, 1024], P('gx', 'gy')
- v_next: float32 [256, 1024], P('gx', 'gy')
The draws below stay inside these ranges and needn't reach their ends.
All inputs are finite; a program needn't handle non-finite values.
Results may differ from the reference program's by a relative error of at most 0.0023.
Values sent between devices are 32-bit elements; how exact they have to be, the bound alone decides.
No kernel may reach another device: no remote copies, remote signals or barrier semaphores. Data moves between devices by JAX's collectives and lax.ppermute only.
A program may use at most 64 MiB of HBM per device.

```python
import math
import jax
import jax.numpy as jnp
from jax import lax

CX = 32
CH = 64
NOUT = 16
NX = 256
NY = 1024
N_GX = 8


def levels(key, dims, pieces, least, top_value):
    loudness, own = 1.0, jax.random.fold_in(key, 6)
    for dim, blocks in pieces:
        draws = jnp.exp(jax.random.uniform(jax.random.fold_in(own, dim), (blocks,), jnp.float32, least / len(pieces), top_value / len(pieces)))
        loudness = loudness * jnp.repeat(draws, dims[dim] // blocks).reshape([-1 if axis == dim else 1 for axis in range(len(dims))])
    return loudness


def gaussian(stream_key, extent, width, reach, cuts=(), held_as=jnp.bfloat16):
    drawn = width * jax.random.normal(stream_key, extent, jnp.float32)
    if cuts:
        drawn = drawn * levels(stream_key, extent, cuts, -0.22, 0.18)
    return jnp.clip(drawn, -reach, reach).astype(held_as)


def setup_inputs(seed: int = 0) -> dict:
    key_of = jax.random.split(jax.random.key(seed), 9)
    return {
        "u_field": gaussian(key_of[0], (NX, NY), 1.0, 6.0, ((0, 8), (1, 4)), jnp.float32),
        "v_field": gaussian(key_of[1], (NX, NY), 1.0, 6.0, ((0, 8), (1, 4)), jnp.float32),
        "w_first": gaussian(key_of[2], (9, CH, 2), 18 ** -0.5, 1.5),
        "b_first": gaussian(key_of[3], (CH,), 0.5, 3.0, (), jnp.float32),
        "w_second": gaussian(key_of[4], (9, CH, CH), (9 * CH) ** -0.5, 0.25),
        "b_second": gaussian(key_of[5], (CH,), 0.5, 3.0, (), jnp.float32),
        "w_third": gaussian(key_of[6], (9, NOUT, CH), (9 * CH) ** -0.5, 0.25),
        "b_third": gaussian(key_of[7], (NOUT,), 0.5, 3.0, (), jnp.float32),
    }


step_ratio = 0.4
stencil_base = (-0.0625, 0.5625, 0.5625, -0.0625)


def conv_layer(inputs, kernel, offsets):
    weights = kernel.astype(jnp.float32).reshape(3, 3, kernel.shape[1], kernel.shape[2]).transpose(2, 3, 0, 1)
    output = lax.conv_general_dilated(inputs.astype(jnp.float32)[None], weights, (1, 1), "VALID", dimension_numbers=("NCHW", "OIHW", "NCHW"), precision=lax.Precision.HIGHEST)[0]
    return output + offsets[:, None, None]


def shifted(values, shift_down, shift_right):
    return jnp.roll(values, (-shift_down, -shift_right), axis=(1, 2))


def wavenumber(counter, whole):
    signed = jnp.where(counter >= whole // 2, counter - whole, counter)
    return signed.astype(jnp.float32) * (2.0 * math.pi / whole)


def reference(u_field, v_field, w_first, b_first, w_second, b_second, w_third, b_third):
    field = jnp.stack([u_field, v_field])
    features = jnp.pad(field.astype(jnp.bfloat16), ((0, 0), (3, 3), (3, 3)), mode="wrap")

    def band(position):
        inputs = lax.dynamic_slice_in_dim(features, position * CX, CX + 6, axis=1)
        first = jax.nn.relu(conv_layer(inputs, w_first, b_first)).astype(jnp.bfloat16)
        second = jax.nn.relu(conv_layer(first, w_second, b_second)).astype(jnp.bfloat16)
        return conv_layer(second, w_third, b_third)

    coeff = lax.map(band, jnp.arange(N_GX, dtype=jnp.int32))
    coeff = jnp.transpose(coeff, (1, 0, 2, 3)).reshape(NOUT, NX, NY)
    weights = coeff.reshape(2, 2, 4, NX, NY)
    weights = jnp.asarray(stencil_base, jnp.float32)[:, None, None] + weights - jnp.mean(weights, axis=2, keepdims=True)
    east = weights[0, :, 0] * shifted(field, -1, 0) + weights[0, :, 1] * field + weights[0, :, 2] * shifted(field, 1, 0) + weights[0, :, 3] * shifted(field, 2, 0)
    north = weights[1, :, 0] * shifted(field, 0, -1) + weights[1, :, 1] * field + weights[1, :, 2] * shifted(field, 0, 1) + weights[1, :, 3] * shifted(field, 0, 2)
    carry_x = 0.5 * (field[0] + shifted(field, 1, 0)[0])
    carry_y = 0.5 * (field[1] + shifted(field, 0, 1)[1])
    flow_x = carry_x * east
    flow_y = carry_y * north
    star = field - step_ratio * (flow_x - shifted(flow_x, -1, 0) + flow_y - shifted(flow_y, 0, -1))
    spectra = jnp.fft.fft2(star, axes=(1, 2))
    wave_x = wavenumber(jnp.arange(NX, dtype=jnp.int32), NX)[:, None]
    wave_y = wavenumber(jnp.arange(NY, dtype=jnp.int32), NY)[None, :]
    denominator = wave_x * wave_x + wave_y * wave_y
    denominator = jnp.where(denominator == 0, 1.0, denominator)
    share = (wave_x * spectra[0] + wave_y * spectra[1]) / denominator
    projected = jnp.stack([spectra[0] - wave_x * share, spectra[1] - wave_y * share])
    result = jnp.fft.ifft2(projected, axes=(1, 2)).real
    return result[0].astype(jnp.float32), result[1].astype(jnp.float32)
```

```python
import functools
import math

import jax
import jax.numpy as jnp
import ml_dtypes
import numpy as np
from jax import lax
from jax.experimental import pallas as pl
from jax.experimental.pallas import tpu as pltpu
from jax.sharding import PartitionSpec as P

step_ratio = 0.4
stencil_base = (-0.0625, 0.5625, 0.5625, -0.0625)
f32 = jnp.float32
bf16 = jnp.bfloat16

vmem_limit = 48 * 1024 * 1024


def split(value):
    high = value.astype(bf16)
    return high, (value - high.astype(f32)).astype(bf16)


def split_table(table):
    high = table.astype(ml_dtypes.bfloat16)
    low = (table - high.astype(np.float64)).astype(ml_dtypes.bfloat16)
    return high, low


def dot(a, b):
    return jnp.dot(a, b, preferred_element_type=f32)


def product_3(value, high, low):
    rows = value.shape[0]
    first, second = split(value)
    both = dot(jnp.concatenate([first, second], axis=0), high)
    return both[:rows] + both[rows:] + dot(first, low)


def parity(shape):
    rows = lax.broadcasted_iota(jnp.int32, shape, 0)
    return jnp.where(rows % 8 < 4, 1.0, -1.0).astype(f32)


def swap(value):
    rows = value.shape[0]
    lower = lax.broadcasted_iota(jnp.int32, value.shape, 0) % 8 < 4
    return jnp.where(lower, pltpu.roll(value, rows - 4, 0), pltpu.roll(value, 4, 0))


def advance_kernel(
    u_ref, v_ref, bot_ref, top_ref, right_ref, left_ref, w1_ref, w2_ref, w3e_ref, w3o_ref,
    b1_ref, b2_ref, b3_ref, star_ref, field, first, second, coeff,
):
    height, breadth = u_ref.shape
    rows = height + 8
    groups = rows // 4
    lanes = breadth + 128
    field[:, :, breadth:] = jnp.zeros((2, rows + 16, 128), f32)
    for q, ref in enumerate((u_ref, v_ref)):
        field[q, 8 : 8 + height, :breadth] = ref[...]
        field[q, 8 + height : 12 + height, :breadth] = bot_ref[q]
        field[q, 12 + height : 16 + height, :breadth] = top_ref[q]
        field[q, 8 : 8 + rows, breadth : breadth + 4] = right_ref[q]
        field[q, 8 : 8 + rows, lanes - 4 : lanes] = left_ref[q]
        field[q, 0:8, :] = field[q, rows : rows + 8, :]
        field[q, 8 + rows : 16 + rows, :] = field[q, 8:16, :]
    whole = jnp.concatenate([field[0, 8 : 8 + rows], field[1, 8 : 8 + rows]], axis=0)
    pieces = [pltpu.roll(whole, 1, 1), whole, pltpu.roll(whole, lanes - 1, 1)]
    depth = w1_ref.shape[1]
    pieces.append(jnp.zeros((depth - 6 * rows, lanes), f32))
    turned = jnp.concatenate(pieces, axis=0).T
    patches = jnp.concatenate([turned[: breadth + 8], turned[lanes - 8 :]], axis=0).astype(bf16)
    span = breadth + 16
    for r in range(groups):
        first[r] = jnp.maximum(dot(patches, w1_ref[r]) + b1_ref[...], 0.0).astype(bf16)

    def gathered(source, r):
        before, after = (r - 1) % groups, (r + 1) % groups
        beside = jnp.concatenate([source[before, :, 128:], source[after, :, :128]], axis=1)
        return source[r], beside

    for r in range(groups):
        own, beside = gathered(first, r)
        total = dot(own, w2_ref[:256]) + dot(beside, w2_ref[256:])
        total = pltpu.roll(total[:, :256], 1, 0) + total[:, 256:512] + pltpu.roll(total[:, 512:], span - 1, 0)
        second[r] = jnp.maximum(total + b2_ref[...], 0.0).astype(bf16)

    def last(r, ref):
        own, beside = gathered(second, r)
        total = dot(own, ref[:256]) + dot(beside, ref[256:])
        left_part = total[:, :128]
        return pltpu.roll(left_part, 1, 0) + pltpu.roll(left_part, 64, 1) + pltpu.roll(total[:, 128:], span - 1, 0)

    def keep(r, block):
        coeff[r, :, :breadth] = block[:, :breadth]
        coeff[r, :, breadth:] = block[:, breadth:]

    pairs = [(i, i + 1) for i in range(0, groups - 2, 2)] + [(groups - 1, None)]
    for even, odd in pairs:
        block = last(even, w3e_ref)
        if odd is not None:
            other = last(odd, w3o_ref)
            lower = lax.broadcasted_iota(jnp.int32, block.shape, 1) < 64
            block = jnp.where(lower, block, other)
        block = jnp.concatenate(
            [block[: breadth + 8], jnp.zeros((lanes - span, 128), f32), block[breadth + 8 :]], axis=0
        ).T
        keep(even, block[:64])
        if odd is not None:
            keep(odd, block[64:])

    offsets = b3_ref[...]
    sub = lax.broadcasted_iota(jnp.int32, (8, breadth), 0) % 4

    def stacked(r, shift, qs=(0, 1)):
        start = 8 + 4 * r + shift
        return jnp.concatenate([field[q, start : start + 4, :] for q in qs], axis=0)

    previous = None
    for r in [groups - 1] + list(range(groups - 2)):
        weights = coeff[r] + offsets
        weights = [weights[8 * i : 8 * i + 8] for i in range(8)]
        centre = stacked(r, 0)

        def stencil(d):
            four = weights[4 * d : 4 * d + 4]
            mean = (four[0] + four[1] + four[2] + four[3]) * 0.25
            return [base + w - mean for base, w in zip(stencil_base, four)]

        east = stencil(0)
        flow_x = (
            east[0] * stacked(r, -1) + east[1] * centre + east[2] * stacked(r, 1) + east[3] * stacked(r, 2)
        )
        flow_x = flow_x * (0.5 * (stacked(r, 0, (0, 0)) + stacked(r, 1, (0, 0))))
        flow_x = flow_x[:, :breadth]
        if previous is not None:
            north = stencil(1)
            flow_y = (
                north[0] * pltpu.roll(centre, 1, 1)
                + north[1] * centre
                + north[2] * pltpu.roll(centre, lanes - 1, 1)
                + north[3] * pltpu.roll(centre, lanes - 2, 1)
            )
            carrier = stacked(r, 0, (1, 1))
            flow_y = flow_y * (0.5 * (carrier + pltpu.roll(carrier, lanes - 1, 1)))
            change_y = (flow_y - pltpu.roll(flow_y, 1, 1))[:, :breadth]
            above = jnp.where(sub == 0, pltpu.roll(previous, 5, 0), pltpu.roll(flow_x, 1, 0))
            star_ref[8 * r : 8 * r + 8, :] = centre[:, :breadth] - step_ratio * (flow_x - above + change_y)
        previous = flow_x


def column_kernel(blocks_ref, cos_ref, sin_ref, high_ref, low_ref, out_ref):
    count, rows, breadth = blocks_ref.shape
    sign = parity((rows, breadth))
    mixed = None
    for b in range(count):
        block = blocks_ref[b] * sign
        term = block * cos_ref[b : b + 1, :] + swap(block) * (sign * sin_ref[b : b + 1, :])
        mixed = term if mixed is None else mixed + term
    spectra = product_3(mixed, high_ref[...], low_ref[...])
    out_ref[...] = spectra[:, :breadth] + sign * swap(spectra[:, breadth:])


def row_kernel(
    gathered_ref, fwd_ref, fwd_low_ref, inv_ref, inv_low_ref, high_ref, low_ref, wave_ref, out_ref, *, scale
):
    length = gathered_ref.shape[0] // 2
    breadth = gathered_ref.shape[1]
    data, data_low = split(gathered_ref[...])
    spectra = dot(fwd_ref[...], data) + dot(fwd_ref[...], data_low) + dot(fwd_low_ref[...], data)
    real_part, imag_part = spectra[:length], spectra[length:]
    index = lax.broadcasted_iota(jnp.int32, (length, breadth), 0)
    wave_x = jnp.where(index >= length // 2, index - length, index).astype(f32) * (2.0 * math.pi / length)
    wave_y = wave_ref[0:1, :]
    edge_y = wave_ref[1:2, :] > 0.5
    edge_x = index == length // 2
    total = wave_x * wave_x + wave_y * wave_y
    zero = total == 0.0
    inverse = scale / jnp.where(zero, 1.0, total)
    same = (0.5 * inverse) * (wave_y * wave_y - wave_x * wave_x)
    cross = jnp.where(edge_x != edge_y, 0.0, -inverse * wave_x * wave_y)
    same_real = jnp.where(zero, 0.5 * scale, same)
    same_imag = jnp.where(zero, -0.5 * scale, same)
    kept_real = same_real * real_part - cross * imag_part
    kept_imag = same_imag * imag_part + cross * real_part
    kept, kept_low = split(jnp.concatenate([kept_real, kept_imag], axis=0))
    home = dot(inv_ref[...], kept) + dot(inv_ref[...], kept_low) + dot(inv_low_ref[...], kept)
    columns = product_3(home, high_ref[...], low_ref[...])
    rows = home.shape[0]
    out_ref[...] = columns[:, :breadth] - parity((rows, breadth)) * swap(columns[:, breadth:])


def home_kernel(blocks_ref, cos_ref, sin_ref, star_ref, u_ref, v_ref):
    count, rows, breadth = blocks_ref.shape
    sign = parity((rows, breadth))
    result = 0.5 * star_ref[...]
    for b in range(count):
        block = blocks_ref[b]
        result = result + block * cos_ref[b : b + 1, :] - swap(block) * (sign * sin_ref[b : b + 1, :])
    for r in range(rows // 8):
        u_ref[4 * r : 4 * r + 4, :] = result[8 * r : 8 * r + 4]
        v_ref[4 * r : 4 * r + 4, :] = result[8 * r + 4 : 8 * r + 8]


def call(kernel, shapes, scratch=(), flops=10**7):
    return pl.pallas_call(
        kernel,
        out_shape=shapes,
        scratch_shapes=list(scratch),
        compiler_params=pltpu.CompilerParams(vmem_limit_bytes=vmem_limit),
        cost_estimate=pl.CostEstimate(flops=flops, bytes_accessed=2**20, transcendentals=0),
    )


@functools.lru_cache(None)
def tables(height, breadth, members_x, members_y):
    turn = 2.0 * math.pi
    j = np.arange(breadth)
    phase = turn * (np.outer(j, j) % breadth) / breadth
    column = split_table(np.concatenate([np.cos(phase), np.sin(phase)], axis=1))
    length = height * members_x
    k = np.arange(length)
    phase = turn * (np.outer(k, k) % length) / length
    cosine = np.cos(phase).reshape(length, length // 4, 1, 4)
    sine = np.sin(phase).reshape(length, length // 4, 1, 4)
    real_rows = np.concatenate([cosine, sine], axis=2).reshape(length, 2 * length)
    imag_rows = np.concatenate([-sine, cosine], axis=2).reshape(length, 2 * length)
    forward = np.concatenate([real_rows, imag_rows], axis=0)
    forward_pair = split_table(forward)
    backward_pair = split_table(np.ascontiguousarray(forward.T))
    g = np.arange(members_y)
    count = np.multiply.outer(np.outer(g, g) * breadth, np.ones(breadth, np.int64)) + np.outer(
        np.ones(members_y, np.int64), j
    )[None] * g[None, :, None]
    phase = turn * (count % (breadth * members_y)) / (breadth * members_y)
    twiddle = np.stack([np.cos(phase), np.sin(phase)]).astype(np.float32)
    return column, forward_pair, backward_pair, twiddle


def own_part(table, index):
    return lax.dynamic_index_in_dim(jnp.asarray(table), index, 0, keepdims=False)


def stacked_weights(w_first, w_second, w_third, rows):
    groups = rows // 4
    taps_1 = w_first.astype(f32).reshape(3, 3, 64, 2).transpose(0, 1, 3, 2)
    wide = jnp.concatenate([taps_1] * 4, axis=-1).reshape(3, 6, 1, 256)
    wide = jnp.broadcast_to(wide, (3, 6, rows, 256)).reshape(3, 6 * rows, 256)
    depth = -(-6 * rows // 128) * 128
    wide = jnp.pad(wide, ((0, 0), (0, depth - 6 * rows), (0, 0)))
    place = (
        lax.broadcasted_iota(jnp.int32, (depth, 256), 0) % rows
        - lax.broadcasted_iota(jnp.int32, (depth, 256), 1) // 64
        + rows
    )
    group = jnp.arange(groups, dtype=jnp.int32)[:, None, None]
    kernel_1 = sum(
        jnp.where((place[None] - 4 * group + 2 * rows - d + 1) % rows == 0, wide[d][None], 0.0) for d in range(3)
    ).astype(bf16)
    choose = np.zeros((3, 8, 4), np.float32)
    for t in range(4):
        for d in range(3):
            source = t + d - 1
            slot = 5 if source < 0 else 6 if source > 3 else source
            choose[d, slot, t] = 1.0
    choose = jnp.asarray(choose, bf16)
    taps_2 = w_second.reshape(3, 3, 64, 64)
    kernel_2 = jnp.einsum("dkt,dcoi->kicto", choose, taps_2, preferred_element_type=f32)
    kernel_2 = kernel_2.astype(bf16).reshape(512, 768)
    order = np.array([8 * d + 4 * q + s for d in range(2) for s in range(4) for q in range(2)])
    taps_3 = w_third.reshape(3, 3, 16, 64)[:, :, order]
    kernel_3 = jnp.einsum("dkt,dcoi->kicot", choose, taps_3, preferred_element_type=f32)
    kernel_3 = kernel_3.astype(bf16).reshape(512, 3, 64)
    blank = jnp.zeros((512, 64), bf16)
    even = jnp.concatenate([kernel_3[:, 0], kernel_3[:, 1], kernel_3[:, 2], blank], axis=1)
    odd = jnp.concatenate([kernel_3[:, 1], kernel_3[:, 0], blank, kernel_3[:, 2]], axis=1)
    return kernel_1, kernel_2, even, odd, order


def gather(block, axis):
    return lax.all_gather(block, axis, axis=0, tiled=False)


def on_device(u_field, v_field, w_first, b_first, w_second, b_second, w_third, b_third):
    height, breadth = u_field.shape
    members_x, members_y = lax.axis_size("gx"), lax.axis_size("gy")
    index_x, index_y = lax.axis_index("gx"), lax.axis_index("gy")
    grid_x, grid_y = height * members_x, breadth * members_y
    rows = height + 8

    def shifted(value, axis, distance):
        peers = lax.axis_size(axis)
        return lax.ppermute(value, axis, [(i, (i + distance) % peers) for i in range(peers)])

    top = shifted(jnp.stack([u_field[-4:], v_field[-4:]]), "gx", 1)
    bottom = shifted(jnp.stack([u_field[:4], v_field[:4]]), "gx", -1)

    def edge(part):
        centre = jnp.stack([part(u_field), part(v_field)])
        return jnp.concatenate([centre, part(bottom), part(top)], axis=1)

    left = shifted(edge(lambda a: a[..., -4:]), "gy", 1)
    right = shifted(edge(lambda a: a[..., :4]), "gy", -1)

    kernel_1, kernel_2, even, odd, order = stacked_weights(w_first, w_second, w_third, rows)
    bias_1 = jnp.tile(b_first, 4)[None]
    bias_2 = jnp.tile(b_second, 4)[None]
    bias_3 = jnp.repeat(b_third[order], 4)[:, None]
    groups = rows // 4
    span = breadth + 16
    block = jax.ShapeDtypeStruct((2 * height, breadth), f32)
    star = call(
        advance_kernel,
        block,
        (
            pltpu.VMEM((2, rows + 16, breadth + 128), f32),
            pltpu.VMEM((groups, span, 256), bf16),
            pltpu.VMEM((groups, span, 256), bf16),
            pltpu.VMEM((groups, 64, breadth + 128), f32),
        ),
        flops=10**9,
    )(u_field, v_field, bottom, top, right, left, kernel_1, kernel_2, even, odd, bias_1, bias_2, bias_3)

    column, forward, backward, twiddle = tables(height, breadth, members_x, members_y)
    cosine, sine = own_part(twiddle[0], index_y), own_part(twiddle[1], index_y)
    turned = twiddle.transpose(0, 2, 1, 3)
    cosine_out, sine_out = own_part(turned[0], index_y), own_part(turned[1], index_y)
    column = [jnp.asarray(t) for t in column]
    spectra = call(column_kernel, block)(gather(star, "gy"), cosine_out, sine_out, *column)
    number_y = index_y + members_y * jnp.arange(breadth, dtype=jnp.int32)
    wave_y = jnp.where(number_y >= grid_y // 2, number_y - grid_y, number_y).astype(f32) * (2.0 * math.pi / grid_y)
    wave = jnp.stack([wave_y, (number_y == grid_y // 2).astype(f32)])
    back = [
        lax.dynamic_slice_in_dim(jnp.asarray(t), index_x * 2 * height, 2 * height, axis=0) for t in backward
    ]
    everything = gather(spectra, "gx").reshape(2 * grid_x, breadth)
    columns = call(functools.partial(row_kernel, scale=1.0 / (grid_x * grid_y)), block)(
        everything, *[jnp.asarray(t) for t in forward], *back, *column, wave
    )
    part = jax.ShapeDtypeStruct((height, breadth), f32)
    return tuple(call(home_kernel, (part, part))(gather(columns, "gy"), cosine, sine, star))


def solution(mesh):
    return jax.shard_map(
        on_device,
        mesh=mesh,
        in_specs=(P("gx", "gy"), P("gx", "gy"), P(), P(), P(), P(), P(), P()),
        out_specs=(P("gx", "gy"), P("gx", "gy")),
        check_vma=False,
    )
```

```python
import functools
import math

import jax
import jax.numpy as jnp
import ml_dtypes
import numpy as np
from jax import lax
from jax.experimental import pallas as pl
from jax.experimental.pallas import tpu as pltpu
from jax.sharding import PartitionSpec as P

step_ratio = 0.4
stencil_base = (-0.0625, 0.5625, 0.5625, -0.0625)
f32 = jnp.float32
bf16 = jnp.bfloat16

vmem_limit = 48 * 1024 * 1024


def split(value):
    high = value.astype(bf16)
    return high, (value - high.astype(f32)).astype(bf16)


def split_table(table):
    high = table.astype(ml_dtypes.bfloat16)
    low = (table - high.astype(np.float64)).astype(ml_dtypes.bfloat16)
    return high, low


def dot(a, b):
    return jnp.dot(a, b, preferred_element_type=f32)


def product_3(value, high, low):
    rows = value.shape[0]
    first, second = split(value)
    both = dot(jnp.concatenate([first, second], axis=0), high)
    return both[:rows] + both[rows:] + dot(first, low)


def parity(shape):
    rows = lax.broadcasted_iota(jnp.int32, shape, 0)
    return jnp.where(rows < shape[0] // 2, 1.0, -1.0).astype(f32)


def swap(value):
    half = value.shape[0] // 2
    return jnp.concatenate([value[half:], value[:half]], axis=0)


def rows_kernel(u_ref, v_ref, last_ref, first_ref):
    height = u_ref.shape[0]
    for q, ref in enumerate((u_ref, v_ref)):
        last_ref[4 * q : 4 * q + 4, :] = ref[height - 4 : height, :]
        first_ref[4 * q : 4 * q + 4, :] = ref[0:4, :]


def columns_kernel(u_ref, v_ref, bot_ref, top_ref, last_ref, first_ref, strip):
    height, breadth = u_ref.shape
    rows = height + 8
    for side, out in ((0, first_ref), (breadth - 128, last_ref)):
        strip[...] = jnp.zeros_like(strip)
        for q, ref in enumerate((u_ref, v_ref)):
            start = rows * q
            strip[start : start + height, :] = ref[:, side : side + 128]
            strip[start + height : start + height + 4, :] = bot_ref[4 * q : 4 * q + 4, side : side + 128]
            strip[start + height + 4 : start + rows, :] = top_ref[4 * q : 4 * q + 4, side : side + 128]
        turned = strip[...].T
        out[...] = turned[0:8] if side == 0 else turned[120:128]


def weights_kernel(
    w1_ref, w2_ref, w3_ref, b1_ref, b2_ref, b3_ref, k1_ref, k2_ref, even_ref, odd_ref, c1_ref, c2_ref, c3_ref, *, rows
):
    groups, depth, _ = k1_ref.shape
    c1_ref[...] = jnp.concatenate([b1_ref[...]] * 4, axis=1)
    c2_ref[...] = jnp.concatenate([b2_ref[...]] * 4, axis=1)
    place = lax.broadcasted_iota(jnp.int32, (64, 16), 0) // 4
    channel = 8 * (place // 8) + 4 * (place % 2) + (place // 2) % 4
    hit = channel == lax.broadcasted_iota(jnp.int32, (64, 16), 1)
    c3_ref[...] = jnp.sum(jnp.where(hit, b3_ref[...], 0.0), axis=1, keepdims=True)

    wide = jnp.concatenate([w1_ref[...].astype(f32)] * 4, axis=1)
    spread = []
    for d in range(3):
        parts = [
            jnp.broadcast_to(wide[(3 * d + s) * 2 + q : (3 * d + s) * 2 + q + 1, :], (rows, 256))
            for s in range(3)
            for q in range(2)
        ]
        parts.append(jnp.zeros((depth - 6 * rows, 256), f32))
        spread.append(jnp.concatenate(parts, axis=0))
    row = lax.broadcasted_iota(jnp.int32, (rows, 256), 0) - lax.broadcasted_iota(jnp.int32, (rows, 256), 1) // 64
    row = jnp.where(row < 0, row + rows, row)
    row = jnp.concatenate([row] * 6 + [jnp.full((depth - 6 * rows, 256), -1, jnp.int32)], axis=0)
    for r in range(groups):
        near = [row == (4 * r + d - 1) % rows for d in range(3)]
        block = jnp.where(near[0], spread[0], jnp.where(near[1], spread[1], jnp.where(near[2], spread[2], 0.0)))
        k1_ref[r] = block.astype(bf16)

    k2_ref[...] = jnp.zeros(k2_ref.shape, bf16)
    slots = {-1: 5, 0: 0, 1: 1, 2: 2, 3: 3, 4: 6}
    blank = jnp.zeros((64, 64), f32)
    for c in range(3):
        taps = [w2_ref[3 * d + c].astype(f32) for d in range(3)]
        two = [(taps[0], blank), (taps[1], taps[0]), (taps[2], taps[1]), (blank, taps[2])]
        two = [jnp.concatenate(pair, axis=0).T.astype(bf16) for pair in two]
        for h in range(2):
            for d in range(4):
                slot = slots[d + 2 * h - 1]
                k2_ref[64 * slot : 64 * slot + 64, 256 * c + 128 * h : 256 * c + 128 * h + 128] = two[d]

    taps = [[w3_ref[3 * d + c].astype(f32) for d in range(3)] for c in range(3)]
    blank = jnp.zeros((16, 64), f32)
    filler = jnp.zeros((64, 256), bf16)
    parts = [filler] * 8
    for k, slot in slots.items():
        pieces = [taps[c][k - t + 1] if 0 <= k - t + 1 < 3 else blank for c in range(3) for t in range(4)]
        pieces += [blank] * 4
        parts[slot] = jnp.concatenate(pieces, axis=0).T.astype(bf16)
    raw = jnp.concatenate(parts, axis=0)
    source = lax.broadcasted_iota(jnp.int32, (256, 256), 0)
    target = lax.broadcasted_iota(jnp.int32, (256, 256), 1)
    inner = target % 64
    place = inner // 4
    channel = 8 * (place // 8) + 4 * (place % 2) + (place // 2) % 4
    lane = 16 * (inner % 4) + channel
    part = target // 64
    column_even = jnp.where(part == 3, -1, 64 * part + lane)
    column_odd = jnp.where(
        part == 2, -1, jnp.where(part == 3, 128 + lane, jnp.where(part == 0, 64 + lane, lane))
    )
    even_ref[...] = dot(raw, jnp.where(source == column_even, 1.0, 0.0).astype(bf16)).astype(bf16)
    odd_ref[...] = dot(raw, jnp.where(source == column_odd, 1.0, 0.0).astype(bf16)).astype(bf16)


def advance_kernel(
    u_ref, v_ref, bot_ref, top_ref, right_ref, left_ref, w1_ref, w2_ref, w3e_ref, w3o_ref,
    b1_ref, b2_ref, b3_ref, star_ref, field, first, second, coeff, strip,
):
    height, breadth = u_ref.shape
    rows = height + 8
    groups = rows // 4
    lanes = breadth + 128
    strip[...] = jnp.zeros_like(strip)
    strip[0:4, :] = right_ref[0:4, :]
    strip[124:128, :] = left_ref[4:8, :]
    beside = strip[...].T
    for q, ref in enumerate((u_ref, v_ref)):
        field[q, 8 : 8 + height, :breadth] = ref[...]
        field[q, 8 + height : 12 + height, :breadth] = bot_ref[4 * q : 4 * q + 4, :]
        field[q, 12 + height : 16 + height, :breadth] = top_ref[4 * q : 4 * q + 4, :]
        field[q, 8 : 8 + rows, breadth:] = beside[rows * q : rows * q + rows]
        field[q, 0:8, :] = field[q, rows : rows + 8, :]
        field[q, 8 + rows : 16 + rows, :] = field[q, 8:16, :]
    whole = jnp.concatenate([field[0, 8 : 8 + rows], field[1, 8 : 8 + rows]], axis=0)
    pieces = [pltpu.roll(whole, 1, 1), whole, pltpu.roll(whole, lanes - 1, 1)]
    depth = w1_ref.shape[1]
    pieces.append(jnp.zeros((depth - 6 * rows, lanes), f32))
    turned = jnp.concatenate(pieces, axis=0).T
    patches = jnp.concatenate([turned[: breadth + 8], turned[lanes - 8 :]], axis=0).astype(bf16)
    span = breadth + 16
    for r in range(groups):
        first[r] = jnp.maximum(dot(patches, w1_ref[r]) + b1_ref[...], 0.0).astype(bf16)

    def gathered(source, r):
        before, after = (r - 1) % groups, (r + 1) % groups
        beside = jnp.concatenate([source[before, :, 128:], source[after, :, :128]], axis=1)
        return source[r], beside

    for r in range(groups):
        own, beside = gathered(first, r)
        total = dot(own, w2_ref[:256]) + dot(beside, w2_ref[256:])
        total = pltpu.roll(total[:, :256], 1, 0) + total[:, 256:512] + pltpu.roll(total[:, 512:], span - 1, 0)
        second[r] = jnp.maximum(total + b2_ref[...], 0.0).astype(bf16)

    def last(r, ref):
        own, beside = gathered(second, r)
        total = dot(own, ref[:256]) + dot(beside, ref[256:])
        left_part = total[:, :128]
        return pltpu.roll(left_part, 1, 0) + pltpu.roll(left_part, 64, 1) + pltpu.roll(total[:, 128:], span - 1, 0)

    def keep(r, block):
        coeff[r, :, :breadth] = block[:, :breadth]
        coeff[r, :, breadth:] = block[:, breadth:]

    pairs = [(i, i + 1) for i in range(0, groups - 2, 2)] + [(groups - 1, None)]
    for even, odd in pairs:
        block = last(even, w3e_ref)
        if odd is not None:
            other = last(odd, w3o_ref)
            lower = lax.broadcasted_iota(jnp.int32, block.shape, 1) < 64
            block = jnp.where(lower, block, other)
        block = jnp.concatenate(
            [block[: breadth + 8], jnp.zeros((lanes - span, 128), f32), block[breadth + 8 :]], axis=0
        ).T
        keep(even, block[:64])
        if odd is not None:
            keep(odd, block[64:])

    offsets = b3_ref[...]
    sub = lax.broadcasted_iota(jnp.int32, (8, breadth), 0) % 4

    def stacked(r, shift, qs=(0, 1)):
        start = 8 + 4 * r + shift
        return jnp.concatenate([field[q, start : start + 4, :] for q in qs], axis=0)

    previous = None
    for r in [groups - 1] + list(range(groups - 2)):
        weights = coeff[r] + offsets
        weights = [weights[8 * i : 8 * i + 8] for i in range(8)]
        centre = stacked(r, 0)

        def stencil(d):
            four = weights[4 * d : 4 * d + 4]
            mean = (four[0] + four[1] + four[2] + four[3]) * 0.25
            return [base + w - mean for base, w in zip(stencil_base, four)]

        east = stencil(0)
        flow_x = (
            east[0] * stacked(r, -1) + east[1] * centre + east[2] * stacked(r, 1) + east[3] * stacked(r, 2)
        )
        flow_x = flow_x * (0.5 * (stacked(r, 0, (0, 0)) + stacked(r, 1, (0, 0))))
        flow_x = flow_x[:, :breadth]
        if previous is not None:
            north = stencil(1)
            flow_y = (
                north[0] * pltpu.roll(centre, 1, 1)
                + north[1] * centre
                + north[2] * pltpu.roll(centre, lanes - 1, 1)
                + north[3] * pltpu.roll(centre, lanes - 2, 1)
            )
            carrier = stacked(r, 0, (1, 1))
            flow_y = flow_y * (0.5 * (carrier + pltpu.roll(carrier, lanes - 1, 1)))
            change_y = (flow_y - pltpu.roll(flow_y, 1, 1))[:, :breadth]
            above = jnp.where(sub == 0, pltpu.roll(previous, 5, 0), pltpu.roll(flow_x, 1, 0))
            star = centre[:, :breadth] - step_ratio * (flow_x - above + change_y)
            star_ref[4 * r : 4 * r + 4, :] = star[:4]
            star_ref[height + 4 * r : height + 4 * r + 4, :] = star[4:]
        previous = flow_x


def own_twiddle(ref):
    own = ref[lax.axis_index("gy")]
    half = own.shape[0] // 2
    return own[:half], own[half:]


def column_kernel(blocks_ref, twiddle_ref, high_ref, low_ref, out_ref):
    count, rows, breadth = blocks_ref.shape
    cosine, sine = own_twiddle(twiddle_ref)
    sign = parity((rows, breadth))
    mixed = None
    for b in range(count):
        block = blocks_ref[b] * sign
        term = block * cosine[b : b + 1, :] + swap(block) * (sign * sine[b : b + 1, :])
        mixed = term if mixed is None else mixed + term
    spectra = product_3(mixed, high_ref[...], low_ref[...])
    out_ref[...] = spectra[:, :breadth] + sign * swap(spectra[:, breadth:])


def row_kernel(gathered_ref, table_ref, table_low_ref, high_ref, low_ref, out_ref, *, scale):
    members, rows, breadth = gathered_ref.shape
    height = rows // 2
    length = members * height
    data = jnp.concatenate(
        [
            jnp.concatenate([gathered_ref[a, :height, :] for a in range(members)], axis=0),
            jnp.concatenate([gathered_ref[a, height:, :] for a in range(members)], axis=0),
        ],
        axis=1,
    )
    data, data_low = split(data)
    spectra = dot(table_ref[...], data) + dot(table_ref[...], data_low) + dot(table_low_ref[...], data)
    real_part = spectra[:length, :breadth] + spectra[length:, breadth:]
    imag_part = spectra[:length, breadth:] - spectra[length:, :breadth]
    index = lax.broadcasted_iota(jnp.int32, (length, breadth), 0)
    wave_x = jnp.where(index >= length // 2, index - length, index).astype(f32) * (2.0 * math.pi / length)
    members_y = lax.axis_size("gy")
    grid_y = members_y * breadth
    number_y = lax.axis_index("gy") + members_y * lax.broadcasted_iota(jnp.int32, (1, breadth), 1)
    wave_y = jnp.where(number_y >= grid_y // 2, number_y - grid_y, number_y).astype(f32) * (2.0 * math.pi / grid_y)
    edge_y = number_y == grid_y // 2
    edge_x = index == length // 2
    total = wave_x * wave_x + wave_y * wave_y
    zero = total == 0.0
    inverse = scale / jnp.where(zero, 1.0, total)
    same = (0.5 * inverse) * (wave_y * wave_y - wave_x * wave_x)
    cross = jnp.where(edge_x != edge_y, 0.0, -inverse * wave_x * wave_y)
    same_real = jnp.where(zero, 0.5 * scale, same)
    same_imag = jnp.where(zero, -0.5 * scale, same)
    kept_real = same_real * real_part - cross * imag_part
    kept_imag = same_imag * imag_part + cross * real_part
    kept, kept_low = split(jnp.concatenate([kept_real, kept_imag], axis=1))
    start = pl.multiple_of(lax.axis_index("gx") * height, height)

    def own(ref):
        parts = [ref[pl.ds(start, height), :], ref[pl.ds(pl.multiple_of(length + start, height), height), :]]
        return jnp.concatenate(parts, axis=0)

    table, table_low = own(table_ref), own(table_low_ref)
    home = dot(table, kept) + dot(table, kept_low) + dot(table_low, kept)
    home = jnp.concatenate(
        [
            home[:height, :breadth] - home[height:, breadth:],
            home[:height, breadth:] + home[height:, :breadth],
        ],
        axis=0,
    )
    columns = product_3(home, high_ref[...], low_ref[...])
    out_ref[...] = columns[:, :breadth] - parity((rows, breadth)) * swap(columns[:, breadth:])


def home_kernel(blocks_ref, twiddle_ref, star_ref, u_ref, v_ref):
    count, rows, breadth = blocks_ref.shape
    cosine, sine = own_twiddle(twiddle_ref)
    sign = parity((rows, breadth))
    result = 0.5 * star_ref[...]
    for b in range(count):
        block = blocks_ref[b]
        result = result + block * cosine[b : b + 1, :] - swap(block) * (sign * sine[b : b + 1, :])
    u_ref[...] = result[: rows // 2]
    v_ref[...] = result[rows // 2 :]


def call(kernel, shapes, scratch=(), flops=10**7):
    return pl.pallas_call(
        kernel,
        out_shape=shapes,
        scratch_shapes=list(scratch),
        compiler_params=pltpu.CompilerParams(vmem_limit_bytes=vmem_limit),
        cost_estimate=pl.CostEstimate(flops=flops, bytes_accessed=2**20, transcendentals=0),
    )


@functools.lru_cache(None)
def tables(height, breadth, members_x, members_y):
    turn = 2.0 * math.pi
    j = np.arange(breadth)
    phase = turn * (np.outer(j, j) % breadth) / breadth
    column = split_table(np.concatenate([np.cos(phase), np.sin(phase)], axis=1))
    length = height * members_x
    k = np.arange(length)
    phase = turn * (np.outer(k, k) % length) / length
    row = split_table(np.concatenate([np.cos(phase), np.sin(phase)], axis=0))
    g = np.arange(members_y)
    count = np.multiply.outer(np.outer(g, g) * breadth, np.ones(breadth, np.int64)) + np.outer(
        np.ones(members_y, np.int64), j
    )[None] * g[None, :, None]
    phase = turn * (count % (breadth * members_y)) / (breadth * members_y)
    twiddle_home = np.concatenate([np.cos(phase), np.sin(phase)], axis=1).astype(np.float32)
    phase = phase.transpose(1, 0, 2)
    twiddle_out = np.concatenate([np.cos(phase), np.sin(phase)], axis=1).astype(np.float32)
    return column, row, twiddle_out, twiddle_home


def gather(block, axis):
    return lax.all_gather(block, axis, axis=0, tiled=False)


def on_device(u_field, v_field, w_first, b_first, w_second, b_second, w_third, b_third):
    height, breadth = u_field.shape
    members_x, members_y = lax.axis_size("gx"), lax.axis_size("gy")
    grid_x, grid_y = height * members_x, breadth * members_y
    rows = height + 8
    groups = rows // 4
    span = breadth + 16
    shape = jax.ShapeDtypeStruct

    def shifted(value, axis, distance):
        peers = lax.axis_size(axis)
        return lax.ppermute(value, axis, [(i, (i + distance) % peers) for i in range(peers)])

    with jax.named_scope("surroundings"):
        edge = shape((8, breadth), f32)
        last, first = call(rows_kernel, (edge, edge))(u_field, v_field)
        top, bottom = shifted(last, "gx", 1), shifted(first, "gx", -1)
        edge = shape((8, 128), f32)
        last, first = call(columns_kernel, (edge, edge), (pltpu.VMEM((128, 128), f32),))(
            u_field, v_field, bottom, top
        )
        left, right = shifted(last, "gy", 1), shifted(first, "gy", -1)

    with jax.named_scope("weights"):
        weights = call(
            functools.partial(weights_kernel, rows=rows),
            (
                shape((groups, -(-6 * rows // 128) * 128, 256), bf16),
                shape((512, 768), bf16),
                shape((512, 256), bf16),
                shape((512, 256), bf16),
                shape((1, 256), f32),
                shape((1, 256), f32),
                shape((64, 1), f32),
            ),
        )(
            w_first.transpose(0, 2, 1).reshape(18, 64), w_second, w_third, b_first[None], b_second[None], b_third[None]
        )

    block = shape((2 * height, breadth), f32)
    with jax.named_scope("advance"):
        star = call(
            advance_kernel,
            block,
            (
                pltpu.VMEM((2, rows + 16, breadth + 128), f32),
                pltpu.VMEM((groups, span, 256), bf16),
                pltpu.VMEM((groups, span, 256), bf16),
                pltpu.VMEM((groups, 64, breadth + 128), f32),
                pltpu.VMEM((128, 128), f32),
            ),
            flops=10**9,
        )(u_field, v_field, bottom, top, right, left, *weights)

    column, row, twiddle_out, twiddle_home = tables(height, breadth, members_x, members_y)
    column, row = [[jnp.asarray(t) for t in pair] for pair in (column, row)]
    spectra = call(column_kernel, block)(gather(star, "gy"), jnp.asarray(twiddle_out), *column)
    columns = call(functools.partial(row_kernel, scale=1.0 / (grid_x * grid_y)), block)(
        gather(spectra, "gx"), *row, *column
    )
    part = shape((height, breadth), f32)
    return tuple(call(home_kernel, (part, part))(gather(columns, "gy"), jnp.asarray(twiddle_home), star))


def solution(mesh):
    return jax.shard_map(
        on_device,
        mesh=mesh,
        in_specs=(P("gx", "gy"), P("gx", "gy"), P(), P(), P(), P(), P(), P()),
        out_specs=(P("gx", "gy"), P("gx", "gy")),
        check_vma=False,
    )
```

```python
import functools
import math

import jax
import jax.numpy as jnp
import ml_dtypes
import numpy as np
from jax import lax
from jax.experimental import pallas as pl
from jax.experimental.pallas import tpu as pltpu
from jax.sharding import PartitionSpec as P

step_ratio = 0.4
stencil_base = (-0.0625, 0.5625, 0.5625, -0.0625)
f32 = jnp.float32
bf16 = jnp.bfloat16

vmem_limit = 48 * 1024 * 1024


def split(value):
    high = value.astype(bf16)
    return high, (value - high.astype(f32)).astype(bf16)


def split_table(table):
    high = table.astype(ml_dtypes.bfloat16)
    low = (table - high.astype(np.float64)).astype(ml_dtypes.bfloat16)
    return high, low


def dot(a, b):
    return jnp.dot(a, b, preferred_element_type=f32)


def product_3(value, high, low):
    rows = value.shape[0]
    first, second = split(value)
    both = dot(jnp.concatenate([first, second], axis=0), high)
    return both[:rows] + both[rows:] + dot(first, low)


def parity(shape):
    rows = lax.broadcasted_iota(jnp.int32, shape, 0)
    return jnp.where(rows < shape[0] // 2, 1.0, -1.0).astype(f32)


def swap(value):
    half = value.shape[0] // 2
    return jnp.concatenate([value[half:], value[:half]], axis=0)


def fetch(sources, targets, sems):
    copies = [pltpu.make_async_copy(a, b, sems.at[i]) for i, (a, b) in enumerate(zip(sources, targets))]
    for copy in copies:
        copy.start()
    for copy in copies:
        copy.wait()


def rows_kernel(u_hbm, v_hbm, last_ref, first_ref, u_ref, v_ref, sems):
    fetch((u_hbm, v_hbm), (u_ref, v_ref), sems)
    height = u_ref.shape[0]
    for q, ref in enumerate((u_ref, v_ref)):
        last_ref[4 * q : 4 * q + 4, :] = ref[height - 4 : height, :]
        first_ref[4 * q : 4 * q + 4, :] = ref[0:4, :]


def columns_kernel(u_ref, v_ref, bot_ref, top_ref, last_ref, first_ref, strip):
    height, breadth = u_ref.shape
    rows = height + 8
    for side, out in ((0, first_ref), (breadth - 128, last_ref)):
        strip[...] = jnp.zeros_like(strip)
        for q, ref in enumerate((u_ref, v_ref)):
            start = rows * q
            strip[start : start + height, :] = ref[:, side : side + 128]
            strip[start + height : start + height + 4, :] = bot_ref[4 * q : 4 * q + 4, side : side + 128]
            strip[start + height + 4 : start + rows, :] = top_ref[4 * q : 4 * q + 4, side : side + 128]
        turned = strip[...].T
        out[...] = turned[0:8] if side == 0 else turned[120:128]


def weights_kernel(
    w1_hbm, w2_hbm, w3_hbm, b1_hbm, b2_hbm, b3_hbm, k1_ref, k2_ref, even_ref, odd_ref, c1_ref, c2_ref, c3_ref,
    w1_ref, w2_ref, w3_ref, b1_ref, b2_ref, b3_ref, sems, *, rows
):
    fetch(
        (w1_hbm, w2_hbm, w3_hbm, b1_hbm, b2_hbm, b3_hbm), (w1_ref, w2_ref, w3_ref, b1_ref, b2_ref, b3_ref), sems
    )
    groups, depth, _ = k1_ref.shape
    c1_ref[...] = jnp.concatenate([b1_ref[...]] * 4, axis=1)
    c2_ref[...] = jnp.concatenate([b2_ref[...]] * 4, axis=1)
    place = lax.broadcasted_iota(jnp.int32, (64, 16), 0) // 4
    channel = 8 * (place // 8) + 4 * (place % 2) + (place // 2) % 4
    hit = channel == lax.broadcasted_iota(jnp.int32, (64, 16), 1)
    c3_ref[...] = jnp.sum(jnp.where(hit, b3_ref[...], 0.0), axis=1, keepdims=True)

    pick = lax.broadcasted_iota(jnp.int32, (8, 2), 0) == lax.broadcasted_iota(jnp.int32, (8, 2), 1)
    pick = jnp.where(pick, 1.0, 0.0).astype(bf16)
    turned = [
        lax.dot_general(pick, w1_ref[tap], (((1,), (1,)), ((), ())), preferred_element_type=f32) for tap in range(9)
    ]
    turned = [jnp.concatenate([tap] * 4, axis=1) for tap in turned]
    spread = []
    for d in range(3):
        parts = [
            jnp.broadcast_to(turned[3 * d + s][q : q + 1, :], (rows, 256))
            for s in range(3)
            for q in range(2)
        ]
        parts.append(jnp.zeros((depth - 6 * rows, 256), f32))
        spread.append(jnp.concatenate(parts, axis=0))
    row = lax.broadcasted_iota(jnp.int32, (rows, 256), 0) - lax.broadcasted_iota(jnp.int32, (rows, 256), 1) // 64
    row = jnp.where(row < 0, row + rows, row)
    row = jnp.concatenate([row] * 6 + [jnp.full((depth - 6 * rows, 256), -1, jnp.int32)], axis=0)
    for r in range(groups):
        near = [row == (4 * r + d - 1) % rows for d in range(3)]
        block = jnp.where(near[0], spread[0], jnp.where(near[1], spread[1], jnp.where(near[2], spread[2], 0.0)))
        k1_ref[r] = block.astype(bf16)

    k2_ref[...] = jnp.zeros(k2_ref.shape, bf16)
    slots = {-1: 5, 0: 0, 1: 1, 2: 2, 3: 3, 4: 6}
    blank = jnp.zeros((64, 64), f32)
    for c in range(3):
        taps = [w2_ref[3 * d + c].astype(f32) for d in range(3)]
        two = [(taps[0], blank), (taps[1], taps[0]), (taps[2], taps[1]), (blank, taps[2])]
        two = [jnp.concatenate(pair, axis=0).T.astype(bf16) for pair in two]
        for h in range(2):
            for d in range(4):
                slot = slots[d + 2 * h - 1]
                k2_ref[64 * slot : 64 * slot + 64, 256 * c + 128 * h : 256 * c + 128 * h + 128] = two[d]

    taps = [[w3_ref[3 * d + c].astype(f32) for d in range(3)] for c in range(3)]
    blank = jnp.zeros((16, 64), f32)
    filler = jnp.zeros((64, 256), bf16)
    parts = [filler] * 8
    for k, slot in slots.items():
        pieces = [taps[c][k - t + 1] if 0 <= k - t + 1 < 3 else blank for c in range(3) for t in range(4)]
        pieces += [blank] * 4
        parts[slot] = jnp.concatenate(pieces, axis=0).T.astype(bf16)
    raw = jnp.concatenate(parts, axis=0)
    source = lax.broadcasted_iota(jnp.int32, (256, 256), 0)
    target = lax.broadcasted_iota(jnp.int32, (256, 256), 1)
    inner = target % 64
    place = inner // 4
    channel = 8 * (place // 8) + 4 * (place % 2) + (place // 2) % 4
    lane = 16 * (inner % 4) + channel
    part = target // 64
    column_even = jnp.where(part == 3, -1, 64 * part + lane)
    column_odd = jnp.where(
        part == 2, -1, jnp.where(part == 3, 128 + lane, jnp.where(part == 0, 64 + lane, lane))
    )
    even_ref[...] = dot(raw, jnp.where(source == column_even, 1.0, 0.0).astype(bf16)).astype(bf16)
    odd_ref[...] = dot(raw, jnp.where(source == column_odd, 1.0, 0.0).astype(bf16)).astype(bf16)


def advance_kernel(
    u_ref, v_ref, bot_ref, top_ref, right_ref, left_ref, w1_ref, w2_ref, w3e_ref, w3o_ref,
    b1_ref, b2_ref, b3_ref, star_ref, field, first, second, coeff, strip,
):
    height, breadth = u_ref.shape
    rows = height + 8
    groups = rows // 4
    lanes = breadth + 128
    strip[...] = jnp.zeros_like(strip)
    strip[0:4, :] = right_ref[0:4, :]
    strip[124:128, :] = left_ref[4:8, :]
    beside = strip[...].T
    for q, ref in enumerate((u_ref, v_ref)):
        field[q, 8 : 8 + height, :breadth] = ref[...]
        field[q, 8 + height : 12 + height, :breadth] = bot_ref[4 * q : 4 * q + 4, :]
        field[q, 12 + height : 16 + height, :breadth] = top_ref[4 * q : 4 * q + 4, :]
        field[q, 8 : 8 + rows, breadth:] = beside[rows * q : rows * q + rows]
        field[q, 0:8, :] = field[q, rows : rows + 8, :]
        field[q, 8 + rows : 16 + rows, :] = field[q, 8:16, :]
    whole = jnp.concatenate([field[0, 8 : 8 + rows], field[1, 8 : 8 + rows]], axis=0)
    pieces = [pltpu.roll(whole, 1, 1), whole, pltpu.roll(whole, lanes - 1, 1)]
    depth = w1_ref.shape[1]
    pieces.append(jnp.zeros((depth - 6 * rows, lanes), f32))
    turned = jnp.concatenate(pieces, axis=0).T
    patches = jnp.concatenate([turned[: breadth + 8], turned[lanes - 8 :]], axis=0).astype(bf16)
    span = breadth + 16
    for r in range(groups):
        first[r] = jnp.maximum(dot(patches, w1_ref[r]) + b1_ref[...], 0.0).astype(bf16)

    def gathered(source, r):
        before, after = (r - 1) % groups, (r + 1) % groups
        beside = jnp.concatenate([source[before, :, 128:], source[after, :, :128]], axis=1)
        return source[r], beside

    for r in range(groups):
        own, beside = gathered(first, r)
        total = dot(own, w2_ref[:256]) + dot(beside, w2_ref[256:])
        total = pltpu.roll(total[:, :256], 1, 0) + total[:, 256:512] + pltpu.roll(total[:, 512:], span - 1, 0)
        second[r] = jnp.maximum(total + b2_ref[...], 0.0).astype(bf16)

    def last(r, ref):
        own, beside = gathered(second, r)
        total = dot(own, ref[:256]) + dot(beside, ref[256:])
        left_part = total[:, :128]
        return pltpu.roll(left_part, 1, 0) + pltpu.roll(left_part, 64, 1) + pltpu.roll(total[:, 128:], span - 1, 0)

    def keep(r, block):
        coeff[r, :, :breadth] = block[:, :breadth]
        coeff[r, :, breadth:] = block[:, breadth:]

    pairs = [(i, i + 1) for i in range(0, groups - 2, 2)] + [(groups - 1, None)]
    for even, odd in pairs:
        block = last(even, w3e_ref)
        if odd is not None:
            other = last(odd, w3o_ref)
            lower = lax.broadcasted_iota(jnp.int32, block.shape, 1) < 64
            block = jnp.where(lower, block, other)
        block = jnp.concatenate(
            [block[: breadth + 8], jnp.zeros((lanes - span, 128), f32), block[breadth + 8 :]], axis=0
        ).T
        keep(even, block[:64])
        if odd is not None:
            keep(odd, block[64:])

    offsets = b3_ref[...]
    sub = lax.broadcasted_iota(jnp.int32, (8, breadth), 0) % 4

    def stacked(r, shift, qs=(0, 1)):
        start = 8 + 4 * r + shift
        return jnp.concatenate([field[q, start : start + 4, :] for q in qs], axis=0)

    previous = None
    for r in [groups - 1] + list(range(groups - 2)):
        weights = coeff[r] + offsets
        weights = [weights[8 * i : 8 * i + 8] for i in range(8)]
        centre = stacked(r, 0)

        def stencil(d):
            four = weights[4 * d : 4 * d + 4]
            mean = (four[0] + four[1] + four[2] + four[3]) * 0.25
            return [base + w - mean for base, w in zip(stencil_base, four)]

        east = stencil(0)
        flow_x = (
            east[0] * stacked(r, -1) + east[1] * centre + east[2] * stacked(r, 1) + east[3] * stacked(r, 2)
        )
        flow_x = flow_x * (0.5 * (stacked(r, 0, (0, 0)) + stacked(r, 1, (0, 0))))
        flow_x = flow_x[:, :breadth]
        if previous is not None:
            north = stencil(1)
            flow_y = (
                north[0] * pltpu.roll(centre, 1, 1)
                + north[1] * centre
                + north[2] * pltpu.roll(centre, lanes - 1, 1)
                + north[3] * pltpu.roll(centre, lanes - 2, 1)
            )
            carrier = stacked(r, 0, (1, 1))
            flow_y = flow_y * (0.5 * (carrier + pltpu.roll(carrier, lanes - 1, 1)))
            change_y = (flow_y - pltpu.roll(flow_y, 1, 1))[:, :breadth]
            above = jnp.where(sub == 0, pltpu.roll(previous, 5, 0), pltpu.roll(flow_x, 1, 0))
            star = centre[:, :breadth] - step_ratio * (flow_x - above + change_y)
            star_ref[4 * r : 4 * r + 4, :] = star[:4]
            star_ref[height + 4 * r : height + 4 * r + 4, :] = star[4:]
        previous = flow_x


def own_twiddle(ref):
    own = ref[lax.axis_index("gy")]
    half = own.shape[0] // 2
    return own[:half], own[half:]


def column_kernel(*refs):
    *blocks, twiddle_ref, high_ref, low_ref, out_ref = refs
    rows, breadth = out_ref.shape
    cosine, sine = own_twiddle(twiddle_ref)
    sign = parity((rows, breadth))
    mixed = None
    for k, ref in enumerate(blocks):
        block = ref[...] * sign
        term = block * cosine[k : k + 1, :] + swap(block) * (sign * sine[k : k + 1, :])
        mixed = term if mixed is None else mixed + term
    spectra = product_3(mixed, high_ref[...], low_ref[...])
    out_ref[...] = spectra[:, :breadth] + sign * swap(spectra[:, breadth:])


def row_kernel(*refs, scale):
    *blocks, table_ref, table_low_ref, high_ref, low_ref, out_ref, gathered = refs
    rows, breadth = out_ref.shape
    height = rows // 2
    length = len(blocks) * height
    own_index = lax.axis_index("gx")
    for k, ref in enumerate(blocks):
        start = pl.multiple_of((own_index ^ k) * height, height)
        gathered[pl.ds(start, height), :breadth] = ref[:height, :]
        gathered[pl.ds(start, height), breadth:] = ref[height:, :]
    data = gathered[...]
    data, data_low = split(data)
    spectra = dot(table_ref[...], data) + dot(table_ref[...], data_low) + dot(table_low_ref[...], data)
    real_part = spectra[:length, :breadth] + spectra[length:, breadth:]
    imag_part = spectra[:length, breadth:] - spectra[length:, :breadth]
    index = lax.broadcasted_iota(jnp.int32, (length, breadth), 0)
    wave_x = jnp.where(index >= length // 2, index - length, index).astype(f32) * (2.0 * math.pi / length)
    members_y = lax.axis_size("gy")
    grid_y = members_y * breadth
    number_y = lax.axis_index("gy") + members_y * lax.broadcasted_iota(jnp.int32, (1, breadth), 1)
    wave_y = jnp.where(number_y >= grid_y // 2, number_y - grid_y, number_y).astype(f32) * (2.0 * math.pi / grid_y)
    edge_y = number_y == grid_y // 2
    edge_x = index == length // 2
    total = wave_x * wave_x + wave_y * wave_y
    zero = total == 0.0
    inverse = scale / jnp.where(zero, 1.0, total)
    same = (0.5 * inverse) * (wave_y * wave_y - wave_x * wave_x)
    cross = jnp.where(edge_x != edge_y, 0.0, -inverse * wave_x * wave_y)
    same_real = jnp.where(zero, 0.5 * scale, same)
    same_imag = jnp.where(zero, -0.5 * scale, same)
    kept_real = same_real * real_part - cross * imag_part
    kept_imag = same_imag * imag_part + cross * real_part
    kept, kept_low = split(jnp.concatenate([kept_real, kept_imag], axis=1))
    start = pl.multiple_of(own_index * height, height)

    def own(ref):
        parts = [ref[pl.ds(start, height), :], ref[pl.ds(pl.multiple_of(length + start, height), height), :]]
        return jnp.concatenate(parts, axis=0)

    table, table_low = own(table_ref), own(table_low_ref)
    home = dot(table, kept) + dot(table, kept_low) + dot(table_low, kept)
    home = jnp.concatenate(
        [
            home[:height, :breadth] - home[height:, breadth:],
            home[:height, breadth:] + home[height:, :breadth],
        ],
        axis=0,
    )
    columns = product_3(home, high_ref[...], low_ref[...])
    out_ref[...] = columns[:, :breadth] - parity((rows, breadth)) * swap(columns[:, breadth:])


def home_kernel(*refs):
    *blocks, twiddle_ref, star_ref, u_ref, v_ref = refs
    rows, breadth = star_ref.shape
    cosine, sine = own_twiddle(twiddle_ref)
    sign = parity((rows, breadth))
    result = 0.5 * star_ref[...]
    for k, ref in enumerate(blocks):
        block = ref[...]
        result = result + block * cosine[k : k + 1, :] - swap(block) * (sign * sine[k : k + 1, :])
    u_ref[...] = result[: rows // 2]
    v_ref[...] = result[rows // 2 :]


def call(kernel, shapes, scratch=(), flops=10**7, outside=0):
    specs = {"in_specs": [pl.BlockSpec(memory_space=pltpu.HBM)] * outside} if outside else {}
    return pl.pallas_call(
        kernel,
        out_shape=shapes,
        scratch_shapes=list(scratch),
        compiler_params=pltpu.CompilerParams(vmem_limit_bytes=vmem_limit),
        cost_estimate=pl.CostEstimate(flops=flops, bytes_accessed=2**20, transcendentals=0),
        **specs,
    )


@functools.lru_cache(None)
def tables(height, breadth, members_x, members_y):
    turn = 2.0 * math.pi
    j = np.arange(breadth)
    phase = turn * (np.outer(j, j) % breadth) / breadth
    column = split_table(np.concatenate([np.cos(phase), np.sin(phase)], axis=1))
    length = height * members_x
    k = np.arange(length)
    phase = turn * (np.outer(k, k) % length) / length
    row = split_table(np.concatenate([np.cos(phase), np.sin(phase)], axis=0))
    g = np.arange(members_y)[:, None, None]
    partner = g ^ np.arange(members_y)[None, :, None]
    whole = breadth * members_y
    out = turn * ((partner * breadth + j) * g % whole) / whole
    home = turn * ((g * breadth + j) * partner % whole) / whole
    twiddle_out, twiddle_home = [
        np.concatenate([np.cos(phase), np.sin(phase)], axis=1).astype(np.float32) for phase in (out, home)
    ]
    return column, row, twiddle_out, twiddle_home


def partner(block, axis, k):
    return lax.ppermute(block, axis, [(i, i ^ k) for i in range(lax.axis_size(axis))])


def gather_y(block):
    return [block] + [partner(block, "gy", k) for k in range(1, lax.axis_size("gy"))]


def gather_x(block):
    own = [block] + [partner(block, "gx", k) for k in range(2, lax.axis_size("gx"), 2)]
    return [other for held in own for other in (held, partner(held, "gx", 1))]


def on_device(u_field, v_field, w_first, b_first, w_second, b_second, w_third, b_third):
    height, breadth = u_field.shape
    members_x, members_y = lax.axis_size("gx"), lax.axis_size("gy")
    grid_x, grid_y = height * members_x, breadth * members_y
    rows = height + 8
    groups = rows // 4
    span = breadth + 16
    shape = jax.ShapeDtypeStruct

    def shifted(value, axis, distance):
        peers = lax.axis_size(axis)
        return lax.ppermute(value, axis, [(i, (i + distance) % peers) for i in range(peers)])

    with jax.named_scope("surroundings"):
        edge = shape((8, breadth), f32)
        block = shape((height, breadth), f32)
        last, first, u_field, v_field = call(
            rows_kernel, (edge, edge, block, block), (pltpu.SemaphoreType.DMA((2,)),), outside=2
        )(u_field, v_field)
        top, bottom = shifted(last, "gx", 1), shifted(first, "gx", -1)
        edge = shape((8, 128), f32)
        last, first = call(columns_kernel, (edge, edge), (pltpu.VMEM((128, 128), f32),))(
            u_field, v_field, bottom, top
        )
        left, right = shifted(last, "gy", 1), shifted(first, "gy", -1)

    with jax.named_scope("weights"):
        weights = call(
            functools.partial(weights_kernel, rows=rows),
            (
                shape((groups, -(-6 * rows // 128) * 128, 256), bf16),
                shape((512, 768), bf16),
                shape((512, 256), bf16),
                shape((512, 256), bf16),
                shape((1, 256), f32),
                shape((1, 256), f32),
                shape((64, 1), f32),
            ),
            (
                pltpu.VMEM(w_first.shape, bf16),
                pltpu.VMEM(w_second.shape, bf16),
                pltpu.VMEM(w_third.shape, bf16),
                pltpu.VMEM((1, 64), f32),
                pltpu.VMEM((1, 64), f32),
                pltpu.VMEM((1, 16), f32),
                pltpu.SemaphoreType.DMA((6,)),
            ),
            outside=6,
        )(w_first, w_second, w_third, b_first[None], b_second[None], b_third[None])

    block = shape((2 * height, breadth), f32)
    with jax.named_scope("advance"):
        star = call(
            advance_kernel,
            block,
            (
                pltpu.VMEM((2, rows + 16, breadth + 128), f32),
                pltpu.VMEM((groups, span, 256), bf16),
                pltpu.VMEM((groups, span, 256), bf16),
                pltpu.VMEM((groups, 64, breadth + 128), f32),
                pltpu.VMEM((128, 128), f32),
            ),
            flops=10**9,
        )(u_field, v_field, bottom, top, right, left, *weights)

    column, row, twiddle_out, twiddle_home = tables(height, breadth, members_x, members_y)
    column, row = [[jnp.asarray(t) for t in pair] for pair in (column, row)]
    spectra = call(column_kernel, block)(*gather_y(star), jnp.asarray(twiddle_out), *column)
    columns = call(
        functools.partial(row_kernel, scale=1.0 / (grid_x * grid_y)),
        block,
        (pltpu.VMEM((grid_x, 2 * breadth), f32),),
    )(*gather_x(spectra), *row, *column)
    part = shape((height, breadth), f32)
    return tuple(call(home_kernel, (part, part))(*gather_y(columns), jnp.asarray(twiddle_home), star))


def solution(mesh):
    return jax.shard_map(
        on_device,
        mesh=mesh,
        in_specs=(P("gx", "gy"), P("gx", "gy"), P(), P(), P(), P(), P(), P()),
        out_specs=(P("gx", "gy"), P("gx", "gy")),
        check_vma=False,
    )
```

```python
import functools
import math

import jax
import jax.numpy as jnp
import ml_dtypes
import numpy as np
from jax import lax
from jax.experimental import pallas as pl
from jax.experimental.pallas import tpu as pltpu
from jax.sharding import PartitionSpec as P

step_ratio = 0.4
stencil_base = (-0.0625, 0.5625, 0.5625, -0.0625)
f32 = jnp.float32
bf16 = jnp.bfloat16

vmem_limit = 48 * 1024 * 1024


def split(value):
    high = value.astype(bf16)
    return high, (value - high.astype(f32)).astype(bf16)


def split_table(table):
    high = table.astype(ml_dtypes.bfloat16)
    low = (table - high.astype(np.float64)).astype(ml_dtypes.bfloat16)
    return high, low


def dot(a, b):
    return jnp.dot(a, b, preferred_element_type=f32)


def product_3(value, high, low):
    rows = value.shape[0]
    first, second = split(value)
    both = dot(jnp.concatenate([first, second], axis=0), high)
    return both[:rows] + both[rows:] + dot(first, low)


def parity(shape):
    rows = lax.broadcasted_iota(jnp.int32, shape, 0)
    return jnp.where(rows < shape[0] // 2, 1.0, -1.0).astype(f32)


def swap(value):
    half = value.shape[0] // 2
    return jnp.concatenate([value[half:], value[:half]], axis=0)


def rows_kernel(both_ref, last_ref, first_ref):
    height = both_ref.shape[0] // 2
    for q in range(2):
        last_ref[4 * q : 4 * q + 4, :] = both_ref[height * (q + 1) - 4 : height * (q + 1), :]
        first_ref[4 * q : 4 * q + 4, :] = both_ref[height * q : height * q + 4, :]


def columns_kernel(both_ref, bot_ref, top_ref, order_ref, last_ref, first_ref, strip):
    height, breadth = both_ref.shape[0] // 2, both_ref.shape[1]
    rows = height + 8
    for side, out in ((0, first_ref), (breadth - 128, last_ref)):
        strip[...] = jnp.zeros_like(strip)
        for q in range(2):
            start = rows * q
            strip[start : start + height, :] = both_ref[height * q : height * (q + 1), side : side + 128]
            strip[start + height : start + height + 4, :] = bot_ref[4 * q : 4 * q + 4, side : side + 128]
            strip[start + height + 4 : start + rows, :] = top_ref[4 * q : 4 * q + 4, side : side + 128]
        turned = strip[...].T
        out[...] = turned[0:8] if side == 0 else turned[120:128]


def first_weights_kernel(packed_ref, k1_ref, c1_ref, c2_ref, c3_ref, *, rows):
    groups, depth, _ = k1_ref.shape
    packed = packed_ref[...]
    wide = jnp.concatenate([packed] * 4, axis=1)
    c1_ref[...] = wide[18:19]
    c2_ref[...] = wide[19:20]
    place = lax.broadcasted_iota(jnp.int32, (64, 64), 0) // 4
    channel = 8 * (place // 8) + 4 * (place % 2) + (place // 2) % 4
    hit = channel == lax.broadcasted_iota(jnp.int32, (64, 64), 1)
    c3_ref[...] = jnp.sum(jnp.where(hit, packed[20:21], 0.0), axis=1, keepdims=True)
    spread = []
    for d in range(3):
        parts = [
            jnp.broadcast_to(wide[(3 * d + s) * 2 + q : (3 * d + s) * 2 + q + 1, :], (rows, 256))
            for s in range(3)
            for q in range(2)
        ]
        parts.append(jnp.zeros((depth - 6 * rows, 256), f32))
        spread.append(jnp.concatenate(parts, axis=0))
    row = lax.broadcasted_iota(jnp.int32, (rows, 256), 0) - lax.broadcasted_iota(jnp.int32, (rows, 256), 1) // 64
    row = jnp.where(row < 0, row + rows, row)
    row = jnp.concatenate([row] * 6 + [jnp.full((depth - 6 * rows, 256), -1, jnp.int32)], axis=0)
    for r in range(groups):
        near = [row == (4 * r + d - 1) % rows for d in range(3)]
        block = jnp.where(near[0], spread[0], jnp.where(near[1], spread[1], jnp.where(near[2], spread[2], 0.0)))
        k1_ref[r] = block.astype(bf16)


def other_weights_kernel(packed_ref, k2_ref, even_ref, odd_ref):
    k2_ref[...] = jnp.zeros(k2_ref.shape, bf16)
    slots = {-1: 5, 0: 0, 1: 1, 2: 2, 3: 3, 4: 6}
    blank = jnp.zeros((64, 64), f32)
    for c in range(3):
        taps = [packed_ref[64 * (3 * d + c) : 64 * (3 * d + c) + 64, :].astype(f32) for d in range(3)]
        two = [(taps[0], blank), (taps[1], taps[0]), (taps[2], taps[1]), (blank, taps[2])]
        two = [jnp.concatenate(pair, axis=0).T.astype(bf16) for pair in two]
        for h in range(2):
            for d in range(4):
                slot = slots[d + 2 * h - 1]
                k2_ref[64 * slot : 64 * slot + 64, 256 * c + 128 * h : 256 * c + 128 * h + 128] = two[d]

    taps = [
        [packed_ref[576 + 16 * (3 * d + c) : 592 + 16 * (3 * d + c), :].astype(f32) for d in range(3)]
        for c in range(3)
    ]
    blank = jnp.zeros((16, 64), f32)
    filler = jnp.zeros((64, 256), bf16)
    parts = [filler] * 8
    for k, slot in slots.items():
        pieces = [taps[c][k - t + 1] if 0 <= k - t + 1 < 3 else blank for c in range(3) for t in range(4)]
        pieces += [blank] * 4
        parts[slot] = jnp.concatenate(pieces, axis=0).T.astype(bf16)
    raw = jnp.concatenate(parts, axis=0)
    source = lax.broadcasted_iota(jnp.int32, (256, 256), 0)
    target = lax.broadcasted_iota(jnp.int32, (256, 256), 1)
    inner = target % 64
    place = inner // 4
    channel = 8 * (place // 8) + 4 * (place % 2) + (place // 2) % 4
    lane = 16 * (inner % 4) + channel
    part = target // 64
    column_even = jnp.where(part == 3, -1, 64 * part + lane)
    column_odd = jnp.where(
        part == 2, -1, jnp.where(part == 3, 128 + lane, jnp.where(part == 0, 64 + lane, lane))
    )
    even_ref[...] = dot(raw, jnp.where(source == column_even, 1.0, 0.0).astype(bf16)).astype(bf16)
    odd_ref[...] = dot(raw, jnp.where(source == column_odd, 1.0, 0.0).astype(bf16)).astype(bf16)


def advance_kernel(
    both_ref, bot_ref, top_ref, right_ref, left_ref, w1_ref, w2_ref, w3e_ref, w3o_ref,
    b1_ref, b2_ref, b3_ref, star_ref, field, first, second, coeff, strip,
):
    height, breadth = both_ref.shape[0] // 2, both_ref.shape[1]
    rows = height + 8
    groups = rows // 4
    lanes = breadth + 128
    strip[...] = jnp.zeros_like(strip)
    strip[0:4, :] = right_ref[0:4, :]
    strip[124:128, :] = left_ref[4:8, :]
    beside = strip[...].T
    for q in range(2):
        field[q, 8 : 8 + height, :breadth] = both_ref[height * q : height * (q + 1), :]
        field[q, 8 + height : 12 + height, :breadth] = bot_ref[4 * q : 4 * q + 4, :]
        field[q, 12 + height : 16 + height, :breadth] = top_ref[4 * q : 4 * q + 4, :]
        field[q, 8 : 8 + rows, breadth:] = beside[rows * q : rows * q + rows]
        field[q, 0:8, :] = field[q, rows : rows + 8, :]
        field[q, 8 + rows : 16 + rows, :] = field[q, 8:16, :]
    whole = jnp.concatenate([field[0, 8 : 8 + rows], field[1, 8 : 8 + rows]], axis=0)
    pieces = [pltpu.roll(whole, 1, 1), whole, pltpu.roll(whole, lanes - 1, 1)]
    depth = w1_ref.shape[1]
    pieces.append(jnp.zeros((depth - 6 * rows, lanes), f32))
    turned = jnp.concatenate(pieces, axis=0).T
    patches = jnp.concatenate([turned[: breadth + 8], turned[lanes - 8 :]], axis=0).astype(bf16)
    span = breadth + 16
    for r in range(groups):
        first[r] = jnp.maximum(dot(patches, w1_ref[r]) + b1_ref[...], 0.0).astype(bf16)

    def gathered(source, r):
        before, after = (r - 1) % groups, (r + 1) % groups
        beside = jnp.concatenate([source[before, :, 128:], source[after, :, :128]], axis=1)
        return source[r], beside

    for r in range(groups):
        own, beside = gathered(first, r)
        total = dot(own, w2_ref[:256]) + dot(beside, w2_ref[256:])
        total = pltpu.roll(total[:, :256], 1, 0) + total[:, 256:512] + pltpu.roll(total[:, 512:], span - 1, 0)
        second[r] = jnp.maximum(total + b2_ref[...], 0.0).astype(bf16)

    def last(r, ref):
        own, beside = gathered(second, r)
        total = dot(own, ref[:256]) + dot(beside, ref[256:])
        left_part = total[:, :128]
        return pltpu.roll(left_part, 1, 0) + pltpu.roll(left_part, 64, 1) + pltpu.roll(total[:, 128:], span - 1, 0)

    def keep(r, block):
        coeff[r, :, :breadth] = block[:, :breadth]
        coeff[r, :, breadth:] = block[:, breadth:]

    pairs = [(i, i + 1) for i in range(0, groups - 2, 2)] + [(groups - 1, None)]
    for even, odd in pairs:
        block = last(even, w3e_ref)
        if odd is not None:
            other = last(odd, w3o_ref)
            lower = lax.broadcasted_iota(jnp.int32, block.shape, 1) < 64
            block = jnp.where(lower, block, other)
        block = jnp.concatenate(
            [block[: breadth + 8], jnp.zeros((lanes - span, 128), f32), block[breadth + 8 :]], axis=0
        ).T
        keep(even, block[:64])
        if odd is not None:
            keep(odd, block[64:])

    offsets = b3_ref[...]
    sub = lax.broadcasted_iota(jnp.int32, (8, breadth), 0) % 4

    def stacked(r, shift, qs=(0, 1)):
        start = 8 + 4 * r + shift
        return jnp.concatenate([field[q, start : start + 4, :] for q in qs], axis=0)

    previous = None
    for r in [groups - 1] + list(range(groups - 2)):
        weights = coeff[r] + offsets
        weights = [weights[8 * i : 8 * i + 8] for i in range(8)]
        centre = stacked(r, 0)

        def stencil(d):
            four = weights[4 * d : 4 * d + 4]
            mean = (four[0] + four[1] + four[2] + four[3]) * 0.25
            return [base + w - mean for base, w in zip(stencil_base, four)]

        east = stencil(0)
        flow_x = (
            east[0] * stacked(r, -1) + east[1] * centre + east[2] * stacked(r, 1) + east[3] * stacked(r, 2)
        )
        flow_x = flow_x * (0.5 * (stacked(r, 0, (0, 0)) + stacked(r, 1, (0, 0))))
        flow_x = flow_x[:, :breadth]
        if previous is not None:
            north = stencil(1)
            flow_y = (
                north[0] * pltpu.roll(centre, 1, 1)
                + north[1] * centre
                + north[2] * pltpu.roll(centre, lanes - 1, 1)
                + north[3] * pltpu.roll(centre, lanes - 2, 1)
            )
            carrier = stacked(r, 0, (1, 1))
            flow_y = flow_y * (0.5 * (carrier + pltpu.roll(carrier, lanes - 1, 1)))
            change_y = (flow_y - pltpu.roll(flow_y, 1, 1))[:, :breadth]
            above = jnp.where(sub == 0, pltpu.roll(previous, 5, 0), pltpu.roll(flow_x, 1, 0))
            star = centre[:, :breadth] - step_ratio * (flow_x - above + change_y)
            star_ref[4 * r : 4 * r + 4, :] = star[:4]
            star_ref[height + 4 * r : height + 4 * r + 4, :] = star[4:]
        previous = flow_x


def own_twiddle(ref):
    own = ref[lax.axis_index("gy")]
    half = own.shape[0] // 2
    return own[:half], own[half:]


def column_kernel(*refs):
    *blocks, twiddle_ref, high_ref, low_ref, out_ref = refs
    rows, breadth = out_ref.shape
    cosine, sine = own_twiddle(twiddle_ref)
    sign = parity((rows, breadth))
    mixed = None
    for k, ref in enumerate(blocks):
        block = ref[...] * sign
        term = block * cosine[k : k + 1, :] + swap(block) * (sign * sine[k : k + 1, :])
        mixed = term if mixed is None else mixed + term
    spectra = product_3(mixed, high_ref[...], low_ref[...])
    out_ref[...] = spectra[:, :breadth] + sign * swap(spectra[:, breadth:])


def row_kernel(*refs, scale):
    *blocks, table_ref, table_low_ref, high_ref, low_ref, out_ref, gathered = refs
    rows, breadth = out_ref.shape
    height = rows // 2
    length = len(blocks) * height
    own_index = lax.axis_index("gx")
    for k, ref in enumerate(blocks):
        start = pl.multiple_of((own_index ^ k) * height, height)
        gathered[pl.ds(start, height), :breadth] = ref[:height, :]
        gathered[pl.ds(start, height), breadth:] = ref[height:, :]
    data = gathered[...]
    data, data_low = split(data)
    spectra = dot(table_ref[...], data) + dot(table_ref[...], data_low) + dot(table_low_ref[...], data)
    real_part = spectra[:length, :breadth] + spectra[length:, breadth:]
    imag_part = spectra[:length, breadth:] - spectra[length:, :breadth]
    index = lax.broadcasted_iota(jnp.int32, (length, breadth), 0)
    wave_x = jnp.where(index >= length // 2, index - length, index).astype(f32) * (2.0 * math.pi / length)
    members_y = lax.axis_size("gy")
    grid_y = members_y * breadth
    number_y = lax.axis_index("gy") + members_y * lax.broadcasted_iota(jnp.int32, (1, breadth), 1)
    wave_y = jnp.where(number_y >= grid_y // 2, number_y - grid_y, number_y).astype(f32) * (2.0 * math.pi / grid_y)
    edge_y = number_y == grid_y // 2
    edge_x = index == length // 2
    total = wave_x * wave_x + wave_y * wave_y
    zero = total == 0.0
    inverse = scale / jnp.where(zero, 1.0, total)
    same = (0.5 * inverse) * (wave_y * wave_y - wave_x * wave_x)
    cross = jnp.where(edge_x != edge_y, 0.0, -inverse * wave_x * wave_y)
    same_real = jnp.where(zero, 0.5 * scale, same)
    same_imag = jnp.where(zero, -0.5 * scale, same)
    kept_real = same_real * real_part - cross * imag_part
    kept_imag = same_imag * imag_part + cross * real_part
    kept, kept_low = split(jnp.concatenate([kept_real, kept_imag], axis=1))
    start = pl.multiple_of(own_index * height, height)

    def own(ref):
        parts = [ref[pl.ds(start, height), :], ref[pl.ds(pl.multiple_of(length + start, height), height), :]]
        return jnp.concatenate(parts, axis=0)

    table, table_low = own(table_ref), own(table_low_ref)
    home = dot(table, kept) + dot(table, kept_low) + dot(table_low, kept)
    home = jnp.concatenate(
        [
            home[:height, :breadth] - home[height:, breadth:],
            home[:height, breadth:] + home[height:, :breadth],
        ],
        axis=0,
    )
    columns = product_3(home, high_ref[...], low_ref[...])
    out_ref[...] = columns[:, :breadth] - parity((rows, breadth)) * swap(columns[:, breadth:])


def home_kernel(*refs):
    *blocks, twiddle_ref, star_ref, u_ref, v_ref = refs
    rows, breadth = star_ref.shape
    cosine, sine = own_twiddle(twiddle_ref)
    sign = parity((rows, breadth))
    result = 0.5 * star_ref[...]
    for k, ref in enumerate(blocks):
        block = ref[...]
        result = result + block * cosine[k : k + 1, :] - swap(block) * (sign * sine[k : k + 1, :])
    u_ref[...] = result[: rows // 2]
    v_ref[...] = result[rows // 2 :]


def call(kernel, shapes, scratch=(), flops=10**7):
    return pl.pallas_call(
        kernel,
        out_shape=shapes,
        scratch_shapes=list(scratch),
        compiler_params=pltpu.CompilerParams(vmem_limit_bytes=vmem_limit),
        cost_estimate=pl.CostEstimate(flops=flops, bytes_accessed=2**20, transcendentals=0),
    )


@functools.lru_cache(None)
def tables(height, breadth, members_x, members_y):
    turn = 2.0 * math.pi
    j = np.arange(breadth)
    phase = turn * (np.outer(j, j) % breadth) / breadth
    column = split_table(np.concatenate([np.cos(phase), np.sin(phase)], axis=1))
    length = height * members_x
    k = np.arange(length)
    phase = turn * (np.outer(k, k) % length) / length
    row = split_table(np.concatenate([np.cos(phase), np.sin(phase)], axis=0))
    g = np.arange(members_y)[:, None, None]
    partner = g ^ np.arange(members_y)[None, :, None]
    whole = breadth * members_y
    out = turn * ((partner * breadth + j) * g % whole) / whole
    home = turn * ((g * breadth + j) * partner % whole) / whole
    twiddle_out, twiddle_home = [
        np.concatenate([np.cos(phase), np.sin(phase)], axis=1).astype(np.float32) for phase in (out, home)
    ]
    return column, row, twiddle_out, twiddle_home


def partner(block, axis, k):
    return lax.ppermute(block, axis, [(i, i ^ k) for i in range(lax.axis_size(axis))])


def gather_y(block):
    return [block] + [partner(block, "gy", k) for k in range(1, lax.axis_size("gy"))]


def gather_x(block):
    own = [block] + [partner(block, "gx", k) for k in range(2, lax.axis_size("gx"), 2)]
    return [other for held in own for other in (held, partner(held, "gx", 1))]


def on_device(u_field, v_field, w_first, b_first, w_second, b_second, w_third, b_third):
    height, breadth = u_field.shape
    members_x, members_y = lax.axis_size("gx"), lax.axis_size("gy")
    grid_x, grid_y = height * members_x, breadth * members_y
    rows = height + 8
    groups = rows // 4
    span = breadth + 16
    shape = jax.ShapeDtypeStruct

    def shifted(value, axis, distance):
        peers = lax.axis_size(axis)
        return lax.ppermute(value, axis, [(i, (i + distance) % peers) for i in range(peers)])

    with jax.named_scope("rows_around"):
        component = lax.broadcasted_iota(jnp.int32, (2, height, breadth), 0)
        both = jnp.where(component == 0, u_field[None], v_field[None]).reshape(2 * height, breadth)
        edge = shape((8, breadth), f32)
        last, first = call(rows_kernel, (edge, edge))(both)
        top, bottom = shifted(last, "gx", 1), shifted(first, "gx", -1)

    with jax.named_scope("weights"):
        biases = jnp.stack([b_first, b_second, jnp.pad(b_third, (0, 64 - b_third.shape[0]))])
        packed = jnp.concatenate([w_first.transpose(0, 2, 1).reshape(18, 64).astype(f32), biases], axis=0)
        kernel_1, *biases = call(
            functools.partial(first_weights_kernel, rows=rows),
            (
                shape((groups, -(-6 * rows // 128) * 128, 256), bf16),
                shape((1, 256), f32),
                shape((1, 256), f32),
                shape((64, 1), f32),
            ),
        )(packed)

    with jax.named_scope("columns_around"):
        edge = shape((8, 128), f32)
        last, first = call(columns_kernel, (edge, edge), (pltpu.VMEM((128, 128), f32),))(
            both, bottom, top, biases[2]
        )
        left, right = shifted(last, "gy", 1), shifted(first, "gy", -1)

    with jax.named_scope("weights"):
        packed = jnp.concatenate([w_second.reshape(576, 64), w_third.reshape(144, 64)], axis=0)
        others = call(
            other_weights_kernel, (shape((512, 768), bf16), shape((512, 256), bf16), shape((512, 256), bf16))
        )(packed)

    block = shape((2 * height, breadth), f32)
    with jax.named_scope("advance"):
        star = call(
            advance_kernel,
            block,
            (
                pltpu.VMEM((2, rows + 16, breadth + 128), f32),
                pltpu.VMEM((groups, span, 256), bf16),
                pltpu.VMEM((groups, span, 256), bf16),
                pltpu.VMEM((groups, 64, breadth + 128), f32),
                pltpu.VMEM((128, 128), f32),
            ),
            flops=10**9,
        )(both, bottom, top, right, left, kernel_1, *others, *biases)

    column, row, twiddle_out, twiddle_home = tables(height, breadth, members_x, members_y)
    column, row = [[jnp.asarray(t) for t in pair] for pair in (column, row)]
    spectra = call(column_kernel, block)(*gather_y(star), jnp.asarray(twiddle_out), *column)
    columns = call(
        functools.partial(row_kernel, scale=1.0 / (grid_x * grid_y)),
        block,
        (pltpu.VMEM((grid_x, 2 * breadth), f32),),
    )(*gather_x(spectra), *row, *column)
    part = shape((height, breadth), f32)
    return tuple(call(home_kernel, (part, part))(*gather_y(columns), jnp.asarray(twiddle_home), star))


def solution(mesh):
    return jax.shard_map(
        on_device,
        mesh=mesh,
        in_specs=(P("gx", "gy"), P("gx", "gy"), P(), P(), P(), P(), P(), P()),
        out_specs=(P("gx", "gy"), P("gx", "gy")),
        check_vma=False,
    )
```

```python
import functools
import math

import jax
import jax.numpy as jnp
import ml_dtypes
import numpy as np
from jax import lax
from jax.experimental import pallas as pl
from jax.experimental.pallas import tpu as pltpu
from jax.sharding import PartitionSpec as P

step_ratio = 0.4
stencil_base = (-0.0625, 0.5625, 0.5625, -0.0625)
f32 = jnp.float32
bf16 = jnp.bfloat16

vmem_limit = 48 * 1024 * 1024


def split(value):
    high = value.astype(bf16)
    return high, (value - high.astype(f32)).astype(bf16)


def split_table(table):
    high = table.astype(ml_dtypes.bfloat16)
    low = (table - high.astype(np.float64)).astype(ml_dtypes.bfloat16)
    return high, low


def dot(a, b):
    return jnp.dot(a, b, preferred_element_type=f32)


def product_3(value, high, low):
    rows = value.shape[0]
    first, second = split(value)
    both = dot(jnp.concatenate([first, second], axis=0), high)
    return both[:rows] + both[rows:] + dot(first, low)


def parity(shape):
    rows = lax.broadcasted_iota(jnp.int32, shape, 0)
    return jnp.where(rows < shape[0] // 2, 1.0, -1.0).astype(f32)


def swap(value):
    half = value.shape[0] // 2
    return jnp.concatenate([value[half:], value[:half]], axis=0)


def rows_kernel(both_ref, last_ref, first_ref):
    height = both_ref.shape[0] // 2
    for q in range(2):
        last_ref[4 * q : 4 * q + 4, :] = both_ref[height * (q + 1) - 4 : height * (q + 1), :]
        first_ref[4 * q : 4 * q + 4, :] = both_ref[height * q : height * q + 4, :]


def columns_kernel(both_ref, bot_ref, top_ref, order_ref, last_ref, first_ref, strip):
    height, breadth = both_ref.shape[0] // 2, both_ref.shape[1]
    rows = height + 8
    for side, out in ((0, first_ref), (breadth - 128, last_ref)):
        strip[...] = jnp.zeros_like(strip)
        for q in range(2):
            start = rows * q
            strip[start : start + height, :] = both_ref[height * q : height * (q + 1), side : side + 128]
            strip[start + height : start + height + 4, :] = bot_ref[4 * q : 4 * q + 4, side : side + 128]
            strip[start + height + 4 : start + rows, :] = top_ref[4 * q : 4 * q + 4, side : side + 128]
        turned = strip[...].T
        out[...] = turned[0:8] if side == 0 else turned[120:128]


def first_weights_kernel(packed_ref, k1_ref, c1_ref, c2_ref, c3_ref, *, rows):
    groups, depth, _ = k1_ref.shape
    packed = packed_ref[...]
    wide = jnp.concatenate([packed] * 4, axis=1)
    c1_ref[...] = wide[18:19]
    c2_ref[...] = wide[19:20]
    place = lax.broadcasted_iota(jnp.int32, (64, 64), 0) // 4
    channel = 8 * (place // 8) + 4 * (place % 2) + (place // 2) % 4
    hit = channel == lax.broadcasted_iota(jnp.int32, (64, 64), 1)
    c3_ref[...] = jnp.sum(jnp.where(hit, packed[20:21], 0.0), axis=1, keepdims=True)
    spread = []
    for d in range(3):
        parts = [
            jnp.broadcast_to(wide[(3 * d + s) * 2 + q : (3 * d + s) * 2 + q + 1, :], (rows, 256))
            for s in range(3)
            for q in range(2)
        ]
        parts.append(jnp.zeros((depth - 6 * rows, 256), f32))
        spread.append(jnp.concatenate(parts, axis=0))
    row = lax.broadcasted_iota(jnp.int32, (rows, 256), 0) - lax.broadcasted_iota(jnp.int32, (rows, 256), 1) // 64
    row = jnp.where(row < 0, row + rows, row)
    row = jnp.concatenate([row] * 6 + [jnp.full((depth - 6 * rows, 256), -1, jnp.int32)], axis=0)
    for r in range(groups):
        near = [row == (4 * r + d - 1) % rows for d in range(3)]
        block = jnp.where(near[0], spread[0], jnp.where(near[1], spread[1], jnp.where(near[2], spread[2], 0.0)))
        k1_ref[r] = block.astype(bf16)


def other_weights_kernel(packed_ref, k2_ref, even_ref, odd_ref):
    k2_ref[...] = jnp.zeros(k2_ref.shape, bf16)
    slots = {-1: 5, 0: 0, 1: 1, 2: 2, 3: 3, 4: 6}
    blank = jnp.zeros((64, 64), f32)
    for c in range(3):
        taps = [packed_ref[64 * (3 * d + c) : 64 * (3 * d + c) + 64, :].astype(f32) for d in range(3)]
        two = [(taps[0], blank), (taps[1], taps[0]), (taps[2], taps[1]), (blank, taps[2])]
        two = [jnp.concatenate(pair, axis=0).T.astype(bf16) for pair in two]
        for h in range(2):
            for d in range(4):
                slot = slots[d + 2 * h - 1]
                k2_ref[64 * slot : 64 * slot + 64, 256 * c + 128 * h : 256 * c + 128 * h + 128] = two[d]

    taps = [
        [packed_ref[576 + 16 * (3 * d + c) : 592 + 16 * (3 * d + c), :].astype(f32) for d in range(3)]
        for c in range(3)
    ]
    blank = jnp.zeros((16, 64), f32)
    filler = jnp.zeros((64, 256), bf16)
    parts = [filler] * 8
    for k, slot in slots.items():
        pieces = [taps[c][k - t + 1] if 0 <= k - t + 1 < 3 else blank for c in range(3) for t in range(4)]
        pieces += [blank] * 4
        parts[slot] = jnp.concatenate(pieces, axis=0).T.astype(bf16)
    raw = jnp.concatenate(parts, axis=0)
    source = lax.broadcasted_iota(jnp.int32, (256, 256), 0)
    target = lax.broadcasted_iota(jnp.int32, (256, 256), 1)
    inner = target % 64
    place = inner // 4
    channel = 8 * (place // 8) + 4 * (place % 2) + (place // 2) % 4
    lane = 16 * (inner % 4) + channel
    part = target // 64
    column_even = jnp.where(part == 3, -1, 64 * part + lane)
    column_odd = jnp.where(
        part == 2, -1, jnp.where(part == 3, 128 + lane, jnp.where(part == 0, 64 + lane, lane))
    )
    even_ref[...] = dot(raw, jnp.where(source == column_even, 1.0, 0.0).astype(bf16)).astype(bf16)
    odd_ref[...] = dot(raw, jnp.where(source == column_odd, 1.0, 0.0).astype(bf16)).astype(bf16)


def advance_kernel(
    both_ref, bot_ref, top_ref, right_ref, left_ref, w1_ref, w2_ref, w3e_ref, w3o_ref,
    b1_ref, b2_ref, b3_ref, star_ref, field, first, second, coeff, strip,
):
    height, breadth = both_ref.shape[0] // 2, both_ref.shape[1]
    rows = height + 8
    groups = rows // 4
    lanes = breadth + 128
    strip[...] = jnp.zeros_like(strip)
    strip[0:4, :] = right_ref[0:4, :]
    strip[124:128, :] = left_ref[4:8, :]
    beside = strip[...].T
    for q in range(2):
        field[q, 8 : 8 + height, :breadth] = both_ref[height * q : height * (q + 1), :]
        field[q, 8 + height : 12 + height, :breadth] = bot_ref[4 * q : 4 * q + 4, :]
        field[q, 12 + height : 16 + height, :breadth] = top_ref[4 * q : 4 * q + 4, :]
        field[q, 8 : 8 + rows, breadth:] = beside[rows * q : rows * q + rows]
        field[q, 0:8, :] = field[q, rows : rows + 8, :]
        field[q, 8 + rows : 16 + rows, :] = field[q, 8:16, :]
    whole = jnp.concatenate([field[0, 8 : 8 + rows], field[1, 8 : 8 + rows]], axis=0)
    pieces = [pltpu.roll(whole, 1, 1), whole, pltpu.roll(whole, lanes - 1, 1)]
    depth = w1_ref.shape[1]
    pieces.append(jnp.zeros((depth - 6 * rows, lanes), f32))
    turned = jnp.concatenate(pieces, axis=0).T
    patches = jnp.concatenate([turned[: breadth + 8], turned[lanes - 8 :]], axis=0).astype(bf16)
    span = breadth + 16
    for r in range(groups):
        first[r] = jnp.maximum(dot(patches, w1_ref[r]) + b1_ref[...], 0.0).astype(bf16)

    def gathered(source, r):
        before, after = (r - 1) % groups, (r + 1) % groups
        beside = jnp.concatenate([source[before, :, 128:], source[after, :, :128]], axis=1)
        return source[r], beside

    for r in range(groups):
        own, beside = gathered(first, r)
        total = dot(own, w2_ref[:256]) + dot(beside, w2_ref[256:])
        total = pltpu.roll(total[:, :256], 1, 0) + total[:, 256:512] + pltpu.roll(total[:, 512:], span - 1, 0)
        second[r] = jnp.maximum(total + b2_ref[...], 0.0).astype(bf16)

    def last(r, ref):
        own, beside = gathered(second, r)
        total = dot(own, ref[:256]) + dot(beside, ref[256:])
        left_part = total[:, :128]
        return pltpu.roll(left_part, 1, 0) + pltpu.roll(left_part, 64, 1) + pltpu.roll(total[:, 128:], span - 1, 0)

    def keep(r, block):
        coeff[r, :, :breadth] = block[:, :breadth]
        coeff[r, :, breadth:] = block[:, breadth:]

    pairs = [(i, i + 1) for i in range(0, groups - 2, 2)] + [(groups - 1, None)]
    for even, odd in pairs:
        block = last(even, w3e_ref)
        if odd is not None:
            other = last(odd, w3o_ref)
            lower = lax.broadcasted_iota(jnp.int32, block.shape, 1) < 64
            block = jnp.where(lower, block, other)
        block = jnp.concatenate(
            [block[: breadth + 8], jnp.zeros((lanes - span, 128), f32), block[breadth + 8 :]], axis=0
        ).T
        keep(even, block[:64])
        if odd is not None:
            keep(odd, block[64:])

    offsets = b3_ref[...]
    sub = lax.broadcasted_iota(jnp.int32, (8, breadth), 0) % 4

    def stacked(r, shift, qs=(0, 1)):
        start = 8 + 4 * r + shift
        return jnp.concatenate([field[q, start : start + 4, :] for q in qs], axis=0)

    previous = None
    for r in [groups - 1] + list(range(groups - 2)):
        weights = coeff[r] + offsets
        weights = [weights[8 * i : 8 * i + 8] for i in range(8)]
        centre = stacked(r, 0)

        def stencil(d):
            four = weights[4 * d : 4 * d + 4]
            mean = (four[0] + four[1] + four[2] + four[3]) * 0.25
            return [base + w - mean for base, w in zip(stencil_base, four)]

        east = stencil(0)
        flow_x = (
            east[0] * stacked(r, -1) + east[1] * centre + east[2] * stacked(r, 1) + east[3] * stacked(r, 2)
        )
        flow_x = flow_x * (0.5 * (stacked(r, 0, (0, 0)) + stacked(r, 1, (0, 0))))
        flow_x = flow_x[:, :breadth]
        if previous is not None:
            north = stencil(1)
            flow_y = (
                north[0] * pltpu.roll(centre, 1, 1)
                + north[1] * centre
                + north[2] * pltpu.roll(centre, lanes - 1, 1)
                + north[3] * pltpu.roll(centre, lanes - 2, 1)
            )
            carrier = stacked(r, 0, (1, 1))
            flow_y = flow_y * (0.5 * (carrier + pltpu.roll(carrier, lanes - 1, 1)))
            change_y = (flow_y - pltpu.roll(flow_y, 1, 1))[:, :breadth]
            above = jnp.where(sub == 0, pltpu.roll(previous, 5, 0), pltpu.roll(flow_x, 1, 0))
            star = centre[:, :breadth] - step_ratio * (flow_x - above + change_y)
            star_ref[4 * r : 4 * r + 4, :] = star[:4]
            star_ref[height + 4 * r : height + 4 * r + 4, :] = star[4:]
        previous = flow_x


def own_twiddle(ref):
    own = ref[lax.axis_index("gy")]
    half = own.shape[0] // 2
    return own[:half], own[half:]


def column_kernel(*refs):
    *blocks, twiddle_ref, high_ref, low_ref, out_ref = refs
    rows, breadth = out_ref.shape
    cosine, sine = own_twiddle(twiddle_ref)
    sign = parity((rows, breadth))
    mixed = None
    for k, ref in enumerate(blocks):
        block = ref[...] * sign
        term = block * cosine[k : k + 1, :] + swap(block) * (sign * sine[k : k + 1, :])
        mixed = term if mixed is None else mixed + term
    spectra = product_3(mixed, high_ref[...], low_ref[...])
    out_ref[...] = spectra[:, :breadth] + sign * swap(spectra[:, breadth:])


def join_kernel(*refs):
    *blocks, out_ref = refs
    for k, ref in enumerate(blocks):
        out_ref[k] = ref[...]


def row_kernel(own_ref, other_ref, table_ref, table_low_ref, high_ref, low_ref, out_ref, gathered, *, scale):
    rows, breadth = out_ref.shape
    height = rows // 2
    length = 2 * own_ref.shape[0] * height
    own_index = lax.axis_index("gx")
    for core, ref in enumerate((own_ref, other_ref)):
        for k in range(own_ref.shape[0]):
            start = pl.multiple_of((own_index ^ (2 * k + core)) * height, height)
            gathered[pl.ds(start, height), :breadth] = ref[k, :height, :]
            gathered[pl.ds(start, height), breadth:] = ref[k, height:, :]
    data = gathered[...]
    data, data_low = split(data)
    spectra = dot(table_ref[...], data) + dot(table_ref[...], data_low) + dot(table_low_ref[...], data)
    real_part = spectra[:length, :breadth] + spectra[length:, breadth:]
    imag_part = spectra[:length, breadth:] - spectra[length:, :breadth]
    index = lax.broadcasted_iota(jnp.int32, (length, breadth), 0)
    wave_x = jnp.where(index >= length // 2, index - length, index).astype(f32) * (2.0 * math.pi / length)
    members_y = lax.axis_size("gy")
    grid_y = members_y * breadth
    number_y = lax.axis_index("gy") + members_y * lax.broadcasted_iota(jnp.int32, (1, breadth), 1)
    wave_y = jnp.where(number_y >= grid_y // 2, number_y - grid_y, number_y).astype(f32) * (2.0 * math.pi / grid_y)
    edge_y = number_y == grid_y // 2
    edge_x = index == length // 2
    total = wave_x * wave_x + wave_y * wave_y
    zero = total == 0.0
    inverse = scale / jnp.where(zero, 1.0, total)
    same = (0.5 * inverse) * (wave_y * wave_y - wave_x * wave_x)
    cross = jnp.where(edge_x != edge_y, 0.0, -inverse * wave_x * wave_y)
    same_real = jnp.where(zero, 0.5 * scale, same)
    same_imag = jnp.where(zero, -0.5 * scale, same)
    kept_real = same_real * real_part - cross * imag_part
    kept_imag = same_imag * imag_part + cross * real_part
    kept, kept_low = split(jnp.concatenate([kept_real, kept_imag], axis=1))
    start = pl.multiple_of(own_index * height, height)

    def own(ref):
        parts = [ref[pl.ds(start, height), :], ref[pl.ds(pl.multiple_of(length + start, height), height), :]]
        return jnp.concatenate(parts, axis=0)

    table, table_low = own(table_ref), own(table_low_ref)
    home = dot(table, kept) + dot(table, kept_low) + dot(table_low, kept)
    home = jnp.concatenate(
        [
            home[:height, :breadth] - home[height:, breadth:],
            home[:height, breadth:] + home[height:, :breadth],
        ],
        axis=0,
    )
    columns = product_3(home, high_ref[...], low_ref[...])
    out_ref[...] = columns[:, :breadth] - parity((rows, breadth)) * swap(columns[:, breadth:])


def home_kernel(*refs):
    *blocks, twiddle_ref, star_ref, u_ref, v_ref = refs
    rows, breadth = star_ref.shape
    cosine, sine = own_twiddle(twiddle_ref)
    sign = parity((rows, breadth))
    result = 0.5 * star_ref[...]
    for k, ref in enumerate(blocks):
        block = ref[...]
        result = result + block * cosine[k : k + 1, :] - swap(block) * (sign * sine[k : k + 1, :])
    u_ref[...] = result[: rows // 2]
    v_ref[...] = result[rows // 2 :]


def call(kernel, shapes, scratch=(), flops=10**7):
    return pl.pallas_call(
        kernel,
        out_shape=shapes,
        scratch_shapes=list(scratch),
        compiler_params=pltpu.CompilerParams(vmem_limit_bytes=vmem_limit),
        cost_estimate=pl.CostEstimate(flops=flops, bytes_accessed=2**20, transcendentals=0),
    )


@functools.lru_cache(None)
def tables(height, breadth, members_x, members_y):
    turn = 2.0 * math.pi
    j = np.arange(breadth)
    phase = turn * (np.outer(j, j) % breadth) / breadth
    column = split_table(np.concatenate([np.cos(phase), np.sin(phase)], axis=1))
    length = height * members_x
    k = np.arange(length)
    phase = turn * (np.outer(k, k) % length) / length
    row = split_table(np.concatenate([np.cos(phase), np.sin(phase)], axis=0))
    g = np.arange(members_y)[:, None, None]
    partner = g ^ np.arange(members_y)[None, :, None]
    whole = breadth * members_y
    out = turn * ((partner * breadth + j) * g % whole) / whole
    home = turn * ((g * breadth + j) * partner % whole) / whole
    twiddle_out, twiddle_home = [
        np.concatenate([np.cos(phase), np.sin(phase)], axis=1).astype(np.float32) for phase in (out, home)
    ]
    return column, row, twiddle_out, twiddle_home


def partner(block, axis, k):
    return lax.ppermute(block, axis, [(i, i ^ k) for i in range(lax.axis_size(axis))])


def gather_y(block):
    return [block] + [partner(block, "gy", k) for k in range(1, lax.axis_size("gy"))]


def gather_x(block):
    blocks = [block] + [partner(block, "gx", k) for k in range(2, lax.axis_size("gx"), 2)]
    own = call(join_kernel, jax.ShapeDtypeStruct((len(blocks), *block.shape), f32))(*blocks)
    return own, partner(own, "gx", 1)


def on_device(u_field, v_field, w_first, b_first, w_second, b_second, w_third, b_third):
    height, breadth = u_field.shape
    members_x, members_y = lax.axis_size("gx"), lax.axis_size("gy")
    grid_x, grid_y = height * members_x, breadth * members_y
    rows = height + 8
    groups = rows // 4
    span = breadth + 16
    shape = jax.ShapeDtypeStruct

    def shifted(value, axis, distance):
        peers = lax.axis_size(axis)
        return lax.ppermute(value, axis, [(i, (i + distance) % peers) for i in range(peers)])

    with jax.named_scope("rows_around"):
        component = lax.broadcasted_iota(jnp.int32, (2, height, breadth), 0)
        both = jnp.where(component == 0, u_field[None], v_field[None]).reshape(2 * height, breadth)
        edge = shape((8, breadth), f32)
        last, first = call(rows_kernel, (edge, edge))(both)
        top, bottom = shifted(last, "gx", 1), shifted(first, "gx", -1)

    with jax.named_scope("weights"):
        biases = jnp.stack([b_first, b_second, jnp.pad(b_third, (0, 64 - b_third.shape[0]))])
        packed = jnp.concatenate([w_first.transpose(0, 2, 1).reshape(18, 64).astype(f32), biases], axis=0)
        kernel_1, *biases = call(
            functools.partial(first_weights_kernel, rows=rows),
            (
                shape((groups, -(-6 * rows // 128) * 128, 256), bf16),
                shape((1, 256), f32),
                shape((1, 256), f32),
                shape((64, 1), f32),
            ),
        )(packed)

    with jax.named_scope("columns_around"):
        edge = shape((8, 128), f32)
        last, first = call(columns_kernel, (edge, edge), (pltpu.VMEM((128, 128), f32),))(
            both, bottom, top, biases[2]
        )
        left, right = shifted(last, "gy", 1), shifted(first, "gy", -1)

    with jax.named_scope("weights"):
        packed = jnp.concatenate([w_second.reshape(576, 64), w_third.reshape(144, 64)], axis=0)
        others = call(
            other_weights_kernel, (shape((512, 768), bf16), shape((512, 256), bf16), shape((512, 256), bf16))
        )(packed)

    block = shape((2 * height, breadth), f32)
    with jax.named_scope("advance"):
        star = call(
            advance_kernel,
            block,
            (
                pltpu.VMEM((2, rows + 16, breadth + 128), f32),
                pltpu.VMEM((groups, span, 256), bf16),
                pltpu.VMEM((groups, span, 256), bf16),
                pltpu.VMEM((groups, 64, breadth + 128), f32),
                pltpu.VMEM((128, 128), f32),
            ),
            flops=10**9,
        )(both, bottom, top, right, left, kernel_1, *others, *biases)

    column, row, twiddle_out, twiddle_home = tables(height, breadth, members_x, members_y)
    column, row = [[jnp.asarray(t) for t in pair] for pair in (column, row)]
    spectra = call(column_kernel, block)(*gather_y(star), jnp.asarray(twiddle_out), *column)
    columns = call(
        functools.partial(row_kernel, scale=1.0 / (grid_x * grid_y)),
        block,
        (pltpu.VMEM((grid_x, 2 * breadth), f32),),
    )(*gather_x(spectra), *row, *column)
    part = shape((height, breadth), f32)
    return tuple(call(home_kernel, (part, part))(*gather_y(columns), jnp.asarray(twiddle_home), star))


def solution(mesh):
    return jax.shard_map(
        on_device,
        mesh=mesh,
        in_specs=(P("gx", "gy"), P("gx", "gy"), P(), P(), P(), P(), P(), P()),
        out_specs=(P("gx", "gy"), P("gx", "gy")),
        check_vma=False,
    )
```

```python
import functools
import math

import jax
import jax.numpy as jnp
import ml_dtypes
import numpy as np
from jax import lax
from jax.experimental import pallas as pl
from jax.experimental.pallas import tpu as pltpu
from jax.sharding import PartitionSpec as P

step_ratio = 0.4
stencil_base = (-0.0625, 0.5625, 0.5625, -0.0625)
f32 = jnp.float32
bf16 = jnp.bfloat16

vmem_limit = 48 * 1024 * 1024


def split(value):
    high = value.astype(bf16)
    return high, (value - high.astype(f32)).astype(bf16)


def split_table(table):
    high = table.astype(ml_dtypes.bfloat16)
    low = (table - high.astype(np.float64)).astype(ml_dtypes.bfloat16)
    return high, low


def dot(a, b):
    return jnp.dot(a, b, preferred_element_type=f32)


def product_3(value, high, low):
    rows = value.shape[0]
    first, second = split(value)
    both = dot(jnp.concatenate([first, second], axis=0), high)
    return both[:rows] + both[rows:] + dot(first, low)


def parity(shape):
    rows = lax.broadcasted_iota(jnp.int32, shape, 0)
    return jnp.where(rows < shape[0] // 2, 1.0, -1.0).astype(f32)


def swap(value):
    half = value.shape[0] // 2
    return jnp.concatenate([value[half:], value[:half]], axis=0)


def columns_kernel(both_ref, last_ref, first_ref, strip):
    cells, breadth = both_ref.shape
    strip[cells:, :] = jnp.zeros((128 - cells, 128), f32)
    for side, out in ((0, first_ref), (breadth - 128, last_ref)):
        strip[:cells, :] = both_ref[:, side : side + 128]
        turned = strip[...].T
        out[...] = turned[0:8] if side == 0 else turned[120:128]


def rows_kernel(both_ref, right_ref, left_ref, order_ref, order_too_ref, last_ref, first_ref, beside_ref, strip):
    height, breadth = both_ref.shape[0] // 2, both_ref.shape[1]
    strip[...] = jnp.zeros_like(strip)
    strip[0:4, :] = right_ref[0:4, :]
    strip[124:128, :] = left_ref[4:8, :]
    beside_ref[...] = strip[...].T[: 2 * height]
    for q in range(2):
        start, end, own = height * q, height * (q + 1), slice(4 * q, 4 * q + 4)
        last_ref[own, :breadth] = both_ref[end - 4 : end, :]
        last_ref[own, breadth:] = beside_ref[end - 4 : end, :]
        first_ref[own, :breadth] = both_ref[start : start + 4, :]
        first_ref[own, breadth:] = beside_ref[start : start + 4, :]


def first_weights_kernel(packed_ref, k1_ref, c1_ref, c2_ref, c3_ref, *, rows):
    groups, depth, _ = k1_ref.shape
    packed = packed_ref[...]
    wide = jnp.concatenate([packed] * 4, axis=1)
    c1_ref[...] = wide[18:19]
    c2_ref[...] = wide[19:20]
    place = lax.broadcasted_iota(jnp.int32, (64, 64), 0) // 4
    channel = 8 * (place // 8) + 4 * (place % 2) + (place // 2) % 4
    hit = channel == lax.broadcasted_iota(jnp.int32, (64, 64), 1)
    c3_ref[...] = jnp.sum(jnp.where(hit, packed[20:21], 0.0), axis=1, keepdims=True)
    spread = []
    for d in range(3):
        parts = [
            jnp.broadcast_to(wide[(3 * d + s) * 2 + q : (3 * d + s) * 2 + q + 1, :], (rows, 256))
            for s in range(3)
            for q in range(2)
        ]
        parts.append(jnp.zeros((depth - 6 * rows, 256), f32))
        spread.append(jnp.concatenate(parts, axis=0))
    row = lax.broadcasted_iota(jnp.int32, (rows, 256), 0) - lax.broadcasted_iota(jnp.int32, (rows, 256), 1) // 64
    row = jnp.where(row < 0, row + rows, row)
    row = jnp.concatenate([row] * 6 + [jnp.full((depth - 6 * rows, 256), -1, jnp.int32)], axis=0)
    for r in range(groups):
        near = [row == (4 * r + d - 1) % rows for d in range(3)]
        block = jnp.where(near[0], spread[0], jnp.where(near[1], spread[1], jnp.where(near[2], spread[2], 0.0)))
        k1_ref[r] = block.astype(bf16)


def other_weights_kernel(packed_ref, k2_ref, even_ref, odd_ref, order_ref):
    order_ref[...] = jnp.zeros(order_ref.shape, f32)
    k2_ref[...] = jnp.zeros(k2_ref.shape, bf16)
    slots = {-1: 5, 0: 0, 1: 1, 2: 2, 3: 3, 4: 6}
    blank = jnp.zeros((64, 64), f32)
    for c in range(3):
        taps = [packed_ref[64 * (3 * d + c) : 64 * (3 * d + c) + 64, :].astype(f32) for d in range(3)]
        two = [(taps[0], blank), (taps[1], taps[0]), (taps[2], taps[1]), (blank, taps[2])]
        two = [jnp.concatenate(pair, axis=0).T.astype(bf16) for pair in two]
        for h in range(2):
            for d in range(4):
                slot = slots[d + 2 * h - 1]
                k2_ref[64 * slot : 64 * slot + 64, 256 * c + 128 * h : 256 * c + 128 * h + 128] = two[d]

    taps = [
        [packed_ref[576 + 16 * (3 * d + c) : 592 + 16 * (3 * d + c), :].astype(f32) for d in range(3)]
        for c in range(3)
    ]
    blank = jnp.zeros((16, 64), f32)
    filler = jnp.zeros((64, 256), bf16)
    parts = [filler] * 8
    for k, slot in slots.items():
        pieces = [taps[c][k - t + 1] if 0 <= k - t + 1 < 3 else blank for c in range(3) for t in range(4)]
        pieces += [blank] * 4
        parts[slot] = jnp.concatenate(pieces, axis=0).T.astype(bf16)
    raw = jnp.concatenate(parts, axis=0)
    source = lax.broadcasted_iota(jnp.int32, (256, 256), 0)
    target = lax.broadcasted_iota(jnp.int32, (256, 256), 1)
    inner = target % 64
    place = inner // 4
    channel = 8 * (place // 8) + 4 * (place % 2) + (place // 2) % 4
    lane = 16 * (inner % 4) + channel
    part = target // 64
    column_even = jnp.where(part == 3, -1, 64 * part + lane)
    column_odd = jnp.where(
        part == 2, -1, jnp.where(part == 3, 128 + lane, jnp.where(part == 0, 64 + lane, lane))
    )
    even_ref[...] = dot(raw, jnp.where(source == column_even, 1.0, 0.0).astype(bf16)).astype(bf16)
    odd_ref[...] = dot(raw, jnp.where(source == column_odd, 1.0, 0.0).astype(bf16)).astype(bf16)


def fill(field, both_ref, beside_ref, height, breadth):
    for q in range(2):
        field[q, 8 : 8 + height, :breadth] = both_ref[height * q : height * (q + 1), :]
        field[q, 8 : 8 + height, breadth:] = beside_ref[height * q : height * (q + 1), :]


def patches_of(field, rows, depth):
    lanes = field.shape[2]
    whole = jnp.concatenate([field[0, 8 : 8 + rows], field[1, 8 : 8 + rows]], axis=0)
    pieces = [pltpu.roll(whole, 1, 1), whole, pltpu.roll(whole, lanes - 1, 1)]
    pieces.append(jnp.zeros((depth - 6 * rows, lanes), f32))
    turned = jnp.concatenate(pieces, axis=0).T
    return jnp.concatenate([turned[: lanes - 120], turned[lanes - 8 :]], axis=0).astype(bf16)


def layer_1(patches, weights_ref, bias_ref, r):
    return jnp.maximum(dot(patches, weights_ref[r]) + bias_ref[...], 0.0).astype(bf16)


def with_neighbours(before, own, after, weights_ref):
    beside = jnp.concatenate([before[:, 128:], after[:, :128]], axis=1)
    return dot(own[...], weights_ref[:256]) + dot(beside, weights_ref[256:])


def layer_2(before, own, after, weights_ref, bias_ref):
    total = with_neighbours(before, own, after, weights_ref)
    span = total.shape[0]
    total = pltpu.roll(total[:, :256], 1, 0) + total[:, 256:512] + pltpu.roll(total[:, 512:], span - 1, 0)
    return jnp.maximum(total + bias_ref[...], 0.0).astype(bf16)


def layer_3(second, groups, r, weights_ref):
    total = with_neighbours(second((r - 1) % groups), second(r), second((r + 1) % groups), weights_ref)
    left_part = total[:, :128]
    return (
        pltpu.roll(left_part, 1, 0)
        + pltpu.roll(left_part, 64, 1)
        + pltpu.roll(total[:, 128:], total.shape[0] - 1, 0)
    )


def coefficients(second, groups, even, odd, even_ref, odd_ref):
    block = layer_3(second, groups, even, even_ref)
    if odd is not None:
        lower = lax.broadcasted_iota(jnp.int32, block.shape, 1) < 64
        block = jnp.where(lower, block, layer_3(second, groups, odd, odd_ref))
    span = block.shape[0]
    filler = jnp.zeros((112, 128), f32)
    return jnp.concatenate([block[: span - 8], filler, block[span - 8 :]], axis=0).T


def inner_kernel(
    both_ref, beside_ref, w1_ref, w2_ref, even_ref, odd_ref, b1_ref, b2_ref, first_ref, second_ref, coeff_ref, field
):
    height, breadth = both_ref.shape[0] // 2, both_ref.shape[1]
    rows = height + 8
    groups = rows // 4
    field[...] = jnp.zeros_like(field)
    fill(field, both_ref, beside_ref, height, breadth)
    patches = patches_of(field, rows, w1_ref.shape[1])
    for r in range(1, groups - 3):
        first_ref[r - 1] = layer_1(patches, w1_ref, b1_ref, r)
        if r >= 3:
            second_ref[r - 3] = layer_2(
                first_ref.at[r - 3], first_ref.at[r - 2], first_ref.at[r - 1], w2_ref, b2_ref
            )
    block = coefficients(lambda r: second_ref.at[r - 2], groups, 3, 4, even_ref, odd_ref)
    coeff_ref[0] = block[:64]
    coeff_ref[1] = block[64:]


def advance_kernel(
    both_ref, beside_ref, bot_ref, top_ref, w1_ref, w2_ref, even_ref, odd_ref, b1_ref, b2_ref, b3_ref,
    first_ref, second_ref, coeff_ref, star_ref, field, outer_first, outer_second, outer_coeff,
):
    height, breadth = both_ref.shape[0] // 2, both_ref.shape[1]
    rows = height + 8
    groups = rows // 4
    lanes = breadth + 128
    fill(field, both_ref, beside_ref, height, breadth)
    for q in range(2):
        field[q, 8 + height : 12 + height, :] = bot_ref[4 * q : 4 * q + 4, :]
        field[q, 12 + height : 16 + height, :] = top_ref[4 * q : 4 * q + 4, :]
        field[q, 0:8, :] = field[q, rows : rows + 8, :]
        field[q, 8 + rows : 16 + rows, :] = field[q, 8:16, :]
    patches = patches_of(field, rows, w1_ref.shape[1])

    ends = (groups - 3, groups - 2, groups - 1, 0, 1, groups - 4)

    def first(r):
        return outer_first.at[ends.index(r)] if r in ends[:4] else first_ref.at[r - 1]

    def second(r):
        return outer_second.at[ends.index(r)] if r in ends else second_ref.at[r - 2]

    held = {3: coeff_ref.at[0], 4: coeff_ref.at[1]}

    def do_first(r):
        outer_first[ends.index(r)] = layer_1(patches, w1_ref, b1_ref, r)

    def do_second(r):
        outer_second[ends.index(r)] = layer_2(
            first((r - 1) % groups), first(r), first((r + 1) % groups), w2_ref, b2_ref
        )

    def do_coefficients(even, odd):
        block = coefficients(second, groups, even, odd, even_ref, odd_ref)
        for r, part in ((even, block[:64]), (odd, block[64:])):
            if r is not None:
                place = len(held)
                outer_coeff[place - 2] = part
                held[r] = outer_coeff.at[place - 2]

    offsets = b3_ref[...]
    sub = lax.broadcasted_iota(jnp.int32, (8, breadth), 0) % 4

    def stacked(r, shift, qs=(0, 1)):
        start = 8 + 4 * r + shift
        return jnp.concatenate([field[q, start : start + 4, :] for q in qs], axis=0)

    def flows(r, previous):
        weights = held[r][...] + offsets
        weights = [weights[8 * i : 8 * i + 8] for i in range(8)]
        centre = stacked(r, 0)

        def stencil(d):
            four = weights[4 * d : 4 * d + 4]
            mean = (four[0] + four[1] + four[2] + four[3]) * 0.25
            return [base + w - mean for base, w in zip(stencil_base, four)]

        east = stencil(0)
        flow_x = (
            east[0] * stacked(r, -1) + east[1] * centre + east[2] * stacked(r, 1) + east[3] * stacked(r, 2)
        )
        flow_x = flow_x * (0.5 * (stacked(r, 0, (0, 0)) + stacked(r, 1, (0, 0))))
        flow_x = flow_x[:, :breadth]
        if previous is not None:
            north = stencil(1)
            flow_y = (
                north[0] * pltpu.roll(centre, 1, 1)
                + north[1] * centre
                + north[2] * pltpu.roll(centre, lanes - 1, 1)
                + north[3] * pltpu.roll(centre, lanes - 2, 1)
            )
            carrier = stacked(r, 0, (1, 1))
            flow_y = flow_y * (0.5 * (carrier + pltpu.roll(carrier, lanes - 1, 1)))
            change_y = (flow_y - pltpu.roll(flow_y, 1, 1))[:, :breadth]
            above = jnp.where(sub == 0, pltpu.roll(previous, 5, 0), pltpu.roll(flow_x, 1, 0))
            star = centre[:, :breadth] - step_ratio * (flow_x - above + change_y)
            star_ref[4 * r : 4 * r + 4, :] = star[:4]
            star_ref[height + 4 * r : height + 4 * r + 4, :] = star[4:]
        return flow_x

    for r in ends[:4]:
        do_first(r)
    for r in ends[1:5]:
        do_second(r)
    do_coefficients(groups - 1, None)
    do_coefficients(0, 1)
    do_second(groups - 4)
    previous = flows(groups - 1, None)
    previous = flows(0, previous)
    previous = flows(1, previous)
    inner = list(range(5, groups - 4))
    do_coefficients(2, inner[0])
    do_second(groups - 3)
    for r in range(2, 5):
        previous = flows(r, previous)
    do_coefficients(groups - 4, groups - 3)
    for r in range(5, groups - 2):
        previous = flows(r, previous)


def own_twiddle(ref):
    own = ref[lax.axis_index("gy")]
    half = own.shape[0] // 2
    return own[:half], own[half:]


def column_kernel(*refs):
    *blocks, twiddle_ref, high_ref, low_ref, out_ref = refs
    rows, breadth = out_ref.shape
    cosine, sine = own_twiddle(twiddle_ref)
    sign = parity((rows, breadth))
    mixed = None
    for k, ref in enumerate(blocks):
        block = ref[...] * sign
        term = block * cosine[k : k + 1, :] + swap(block) * (sign * sine[k : k + 1, :])
        mixed = term if mixed is None else mixed + term
    spectra = product_3(mixed, high_ref[...], low_ref[...])
    out_ref[...] = spectra[:, :breadth] + sign * swap(spectra[:, breadth:])


def row_kernel(*refs, scale):
    *blocks, table_ref, table_low_ref, high_ref, low_ref, out_ref, gathered = refs
    rows, breadth = out_ref.shape
    height = rows // 2
    length = len(blocks) * height
    own_index = lax.axis_index("gx")
    for k, ref in enumerate(blocks):
        start = pl.multiple_of((own_index ^ k) * height, height)
        gathered[pl.ds(start, height), :breadth] = ref[:height, :]
        gathered[pl.ds(start, height), breadth:] = ref[height:, :]
    data = gathered[...]
    data, data_low = split(data)
    spectra = dot(table_ref[...], data) + dot(table_ref[...], data_low) + dot(table_low_ref[...], data)
    real_part = spectra[:length, :breadth] + spectra[length:, breadth:]
    imag_part = spectra[:length, breadth:] - spectra[length:, :breadth]
    index = lax.broadcasted_iota(jnp.int32, (length, breadth), 0)
    wave_x = jnp.where(index >= length // 2, index - length, index).astype(f32) * (2.0 * math.pi / length)
    members_y = lax.axis_size("gy")
    grid_y = members_y * breadth
    number_y = lax.axis_index("gy") + members_y * lax.broadcasted_iota(jnp.int32, (1, breadth), 1)
    wave_y = jnp.where(number_y >= grid_y // 2, number_y - grid_y, number_y).astype(f32) * (2.0 * math.pi / grid_y)
    edge_y = number_y == grid_y // 2
    edge_x = index == length // 2
    total = wave_x * wave_x + wave_y * wave_y
    zero = total == 0.0
    inverse = scale / jnp.where(zero, 1.0, total)
    same = (0.5 * inverse) * (wave_y * wave_y - wave_x * wave_x)
    cross = jnp.where(edge_x != edge_y, 0.0, -inverse * wave_x * wave_y)
    same_real = jnp.where(zero, 0.5 * scale, same)
    same_imag = jnp.where(zero, -0.5 * scale, same)
    kept_real = same_real * real_part - cross * imag_part
    kept_imag = same_imag * imag_part + cross * real_part
    kept, kept_low = split(jnp.concatenate([kept_real, kept_imag], axis=1))
    start = pl.multiple_of(own_index * height, height)

    def own(ref):
        parts = [ref[pl.ds(start, height), :], ref[pl.ds(pl.multiple_of(length + start, height), height), :]]
        return jnp.concatenate(parts, axis=0)

    table, table_low = own(table_ref), own(table_low_ref)
    home = dot(table, kept) + dot(table, kept_low) + dot(table_low, kept)
    home = jnp.concatenate(
        [
            home[:height, :breadth] - home[height:, breadth:],
            home[:height, breadth:] + home[height:, :breadth],
        ],
        axis=0,
    )
    columns = product_3(home, high_ref[...], low_ref[...])
    out_ref[...] = columns[:, :breadth] - parity((rows, breadth)) * swap(columns[:, breadth:])


def home_kernel(*refs):
    *blocks, twiddle_ref, star_ref, u_ref, v_ref = refs
    rows, breadth = star_ref.shape
    cosine, sine = own_twiddle(twiddle_ref)
    sign = parity((rows, breadth))
    result = 0.5 * star_ref[...]
    for k, ref in enumerate(blocks):
        block = ref[...]
        result = result + block * cosine[k : k + 1, :] - swap(block) * (sign * sine[k : k + 1, :])
    u_ref[...] = result[: rows // 2]
    v_ref[...] = result[rows // 2 :]


def call(kernel, shapes, scratch=(), flops=10**7):
    return pl.pallas_call(
        kernel,
        out_shape=shapes,
        scratch_shapes=list(scratch),
        compiler_params=pltpu.CompilerParams(vmem_limit_bytes=vmem_limit),
        cost_estimate=pl.CostEstimate(flops=flops, bytes_accessed=2**20, transcendentals=0),
    )


@functools.lru_cache(None)
def tables(height, breadth, members_x, members_y):
    turn = 2.0 * math.pi
    j = np.arange(breadth)
    phase = turn * (np.outer(j, j) % breadth) / breadth
    column = split_table(np.concatenate([np.cos(phase), np.sin(phase)], axis=1))
    length = height * members_x
    k = np.arange(length)
    phase = turn * (np.outer(k, k) % length) / length
    row = split_table(np.concatenate([np.cos(phase), np.sin(phase)], axis=0))
    g = np.arange(members_y)[:, None, None]
    partner = g ^ np.arange(members_y)[None, :, None]
    whole = breadth * members_y
    out = turn * ((partner * breadth + j) * g % whole) / whole
    home = turn * ((g * breadth + j) * partner % whole) / whole
    twiddle_out, twiddle_home = [
        np.concatenate([np.cos(phase), np.sin(phase)], axis=1).astype(np.float32) for phase in (out, home)
    ]
    return column, row, twiddle_out, twiddle_home


def partner(block, axis, k):
    return lax.ppermute(block, axis, [(i, i ^ k) for i in range(lax.axis_size(axis))])


def gather_y(block):
    return [block] + [partner(block, "gy", k) for k in range(1, lax.axis_size("gy"))]


def gather_x(block):
    own = [block] + [partner(block, "gx", k) for k in range(2, lax.axis_size("gx"), 2)]
    return [other for held in own for other in (held, partner(held, "gx", 1))]


def on_device(u_field, v_field, w_first, b_first, w_second, b_second, w_third, b_third):
    height, breadth = u_field.shape
    members_x, members_y = lax.axis_size("gx"), lax.axis_size("gy")
    grid_x, grid_y = height * members_x, breadth * members_y
    rows = height + 8
    groups = rows // 4
    span = breadth + 16
    shape = jax.ShapeDtypeStruct

    def shifted(value, axis, distance):
        peers = lax.axis_size(axis)
        return lax.ppermute(value, axis, [(i, (i + distance) % peers) for i in range(peers)])

    with jax.named_scope("columns_around"):
        component = lax.broadcasted_iota(jnp.int32, (2, height, breadth), 0)
        both = jnp.where(component == 0, u_field[None], v_field[None]).reshape(2 * height, breadth)
        edge = shape((8, 128), f32)
        last, first = call(columns_kernel, (edge, edge), (pltpu.VMEM((128, 128), f32),))(both)
        left, right = shifted(last, "gy", 1), shifted(first, "gy", -1)

    with jax.named_scope("weights"):
        biases = jnp.stack([b_first, b_second, jnp.pad(b_third, (0, 64 - b_third.shape[0]))])
        packed = jnp.concatenate([w_first.transpose(0, 2, 1).reshape(18, 64).astype(f32), biases], axis=0)
        kernel_1, *biases = call(
            functools.partial(first_weights_kernel, rows=rows),
            (
                shape((groups, -(-6 * rows // 128) * 128, 256), bf16),
                shape((1, 256), f32),
                shape((1, 256), f32),
                shape((64, 1), f32),
            ),
        )(packed)
        packed = jnp.concatenate([w_second.reshape(576, 64), w_third.reshape(144, 64)], axis=0)
        *others, order = call(
            other_weights_kernel,
            (shape((512, 768), bf16), shape((512, 256), bf16), shape((512, 256), bf16), shape((8, 128), f32)),
        )(packed)

    with jax.named_scope("rows_around"):
        edge = shape((8, breadth + 128), f32)
        last, first, beside = call(
            rows_kernel, (edge, edge, shape((2 * height, 128), f32)), (pltpu.VMEM((128, 128), f32),)
        )(both, right, left, biases[2], order)
        top, bottom = shifted(last, "gx", 1), shifted(first, "gx", -1)

    block = shape((2 * height, breadth), f32)
    padded = pltpu.VMEM((2, rows + 16, breadth + 128), f32)
    with jax.named_scope("advance"):
        inner = call(
            inner_kernel,
            (
                shape((groups - 4, span, 256), bf16),
                shape((groups - 6, span, 256), bf16),
                shape((2, 64, breadth + 128), f32),
            ),
            (padded,),
            flops=5 * 10**8,
        )(both, beside, kernel_1, *others, *biases[:2])
        star = call(
            advance_kernel,
            block,
            (
                padded,
                pltpu.VMEM((4, span, 256), bf16),
                pltpu.VMEM((6, span, 256), bf16),
                pltpu.VMEM((groups - 3, 64, breadth + 128), f32),
            ),
            flops=10**9,
        )(both, beside, bottom, top, kernel_1, *others, *biases, *inner)

    column, row, twiddle_out, twiddle_home = tables(height, breadth, members_x, members_y)
    column, row = [[jnp.asarray(t) for t in pair] for pair in (column, row)]
    spectra = call(column_kernel, block)(*gather_y(star), jnp.asarray(twiddle_out), *column)
    columns = call(
        functools.partial(row_kernel, scale=1.0 / (grid_x * grid_y)),
        block,
        (pltpu.VMEM((grid_x, 2 * breadth), f32),),
    )(*gather_x(spectra), *row, *column)
    part = shape((height, breadth), f32)
    return tuple(call(home_kernel, (part, part))(*gather_y(columns), jnp.asarray(twiddle_home), star))


def solution(mesh):
    return jax.shard_map(
        on_device,
        mesh=mesh,
        in_specs=(P("gx", "gy"), P("gx", "gy"), P(), P(), P(), P(), P(), P()),
        out_specs=(P("gx", "gy"), P("gx", "gy")),
        check_vma=False,
    )
```

```python
import functools
import math

import jax
import jax.numpy as jnp
import ml_dtypes
import numpy as np
from jax import lax
from jax.experimental import pallas as pl
from jax.experimental.pallas import tpu as pltpu
from jax.sharding import PartitionSpec as P

step_ratio = 0.4
stencil_base = (-0.0625, 0.5625, 0.5625, -0.0625)
f32 = jnp.float32
bf16 = jnp.bfloat16

vmem_limit = 48 * 1024 * 1024


def split(value):
    high = value.astype(bf16)
    return high, (value - high.astype(f32)).astype(bf16)


def split_table(table):
    high = table.astype(ml_dtypes.bfloat16)
    low = (table - high.astype(np.float64)).astype(ml_dtypes.bfloat16)
    return high, low


def dot(a, b):
    return jnp.dot(a, b, preferred_element_type=f32)


def product_3(value, high, low):
    rows = value.shape[0]
    first, second = split(value)
    both = dot(jnp.concatenate([first, second], axis=0), high)
    return both[:rows] + both[rows:] + dot(first, low)


def parity(shape):
    rows = lax.broadcasted_iota(jnp.int32, shape, 0)
    return jnp.where(rows < shape[0] // 2, 1.0, -1.0).astype(f32)


def swap(value):
    half = value.shape[0] // 2
    return jnp.concatenate([value[half:], value[:half]], axis=0)


def columns_kernel(both_ref, last_ref, first_ref, strip):
    cells, breadth = both_ref.shape
    strip[cells:, :] = jnp.zeros((128 - cells, 128), f32)
    for side, out in ((0, first_ref), (breadth - 128, last_ref)):
        strip[:cells, :] = both_ref[:, side : side + 128]
        turned = strip[...].T
        out[...] = turned[0:8] if side == 0 else turned[120:128]


def rows_kernel(both_ref, right_ref, left_ref, order_ref, order_too_ref, last_ref, first_ref, beside_ref, strip):
    height, breadth = both_ref.shape[0] // 2, both_ref.shape[1]
    strip[...] = jnp.zeros_like(strip)
    strip[0:4, :] = right_ref[0:4, :]
    strip[124:128, :] = left_ref[4:8, :]
    beside_ref[...] = strip[...].T[: 2 * height]
    for q in range(2):
        start, end, own = height * q, height * (q + 1), slice(4 * q, 4 * q + 4)
        last_ref[own, :breadth] = both_ref[end - 4 : end, :]
        last_ref[own, breadth:] = beside_ref[end - 4 : end, :]
        first_ref[own, :breadth] = both_ref[start : start + 4, :]
        first_ref[own, breadth:] = beside_ref[start : start + 4, :]


def first_weights_kernel(taps_ref, biases_ref, k1_ref, c1_ref, c2_ref, c3_ref, *, rows):
    groups, depth, _ = k1_ref.shape
    wide = [jnp.concatenate([taps_ref[i]] * 4, axis=1) for i in range(9)]
    c1_ref[...] = jnp.concatenate([biases_ref[:, :64]] * 4, axis=1)
    c2_ref[...] = jnp.concatenate([biases_ref[:, 64:128]] * 4, axis=1)
    place = lax.broadcasted_iota(jnp.int32, (64, 16), 0) // 4
    channel = 8 * (place // 8) + 4 * (place % 2) + (place // 2) % 4
    hit = channel == lax.broadcasted_iota(jnp.int32, (64, 16), 1)
    c3_ref[...] = jnp.sum(jnp.where(hit, biases_ref[:, 128:144], 0.0), axis=1, keepdims=True)
    spread = []
    for d in range(3):
        parts = [
            jnp.broadcast_to(wide[3 * d + s][q : q + 1, :], (rows, 256))
            for s in range(3)
            for q in range(2)
        ]
        parts.append(jnp.zeros((depth - 6 * rows, 256), f32))
        spread.append(jnp.concatenate(parts, axis=0))
    row = lax.broadcasted_iota(jnp.int32, (rows, 256), 0) - lax.broadcasted_iota(jnp.int32, (rows, 256), 1) // 64
    row = jnp.where(row < 0, row + rows, row)
    row = jnp.concatenate([row] * 6 + [jnp.full((depth - 6 * rows, 256), -1, jnp.int32)], axis=0)
    for r in range(groups):
        near = [row == (4 * r + d - 1) % rows for d in range(3)]
        block = jnp.where(near[0], spread[0], jnp.where(near[1], spread[1], jnp.where(near[2], spread[2], 0.0)))
        k1_ref[r] = block.astype(bf16)


def other_weights_kernel(packed_ref, k2_ref, even_ref, odd_ref, order_ref):
    order_ref[...] = jnp.zeros(order_ref.shape, f32)
    k2_ref[...] = jnp.zeros(k2_ref.shape, bf16)
    slots = {-1: 5, 0: 0, 1: 1, 2: 2, 3: 3, 4: 6}
    blank = jnp.zeros((64, 64), f32)
    for c in range(3):
        taps = [packed_ref[64 * (3 * d + c) : 64 * (3 * d + c) + 64, :].astype(f32) for d in range(3)]
        two = [(taps[0], blank), (taps[1], taps[0]), (taps[2], taps[1]), (blank, taps[2])]
        two = [jnp.concatenate(pair, axis=0).T.astype(bf16) for pair in two]
        for h in range(2):
            for d in range(4):
                slot = slots[d + 2 * h - 1]
                k2_ref[64 * slot : 64 * slot + 64, 256 * c + 128 * h : 256 * c + 128 * h + 128] = two[d]

    taps = [
        [packed_ref[576 + 16 * (3 * d + c) : 592 + 16 * (3 * d + c), :].astype(f32) for d in range(3)]
        for c in range(3)
    ]
    blank = jnp.zeros((16, 64), f32)
    filler = jnp.zeros((64, 256), bf16)
    parts = [filler] * 8
    for k, slot in slots.items():
        pieces = [taps[c][k - t + 1] if 0 <= k - t + 1 < 3 else blank for c in range(3) for t in range(4)]
        pieces += [blank] * 4
        parts[slot] = jnp.concatenate(pieces, axis=0).T.astype(bf16)
    raw = jnp.concatenate(parts, axis=0)
    source = lax.broadcasted_iota(jnp.int32, (256, 256), 0)
    target = lax.broadcasted_iota(jnp.int32, (256, 256), 1)
    inner = target % 64
    place = inner // 4
    channel = 8 * (place // 8) + 4 * (place % 2) + (place // 2) % 4
    lane = 16 * (inner % 4) + channel
    part = target // 64
    column_even = jnp.where(part == 3, -1, 64 * part + lane)
    column_odd = jnp.where(
        part == 2, -1, jnp.where(part == 3, 128 + lane, jnp.where(part == 0, 64 + lane, lane))
    )
    even_ref[...] = dot(raw, jnp.where(source == column_even, 1.0, 0.0).astype(bf16)).astype(bf16)
    odd_ref[...] = dot(raw, jnp.where(source == column_odd, 1.0, 0.0).astype(bf16)).astype(bf16)


def fill(field, both_ref, beside_ref, height, breadth):
    for q in range(2):
        field[q, 8 : 8 + height, :breadth] = both_ref[height * q : height * (q + 1), :]
        field[q, 8 : 8 + height, breadth:] = beside_ref[height * q : height * (q + 1), :]


def patches_of(field, rows, depth):
    lanes = field.shape[2]
    whole = jnp.concatenate([field[0, 8 : 8 + rows], field[1, 8 : 8 + rows]], axis=0)
    pieces = [pltpu.roll(whole, 1, 1), whole, pltpu.roll(whole, lanes - 1, 1)]
    pieces.append(jnp.zeros((depth - 6 * rows, lanes), f32))
    turned = jnp.concatenate(pieces, axis=0).T
    return jnp.concatenate([turned[: lanes - 120], turned[lanes - 8 :]], axis=0).astype(bf16)


def layer_1(patches, weights_ref, bias_ref, r):
    return jnp.maximum(dot(patches, weights_ref[r]) + bias_ref[...], 0.0).astype(bf16)


def with_neighbours(before, own, after, weights_ref):
    beside = jnp.concatenate([before[:, 128:], after[:, :128]], axis=1)
    return dot(own[...], weights_ref[:256]) + dot(beside, weights_ref[256:])


def layer_2(before, own, after, weights_ref, bias_ref):
    total = with_neighbours(before, own, after, weights_ref)
    span = total.shape[0]
    total = pltpu.roll(total[:, :256], 1, 0) + total[:, 256:512] + pltpu.roll(total[:, 512:], span - 1, 0)
    return jnp.maximum(total + bias_ref[...], 0.0).astype(bf16)


def layer_3(second, groups, r, weights_ref):
    total = with_neighbours(second((r - 1) % groups), second(r), second((r + 1) % groups), weights_ref)
    left_part = total[:, :128]
    return (
        pltpu.roll(left_part, 1, 0)
        + pltpu.roll(left_part, 64, 1)
        + pltpu.roll(total[:, 128:], total.shape[0] - 1, 0)
    )


def coefficients(second, groups, even, odd, even_ref, odd_ref):
    block = layer_3(second, groups, even, even_ref)
    if odd is not None:
        lower = lax.broadcasted_iota(jnp.int32, block.shape, 1) < 64
        block = jnp.where(lower, block, layer_3(second, groups, odd, odd_ref))
    span = block.shape[0]
    filler = jnp.zeros((112, 128), f32)
    return jnp.concatenate([block[: span - 8], filler, block[span - 8 :]], axis=0).T


def inner_kernel(
    both_ref, beside_ref, w1_ref, w2_ref, even_ref, odd_ref, b1_ref, b2_ref, first_ref, second_ref, coeff_ref, field
):
    height, breadth = both_ref.shape[0] // 2, both_ref.shape[1]
    rows = height + 8
    groups = rows // 4
    field[...] = jnp.zeros_like(field)
    fill(field, both_ref, beside_ref, height, breadth)
    patches = patches_of(field, rows, w1_ref.shape[1])
    for r in range(1, groups - 3):
        first_ref[r - 1] = layer_1(patches, w1_ref, b1_ref, r)
        if r >= 3:
            second_ref[r - 3] = layer_2(
                first_ref.at[r - 3], first_ref.at[r - 2], first_ref.at[r - 1], w2_ref, b2_ref
            )
    block = coefficients(lambda r: second_ref.at[r - 2], groups, 3, 4, even_ref, odd_ref)
    coeff_ref[0] = block[:64]
    coeff_ref[1] = block[64:]


def advance_kernel(
    both_ref, beside_ref, bot_ref, top_ref, w1_ref, w2_ref, even_ref, odd_ref, b1_ref, b2_ref, b3_ref,
    first_ref, second_ref, coeff_ref, star_ref, field, outer_first, outer_second, outer_coeff,
):
    height, breadth = both_ref.shape[0] // 2, both_ref.shape[1]
    rows = height + 8
    groups = rows // 4
    lanes = breadth + 128
    fill(field, both_ref, beside_ref, height, breadth)
    for q in range(2):
        field[q, 8 + height : 12 + height, :] = bot_ref[4 * q : 4 * q + 4, :]
        field[q, 12 + height : 16 + height, :] = top_ref[4 * q : 4 * q + 4, :]
        field[q, 0:8, :] = field[q, rows : rows + 8, :]
        field[q, 8 + rows : 16 + rows, :] = field[q, 8:16, :]
    patches = patches_of(field, rows, w1_ref.shape[1])

    ends = (groups - 3, groups - 2, groups - 1, 0, 1, groups - 4)

    def first(r):
        return outer_first.at[ends.index(r)] if r in ends[:4] else first_ref.at[r - 1]

    def second(r):
        return outer_second.at[ends.index(r)] if r in ends else second_ref.at[r - 2]

    held = {3: coeff_ref.at[0], 4: coeff_ref.at[1]}

    def do_first(r):
        outer_first[ends.index(r)] = layer_1(patches, w1_ref, b1_ref, r)

    def do_second(r):
        outer_second[ends.index(r)] = layer_2(
            first((r - 1) % groups), first(r), first((r + 1) % groups), w2_ref, b2_ref
        )

    def do_coefficients(even, odd):
        block = coefficients(second, groups, even, odd, even_ref, odd_ref)
        for r, part in ((even, block[:64]), (odd, block[64:])):
            if r is not None:
                place = len(held)
                outer_coeff[place - 2] = part
                held[r] = outer_coeff.at[place - 2]

    offsets = b3_ref[...]
    sub = lax.broadcasted_iota(jnp.int32, (8, breadth), 0) % 4

    def stacked(r, shift, qs=(0, 1)):
        start = 8 + 4 * r + shift
        return jnp.concatenate([field[q, start : start + 4, :] for q in qs], axis=0)

    def flows(r, previous):
        weights = held[r][...] + offsets
        weights = [weights[8 * i : 8 * i + 8] for i in range(8)]
        centre = stacked(r, 0)

        def stencil(d):
            four = weights[4 * d : 4 * d + 4]
            mean = (four[0] + four[1] + four[2] + four[3]) * 0.25
            return [base + w - mean for base, w in zip(stencil_base, four)]

        east = stencil(0)
        flow_x = (
            east[0] * stacked(r, -1) + east[1] * centre + east[2] * stacked(r, 1) + east[3] * stacked(r, 2)
        )
        flow_x = flow_x * (0.5 * (stacked(r, 0, (0, 0)) + stacked(r, 1, (0, 0))))
        flow_x = flow_x[:, :breadth]
        if previous is not None:
            north = stencil(1)
            flow_y = (
                north[0] * pltpu.roll(centre, 1, 1)
                + north[1] * centre
                + north[2] * pltpu.roll(centre, lanes - 1, 1)
                + north[3] * pltpu.roll(centre, lanes - 2, 1)
            )
            carrier = stacked(r, 0, (1, 1))
            flow_y = flow_y * (0.5 * (carrier + pltpu.roll(carrier, lanes - 1, 1)))
            change_y = (flow_y - pltpu.roll(flow_y, 1, 1))[:, :breadth]
            above = jnp.where(sub == 0, pltpu.roll(previous, 5, 0), pltpu.roll(flow_x, 1, 0))
            star = centre[:, :breadth] - step_ratio * (flow_x - above + change_y)
            star_ref[4 * r : 4 * r + 4, :] = star[:4]
            star_ref[height + 4 * r : height + 4 * r + 4, :] = star[4:]
        return flow_x

    for r in ends[:4]:
        do_first(r)
    for r in ends[1:5]:
        do_second(r)
    do_coefficients(groups - 1, None)
    do_coefficients(0, 1)
    do_second(groups - 4)
    previous = flows(groups - 1, None)
    previous = flows(0, previous)
    previous = flows(1, previous)
    inner = list(range(5, groups - 4))
    do_coefficients(2, inner[0])
    do_second(groups - 3)
    for r in range(2, 5):
        previous = flows(r, previous)
    do_coefficients(groups - 4, groups - 3)
    for r in range(5, groups - 2):
        previous = flows(r, previous)


def own_twiddle(ref):
    own = ref[lax.axis_index("gy")]
    half = own.shape[0] // 2
    return own[:half], own[half:]


def column_kernel(*refs):
    *blocks, twiddle_ref, high_ref, low_ref, out_ref = refs
    rows, breadth = out_ref.shape
    cosine, sine = own_twiddle(twiddle_ref)
    sign = parity((rows, breadth))
    mixed = None
    for k, ref in enumerate(blocks):
        block = ref[...] * sign
        term = block * cosine[k : k + 1, :] + swap(block) * (sign * sine[k : k + 1, :])
        mixed = term if mixed is None else mixed + term
    spectra = product_3(mixed, high_ref[...], low_ref[...])
    out_ref[...] = spectra[:, :breadth] + sign * swap(spectra[:, breadth:])


def factors_kernel(out_ref, *, scale):
    _, length, breadth = out_ref.shape
    index = lax.broadcasted_iota(jnp.int32, (length, breadth), 0)
    wave_x = jnp.where(index >= length // 2, index - length, index).astype(f32) * (2.0 * math.pi / length)
    members_y = lax.axis_size("gy")
    grid_y = members_y * breadth
    number_y = lax.axis_index("gy") + members_y * lax.broadcasted_iota(jnp.int32, (1, breadth), 1)
    wave_y = jnp.where(number_y >= grid_y // 2, number_y - grid_y, number_y).astype(f32) * (2.0 * math.pi / grid_y)
    edge_y = number_y == grid_y // 2
    edge_x = index == length // 2
    total = wave_x * wave_x + wave_y * wave_y
    zero = total == 0.0
    inverse = scale / jnp.where(zero, 1.0, total)
    same = (0.5 * inverse) * (wave_y * wave_y - wave_x * wave_x)
    cross = jnp.where(edge_x != edge_y, 0.0, -inverse * wave_x * wave_y)
    out_ref[0] = jnp.where(zero, 0.5 * scale, same)
    out_ref[1] = jnp.where(zero, -0.5 * scale, same)
    out_ref[2] = cross


def row_kernel(*refs):
    *blocks, factors_ref, table_ref, table_low_ref, high_ref, low_ref, out_ref, gathered = refs
    rows, breadth = out_ref.shape
    height = rows // 2
    length = len(blocks) * height
    own_index = lax.axis_index("gx")
    for k, ref in enumerate(blocks):
        start = pl.multiple_of((own_index ^ k) * height, height)
        gathered[pl.ds(start, height), :breadth] = ref[:height, :]
        gathered[pl.ds(start, height), breadth:] = ref[height:, :]
    data = gathered[...]
    data, data_low = split(data)
    spectra = dot(table_ref[...], data) + dot(table_ref[...], data_low) + dot(table_low_ref[...], data)
    real_part = spectra[:length, :breadth] + spectra[length:, breadth:]
    imag_part = spectra[:length, breadth:] - spectra[length:, :breadth]
    same_real, same_imag, cross = factors_ref[0], factors_ref[1], factors_ref[2]
    kept_real = same_real * real_part - cross * imag_part
    kept_imag = same_imag * imag_part + cross * real_part
    kept, kept_low = split(jnp.concatenate([kept_real, kept_imag], axis=1))
    start = pl.multiple_of(own_index * height, height)

    def own(ref):
        parts = [ref[pl.ds(start, height), :], ref[pl.ds(pl.multiple_of(length + start, height), height), :]]
        return jnp.concatenate(parts, axis=0)

    table, table_low = own(table_ref), own(table_low_ref)
    home = dot(table, kept) + dot(table, kept_low) + dot(table_low, kept)
    home = jnp.concatenate(
        [
            home[:height, :breadth] - home[height:, breadth:],
            home[:height, breadth:] + home[height:, :breadth],
        ],
        axis=0,
    )
    columns = product_3(home, high_ref[...], low_ref[...])
    out_ref[...] = columns[:, :breadth] - parity((rows, breadth)) * swap(columns[:, breadth:])


def home_kernel(*refs):
    *blocks, twiddle_ref, star_ref, u_ref, v_ref = refs
    rows, breadth = star_ref.shape
    cosine, sine = own_twiddle(twiddle_ref)
    sign = parity((rows, breadth))
    result = 0.5 * star_ref[...]
    for k, ref in enumerate(blocks):
        block = ref[...]
        result = result + block * cosine[k : k + 1, :] - swap(block) * (sign * sine[k : k + 1, :])
    u_ref[...] = result[: rows // 2]
    v_ref[...] = result[rows // 2 :]


def call(kernel, shapes, scratch=(), flops=10**7):
    return pl.pallas_call(
        kernel,
        out_shape=shapes,
        scratch_shapes=list(scratch),
        compiler_params=pltpu.CompilerParams(vmem_limit_bytes=vmem_limit),
        cost_estimate=pl.CostEstimate(flops=flops, bytes_accessed=2**20, transcendentals=0),
    )


@functools.lru_cache(None)
def tables(height, breadth, members_x, members_y):
    turn = 2.0 * math.pi
    j = np.arange(breadth)
    phase = turn * (np.outer(j, j) % breadth) / breadth
    column = split_table(np.concatenate([np.cos(phase), np.sin(phase)], axis=1))
    length = height * members_x
    k = np.arange(length)
    phase = turn * (np.outer(k, k) % length) / length
    row = split_table(np.concatenate([np.cos(phase), np.sin(phase)], axis=0))
    g = np.arange(members_y)[:, None, None]
    partner = g ^ np.arange(members_y)[None, :, None]
    whole = breadth * members_y
    out = turn * ((partner * breadth + j) * g % whole) / whole
    home = turn * ((g * breadth + j) * partner % whole) / whole
    twiddle_out, twiddle_home = [
        np.concatenate([np.cos(phase), np.sin(phase)], axis=1).astype(np.float32) for phase in (out, home)
    ]
    return column, row, twiddle_out, twiddle_home


def partner(block, axis, k):
    return lax.ppermute(block, axis, [(i, i ^ k) for i in range(lax.axis_size(axis))])


def gather_y(block):
    return [block] + [partner(block, "gy", k) for k in range(1, lax.axis_size("gy"))]


def gather_x(block):
    own = [block] + [partner(block, "gx", k) for k in range(2, lax.axis_size("gx"), 2)]
    return [other for held in own for other in (held, partner(held, "gx", 1))]


def on_device(u_field, v_field, w_first, b_first, w_second, b_second, w_third, b_third):
    height, breadth = u_field.shape
    members_x, members_y = lax.axis_size("gx"), lax.axis_size("gy")
    grid_x, grid_y = height * members_x, breadth * members_y
    rows = height + 8
    groups = rows // 4
    span = breadth + 16
    shape = jax.ShapeDtypeStruct

    def shifted(value, axis, distance):
        peers = lax.axis_size(axis)
        return lax.ppermute(value, axis, [(i, (i + distance) % peers) for i in range(peers)])

    with jax.named_scope("columns_around"):
        both = jnp.stack([u_field, v_field]).reshape(2 * height, breadth)
        edge = shape((8, 128), f32)
        last, first = call(columns_kernel, (edge, edge), (pltpu.VMEM((128, 128), f32),))(both)
        left, right = shifted(last, "gy", 1), shifted(first, "gy", -1)

    with jax.named_scope("weights"):
        taps = w_first.transpose(0, 2, 1).astype(f32)
        biases = jnp.concatenate([b_first, b_second, b_third])[None]
        kernel_1, *biases = call(
            functools.partial(first_weights_kernel, rows=rows),
            (
                shape((groups, -(-6 * rows // 128) * 128, 256), bf16),
                shape((1, 256), f32),
                shape((1, 256), f32),
                shape((64, 1), f32),
            ),
        )(taps, biases)
        packed = jnp.concatenate([w_second.reshape(576, 64), w_third.reshape(144, 64)], axis=0)
        *others, order = call(
            other_weights_kernel,
            (shape((512, 768), bf16), shape((512, 256), bf16), shape((512, 256), bf16), shape((8, 128), f32)),
        )(packed)

    with jax.named_scope("rows_around"):
        edge = shape((8, breadth + 128), f32)
        last, first, beside = call(
            rows_kernel, (edge, edge, shape((2 * height, 128), f32)), (pltpu.VMEM((128, 128), f32),)
        )(both, right, left, biases[2], order)
        top, bottom = shifted(last, "gx", 1), shifted(first, "gx", -1)

    block = shape((2 * height, breadth), f32)
    padded = pltpu.VMEM((2, rows + 16, breadth + 128), f32)
    with jax.named_scope("advance"):
        inner = call(
            inner_kernel,
            (
                shape((groups - 4, span, 256), bf16),
                shape((groups - 6, span, 256), bf16),
                shape((2, 64, breadth + 128), f32),
            ),
            (padded,),
            flops=5 * 10**8,
        )(both, beside, kernel_1, *others, *biases[:2])
        star = call(
            advance_kernel,
            block,
            (
                padded,
                pltpu.VMEM((4, span, 256), bf16),
                pltpu.VMEM((6, span, 256), bf16),
                pltpu.VMEM((groups - 3, 64, breadth + 128), f32),
            ),
            flops=10**9,
        )(both, beside, bottom, top, kernel_1, *others, *biases, *inner)

    column, row, twiddle_out, twiddle_home = tables(height, breadth, members_x, members_y)
    column, row = [[jnp.asarray(t) for t in pair] for pair in (column, row)]
    spectra = call(column_kernel, block)(*gather_y(star), jnp.asarray(twiddle_out), *column)
    factors = call(
        functools.partial(factors_kernel, scale=1.0 / (grid_x * grid_y)), shape((3, grid_x, breadth), f32)
    )()
    columns = call(row_kernel, block, (pltpu.VMEM((grid_x, 2 * breadth), f32),))(
        *gather_x(spectra), factors, *row, *column
    )
    part = shape((height, breadth), f32)
    return tuple(call(home_kernel, (part, part))(*gather_y(columns), jnp.asarray(twiddle_home), star))


def solution(mesh):
    return jax.shard_map(
        on_device,
        mesh=mesh,
        in_specs=(P("gx", "gy"), P("gx", "gy"), P(), P(), P(), P(), P(), P()),
        out_specs=(P("gx", "gy"), P("gx", "gy")),
        check_vma=False,
    )
```

```python
import functools
import math

import jax
import jax.numpy as jnp
import ml_dtypes
import numpy as np
from jax import lax
from jax.experimental import pallas as pl
from jax.experimental.pallas import tpu as pltpu
from jax.sharding import PartitionSpec as P

step_ratio = 0.4
stencil_base = (-0.0625, 0.5625, 0.5625, -0.0625)
f32 = jnp.float32
bf16 = jnp.bfloat16

vmem_limit = 48 * 1024 * 1024


def split(value):
    high = value.astype(bf16)
    return high, (value - high.astype(f32)).astype(bf16)


def split_table(table):
    high = table.astype(ml_dtypes.bfloat16)
    low = (table - high.astype(np.float64)).astype(ml_dtypes.bfloat16)
    return high, low


def dot(a, b):
    return jnp.dot(a, b, preferred_element_type=f32)


def product_3(value, high, low):
    rows = value.shape[0]
    first, second = split(value)
    both = dot(jnp.concatenate([first, second], axis=0), high)
    return both[:rows] + both[rows:] + dot(first, low)


def parity(shape):
    rows = lax.broadcasted_iota(jnp.int32, shape, 0)
    return jnp.where(rows < shape[0] // 2, 1.0, -1.0).astype(f32)


def swap(value):
    half = value.shape[0] // 2
    return jnp.concatenate([value[half:], value[:half]], axis=0)


def columns_kernel(both_ref, last_ref, first_ref, strip):
    cells, breadth = both_ref.shape
    strip[cells:, :] = jnp.zeros((128 - cells, 128), f32)
    for side, out in ((0, first_ref), (breadth - 128, last_ref)):
        strip[:cells, :] = both_ref[:, side : side + 128]
        turned = strip[...].T
        out[...] = turned[0:8] if side == 0 else turned[120:128]


def rows_kernel(both_ref, right_ref, left_ref, order_ref, order_too_ref, last_ref, first_ref, beside_ref, strip):
    height, breadth = both_ref.shape[0] // 2, both_ref.shape[1]
    strip[...] = jnp.zeros_like(strip)
    strip[0:4, :] = right_ref[0:4, :]
    strip[124:128, :] = left_ref[4:8, :]
    beside_ref[...] = strip[...].T[: 2 * height]
    for q in range(2):
        start, end, own = height * q, height * (q + 1), slice(4 * q, 4 * q + 4)
        last_ref[own, :breadth] = both_ref[end - 4 : end, :]
        last_ref[own, breadth:] = beside_ref[end - 4 : end, :]
        first_ref[own, :breadth] = both_ref[start : start + 4, :]
        first_ref[own, breadth:] = beside_ref[start : start + 4, :]


def first_weights_kernel(taps_ref, biases_ref, k1_ref, c1_ref, c2_ref, c3_ref, *, rows):
    groups, depth, _ = k1_ref.shape
    wide = [jnp.concatenate([taps_ref[i]] * 4, axis=1) for i in range(9)]
    c1_ref[...] = jnp.concatenate([biases_ref[:, :64]] * 4, axis=1)
    c2_ref[...] = jnp.concatenate([biases_ref[:, 64:128]] * 4, axis=1)
    place = lax.broadcasted_iota(jnp.int32, (64, 16), 0) // 4
    channel = 8 * (place // 8) + 4 * (place % 2) + (place // 2) % 4
    hit = channel == lax.broadcasted_iota(jnp.int32, (64, 16), 1)
    c3_ref[...] = jnp.sum(jnp.where(hit, biases_ref[:, 128:144], 0.0), axis=1, keepdims=True)
    spread = []
    for d in range(3):
        parts = [
            jnp.broadcast_to(wide[3 * d + s][q : q + 1, :], (rows, 256))
            for s in range(3)
            for q in range(2)
        ]
        parts.append(jnp.zeros((depth - 6 * rows, 256), f32))
        spread.append(jnp.concatenate(parts, axis=0))
    row = lax.broadcasted_iota(jnp.int32, (rows, 256), 0) - lax.broadcasted_iota(jnp.int32, (rows, 256), 1) // 64
    row = jnp.where(row < 0, row + rows, row)
    row = jnp.concatenate([row] * 6 + [jnp.full((depth - 6 * rows, 256), -1, jnp.int32)], axis=0)
    for r in range(groups):
        near = [row == (4 * r + d - 1) % rows for d in range(3)]
        block = jnp.where(near[0], spread[0], jnp.where(near[1], spread[1], jnp.where(near[2], spread[2], 0.0)))
        k1_ref[r] = block.astype(bf16)


def other_weights_kernel(packed_ref, k2_ref, even_ref, odd_ref, order_ref):
    order_ref[...] = jnp.zeros(order_ref.shape, f32)
    slots = {-1: 5, 0: 0, 1: 1, 2: 2, 3: 3, 4: 6}
    blank = jnp.zeros((64, 64), f32)
    for c in range(3):
        taps = [packed_ref[64 * (3 * d + c) : 64 * (3 * d + c) + 64, :].astype(f32) for d in range(3)]
        two = [(taps[0], blank), (taps[1], taps[0]), (taps[2], taps[1]), (blank, taps[2])]
        two = [jnp.concatenate(pair, axis=0).T.astype(bf16) for pair in two]
        for slot, source in enumerate((1, 2, 3, 0)):
            k2_ref[64 * slot : 64 * slot + 64, 128 * c : 128 * c + 128] = two[source]

    taps = [
        [packed_ref[576 + 16 * (3 * d + c) : 592 + 16 * (3 * d + c), :].astype(f32) for d in range(3)]
        for c in range(3)
    ]
    blank = jnp.zeros((16, 64), f32)
    filler = jnp.zeros((64, 256), bf16)
    parts = [filler] * 8
    for k, slot in slots.items():
        pieces = [taps[c][k - t + 1] if 0 <= k - t + 1 < 3 else blank for c in range(3) for t in range(4)]
        pieces += [blank] * 4
        parts[slot] = jnp.concatenate(pieces, axis=0).T.astype(bf16)
    raw = jnp.concatenate(parts, axis=0)
    source = lax.broadcasted_iota(jnp.int32, (256, 256), 0)
    target = lax.broadcasted_iota(jnp.int32, (256, 256), 1)
    inner = target % 64
    place = inner // 4
    channel = 8 * (place // 8) + 4 * (place % 2) + (place // 2) % 4
    lane = 16 * (inner % 4) + channel
    part = target // 64
    column_even = jnp.where(part == 3, -1, 64 * part + lane)
    column_odd = jnp.where(
        part == 2, -1, jnp.where(part == 3, 128 + lane, jnp.where(part == 0, 64 + lane, lane))
    )
    even_ref[...] = dot(raw, jnp.where(source == column_even, 1.0, 0.0).astype(bf16)).astype(bf16)
    odd_ref[...] = dot(raw, jnp.where(source == column_odd, 1.0, 0.0).astype(bf16)).astype(bf16)


def fill(field, both_ref, beside_ref, height, breadth):
    for q in range(2):
        field[q, 8 : 8 + height, :breadth] = both_ref[height * q : height * (q + 1), :]
        field[q, 8 : 8 + height, breadth:] = beside_ref[height * q : height * (q + 1), :]


def patches_of(field, rows, depth):
    lanes = field.shape[2]
    whole = jnp.concatenate([field[0, 8 : 8 + rows], field[1, 8 : 8 + rows]], axis=0)
    pieces = [pltpu.roll(whole, 1, 1), whole, pltpu.roll(whole, lanes - 1, 1)]
    pieces.append(jnp.zeros((depth - 6 * rows, lanes), f32))
    turned = jnp.concatenate(pieces, axis=0).T
    return jnp.concatenate([turned[: lanes - 120], turned[lanes - 8 :]], axis=0).astype(bf16)


def layer_1(patches, weights_ref, bias_ref, r):
    return jnp.maximum(dot(patches, weights_ref[r]) + bias_ref[...], 0.0).astype(bf16)


def with_neighbours(before, own, after, weights_ref):
    beside = jnp.concatenate([before[:, 128:], after[:, :128]], axis=1)
    return dot(own[...], weights_ref[:256]) + dot(beside, weights_ref[256:])


def layer_2(before, own, after, weights_ref, bias_ref):
    span = own.shape[0]
    lower = lax.broadcasted_iota(jnp.int32, (span, 128), 1) < 64
    left, right = own[:, :128], own[:, 128:]
    results = []
    for pair, below, above in ((left, right, before[:, 128:]), (right, after[:, :128], left)):
        total = dot(jnp.concatenate([pair, jnp.where(lower, below, above)], axis=1), weights_ref[...])
        total = pltpu.roll(total[:, :128], 1, 0) + total[:, 128:256] + pltpu.roll(total[:, 256:], span - 1, 0)
        results.append(jnp.maximum(total + bias_ref[:, :128], 0.0).astype(bf16))
    return jnp.concatenate(results, axis=1)


def layer_3(second, groups, r, weights_ref):
    total = with_neighbours(second((r - 1) % groups), second(r), second((r + 1) % groups), weights_ref)
    left_part = total[:, :128]
    return (
        pltpu.roll(left_part, 1, 0)
        + pltpu.roll(left_part, 64, 1)
        + pltpu.roll(total[:, 128:], total.shape[0] - 1, 0)
    )


def coefficients(second, groups, even, odd, even_ref, odd_ref):
    block = layer_3(second, groups, even, even_ref)
    if odd is not None:
        lower = lax.broadcasted_iota(jnp.int32, block.shape, 1) < 64
        block = jnp.where(lower, block, layer_3(second, groups, odd, odd_ref))
    span = block.shape[0]
    filler = jnp.zeros((112, 128), f32)
    return jnp.concatenate([block[: span - 8], filler, block[span - 8 :]], axis=0).T


def inner_kernel(
    both_ref, beside_ref, w1_ref, w2_ref, even_ref, odd_ref, b1_ref, b2_ref, first_ref, second_ref, coeff_ref, field
):
    height, breadth = both_ref.shape[0] // 2, both_ref.shape[1]
    rows = height + 8
    groups = rows // 4
    field[...] = jnp.zeros_like(field)
    fill(field, both_ref, beside_ref, height, breadth)
    patches = patches_of(field, rows, w1_ref.shape[1])
    for r in range(1, groups - 3):
        first_ref[r - 1] = layer_1(patches, w1_ref, b1_ref, r)
        if r >= 3:
            second_ref[r - 3] = layer_2(
                first_ref.at[r - 3], first_ref.at[r - 2], first_ref.at[r - 1], w2_ref, b2_ref
            )
    block = coefficients(lambda r: second_ref.at[r - 2], groups, 3, 4, even_ref, odd_ref)
    coeff_ref[0] = block[:64]
    coeff_ref[1] = block[64:]


def advance_kernel(
    both_ref, beside_ref, bot_ref, top_ref, w1_ref, w2_ref, even_ref, odd_ref, b1_ref, b2_ref, b3_ref,
    first_ref, second_ref, coeff_ref, star_ref, field, outer_first, outer_second, outer_coeff,
):
    height, breadth = both_ref.shape[0] // 2, both_ref.shape[1]
    rows = height + 8
    groups = rows // 4
    lanes = breadth + 128
    fill(field, both_ref, beside_ref, height, breadth)
    for q in range(2):
        field[q, 8 + height : 12 + height, :] = bot_ref[4 * q : 4 * q + 4, :]
        field[q, 12 + height : 16 + height, :] = top_ref[4 * q : 4 * q + 4, :]
        field[q, 0:8, :] = field[q, rows : rows + 8, :]
        field[q, 8 + rows : 16 + rows, :] = field[q, 8:16, :]
    patches = patches_of(field, rows, w1_ref.shape[1])

    ends = (groups - 3, groups - 2, groups - 1, 0, 1, groups - 4)

    def first(r):
        return outer_first.at[ends.index(r)] if r in ends[:4] else first_ref.at[r - 1]

    def second(r):
        return outer_second.at[ends.index(r)] if r in ends else second_ref.at[r - 2]

    held = {3: coeff_ref.at[0], 4: coeff_ref.at[1]}

    def do_first(r):
        outer_first[ends.index(r)] = layer_1(patches, w1_ref, b1_ref, r)

    def do_second(r):
        outer_second[ends.index(r)] = layer_2(
            first((r - 1) % groups), first(r), first((r + 1) % groups), w2_ref, b2_ref
        )

    def do_coefficients(even, odd):
        block = coefficients(second, groups, even, odd, even_ref, odd_ref)
        for r, part in ((even, block[:64]), (odd, block[64:])):
            if r is not None:
                place = len(held)
                outer_coeff[place - 2] = part
                held[r] = outer_coeff.at[place - 2]

    offsets = b3_ref[...]
    sub = lax.broadcasted_iota(jnp.int32, (8, breadth), 0) % 4

    def stacked(r, shift, qs=(0, 1)):
        start = 8 + 4 * r + shift
        return jnp.concatenate([field[q, start : start + 4, :] for q in qs], axis=0)

    def flows(r, previous):
        weights = held[r][...] + offsets
        weights = [weights[8 * i : 8 * i + 8] for i in range(8)]
        centre = stacked(r, 0)

        def stencil(d):
            four = weights[4 * d : 4 * d + 4]
            mean = (four[0] + four[1] + four[2] + four[3]) * 0.25
            return [base + w - mean for base, w in zip(stencil_base, four)]

        east = stencil(0)
        flow_x = (
            east[0] * stacked(r, -1) + east[1] * centre + east[2] * stacked(r, 1) + east[3] * stacked(r, 2)
        )
        flow_x = flow_x * (0.5 * (stacked(r, 0, (0, 0)) + stacked(r, 1, (0, 0))))
        flow_x = flow_x[:, :breadth]
        if previous is not None:
            north = stencil(1)
            flow_y = (
                north[0] * pltpu.roll(centre, 1, 1)
                + north[1] * centre
                + north[2] * pltpu.roll(centre, lanes - 1, 1)
                + north[3] * pltpu.roll(centre, lanes - 2, 1)
            )
            carrier = stacked(r, 0, (1, 1))
            flow_y = flow_y * (0.5 * (carrier + pltpu.roll(carrier, lanes - 1, 1)))
            change_y = (flow_y - pltpu.roll(flow_y, 1, 1))[:, :breadth]
            above = jnp.where(sub == 0, pltpu.roll(previous, 5, 0), pltpu.roll(flow_x, 1, 0))
            star = centre[:, :breadth] - step_ratio * (flow_x - above + change_y)
            star_ref[4 * r : 4 * r + 4, :] = star[:4]
            star_ref[height + 4 * r : height + 4 * r + 4, :] = star[4:]
        return flow_x

    for r in ends[:4]:
        do_first(r)
    for r in ends[1:5]:
        do_second(r)
    do_coefficients(groups - 1, None)
    do_coefficients(0, 1)
    do_second(groups - 4)
    previous = flows(groups - 1, None)
    previous = flows(0, previous)
    previous = flows(1, previous)
    inner = list(range(5, groups - 4))
    do_coefficients(2, inner[0])
    do_second(groups - 3)
    for r in range(2, 5):
        previous = flows(r, previous)
    do_coefficients(groups - 4, groups - 3)
    for r in range(5, groups - 2):
        previous = flows(r, previous)


def own_twiddle(ref):
    own = ref[lax.axis_index("gy")]
    half = own.shape[0] // 2
    return own[:half], own[half:]


def column_kernel(*refs):
    *blocks, twiddle_ref, high_ref, low_ref, out_ref = refs
    rows, breadth = out_ref.shape
    cosine, sine = own_twiddle(twiddle_ref)
    sign = parity((rows, breadth))
    mixed = None
    for k, ref in enumerate(blocks):
        block = ref[...] * sign
        term = block * cosine[k : k + 1, :] + swap(block) * (sign * sine[k : k + 1, :])
        mixed = term if mixed is None else mixed + term
    spectra = product_3(mixed, high_ref[...], low_ref[...])
    out_ref[...] = spectra[:, :breadth] + sign * swap(spectra[:, breadth:])


def factors_kernel(out_ref, *, scale):
    _, length, breadth = out_ref.shape
    index = lax.broadcasted_iota(jnp.int32, (length, breadth), 0)
    wave_x = jnp.where(index >= length // 2, index - length, index).astype(f32) * (2.0 * math.pi / length)
    members_y = lax.axis_size("gy")
    grid_y = members_y * breadth
    number_y = lax.axis_index("gy") + members_y * lax.broadcasted_iota(jnp.int32, (1, breadth), 1)
    wave_y = jnp.where(number_y >= grid_y // 2, number_y - grid_y, number_y).astype(f32) * (2.0 * math.pi / grid_y)
    edge_y = number_y == grid_y // 2
    edge_x = index == length // 2
    total = wave_x * wave_x + wave_y * wave_y
    zero = total == 0.0
    inverse = scale / jnp.where(zero, 1.0, total)
    same = (0.5 * inverse) * (wave_y * wave_y - wave_x * wave_x)
    cross = jnp.where(edge_x != edge_y, 0.0, -inverse * wave_x * wave_y)
    out_ref[0] = jnp.where(zero, 0.5 * scale, same)
    out_ref[1] = jnp.where(zero, -0.5 * scale, same)
    out_ref[2] = cross


def row_kernel(*refs):
    *blocks, factors_ref, table_ref, high_ref, low_ref, out_ref, gathered = refs
    rows, breadth = out_ref.shape
    height = rows // 2
    length = len(blocks) * height
    own_index = lax.axis_index("gx")
    for k, ref in enumerate(blocks):
        start = pl.multiple_of((own_index ^ k) * height, height)
        gathered[pl.ds(start, height), :breadth] = ref[:height, :]
        gathered[pl.ds(start, height), breadth:] = ref[height:, :]
    data = gathered[...]
    data, data_low = split(data)
    both = dot(table_ref[...], data)
    spectra = both[: 2 * length] + both[2 * length :] + dot(table_ref[: 2 * length], data_low)
    real_part = spectra[:length, :breadth] + spectra[length:, breadth:]
    imag_part = spectra[:length, breadth:] - spectra[length:, :breadth]
    same_real, same_imag, cross = factors_ref[0], factors_ref[1], factors_ref[2]
    kept_real = same_real * real_part - cross * imag_part
    kept_imag = same_imag * imag_part + cross * real_part
    kept, kept_low = split(jnp.concatenate([kept_real, kept_imag], axis=1))
    start = pl.multiple_of(own_index * height, height)

    table = jnp.concatenate(
        [table_ref[pl.ds(pl.multiple_of(part * length + start, height), height), :] for part in range(4)], axis=0
    )
    both = dot(table, kept)
    home = both[: 2 * height] + both[2 * height :] + dot(table[: 2 * height], kept_low)
    home = jnp.concatenate(
        [
            home[:height, :breadth] - home[height:, breadth:],
            home[:height, breadth:] + home[height:, :breadth],
        ],
        axis=0,
    )
    columns = product_3(home, high_ref[...], low_ref[...])
    out_ref[...] = columns[:, :breadth] - parity((rows, breadth)) * swap(columns[:, breadth:])


def home_kernel(*refs):
    *blocks, twiddle_ref, star_ref, u_ref, v_ref = refs
    rows, breadth = star_ref.shape
    cosine, sine = own_twiddle(twiddle_ref)
    sign = parity((rows, breadth))
    result = 0.5 * star_ref[...]
    for k, ref in enumerate(blocks):
        block = ref[...]
        result = result + block * cosine[k : k + 1, :] - swap(block) * (sign * sine[k : k + 1, :])
    u_ref[...] = result[: rows // 2]
    v_ref[...] = result[rows // 2 :]


def call(kernel, shapes, scratch=(), flops=10**7):
    return pl.pallas_call(
        kernel,
        out_shape=shapes,
        scratch_shapes=list(scratch),
        compiler_params=pltpu.CompilerParams(vmem_limit_bytes=vmem_limit),
        cost_estimate=pl.CostEstimate(flops=flops, bytes_accessed=2**20, transcendentals=0),
    )


@functools.lru_cache(None)
def tables(height, breadth, members_x, members_y):
    turn = 2.0 * math.pi
    j = np.arange(breadth)
    phase = turn * (np.outer(j, j) % breadth) / breadth
    column = split_table(np.concatenate([np.cos(phase), np.sin(phase)], axis=1))
    length = height * members_x
    k = np.arange(length)
    phase = turn * (np.outer(k, k) % length) / length
    row = np.concatenate(split_table(np.concatenate([np.cos(phase), np.sin(phase)], axis=0)), axis=0)
    g = np.arange(members_y)[:, None, None]
    partner = g ^ np.arange(members_y)[None, :, None]
    whole = breadth * members_y
    out = turn * ((partner * breadth + j) * g % whole) / whole
    home = turn * ((g * breadth + j) * partner % whole) / whole
    twiddle_out, twiddle_home = [
        np.concatenate([np.cos(phase), np.sin(phase)], axis=1).astype(np.float32) for phase in (out, home)
    ]
    return column, row, twiddle_out, twiddle_home


def partner(block, axis, k):
    return lax.ppermute(block, axis, [(i, i ^ k) for i in range(lax.axis_size(axis))])


def gather_y(block):
    return [block] + [partner(block, "gy", k) for k in range(1, lax.axis_size("gy"))]


def gather_x(block):
    own = [block] + [partner(block, "gx", k) for k in range(2, lax.axis_size("gx"), 2)]
    return [other for held in own for other in (held, partner(held, "gx", 1))]


def on_device(u_field, v_field, w_first, b_first, w_second, b_second, w_third, b_third):
    height, breadth = u_field.shape
    members_x, members_y = lax.axis_size("gx"), lax.axis_size("gy")
    grid_x, grid_y = height * members_x, breadth * members_y
    rows = height + 8
    groups = rows // 4
    span = breadth + 16
    shape = jax.ShapeDtypeStruct

    def shifted(value, axis, distance):
        peers = lax.axis_size(axis)
        return lax.ppermute(value, axis, [(i, (i + distance) % peers) for i in range(peers)])

    with jax.named_scope("columns_around"):
        both = jnp.stack([u_field, v_field]).reshape(2 * height, breadth)
        edge = shape((8, 128), f32)
        last, first = call(columns_kernel, (edge, edge), (pltpu.VMEM((128, 128), f32),))(both)
        left, right = shifted(last, "gy", 1), shifted(first, "gy", -1)

    with jax.named_scope("weights"):
        taps = w_first.transpose(0, 2, 1).astype(f32)
        biases = jnp.concatenate([b_first, b_second, b_third])[None]
        kernel_1, *biases = call(
            functools.partial(first_weights_kernel, rows=rows),
            (
                shape((groups, -(-6 * rows // 128) * 128, 256), bf16),
                shape((1, 256), f32),
                shape((1, 256), f32),
                shape((64, 1), f32),
            ),
        )(taps, biases)
        packed = jnp.concatenate([w_second.reshape(576, 64), w_third.reshape(144, 64)], axis=0)
        *others, order = call(
            other_weights_kernel,
            (shape((256, 384), bf16), shape((512, 256), bf16), shape((512, 256), bf16), shape((8, 128), f32)),
        )(packed)

    with jax.named_scope("rows_around"):
        edge = shape((8, breadth + 128), f32)
        last, first, beside = call(
            rows_kernel, (edge, edge, shape((2 * height, 128), f32)), (pltpu.VMEM((128, 128), f32),)
        )(both, right, left, biases[2], order)
        top, bottom = shifted(last, "gx", 1), shifted(first, "gx", -1)

    block = shape((2 * height, breadth), f32)
    padded = pltpu.VMEM((2, rows + 16, breadth + 128), f32)
    with jax.named_scope("advance"):
        inner = call(
            inner_kernel,
            (
                shape((groups - 4, span, 256), bf16),
                shape((groups - 6, span, 256), bf16),
                shape((2, 64, breadth + 128), f32),
            ),
            (padded,),
            flops=5 * 10**8,
        )(both, beside, kernel_1, *others, *biases[:2])
        star = call(
            advance_kernel,
            block,
            (
                padded,
                pltpu.VMEM((4, span, 256), bf16),
                pltpu.VMEM((6, span, 256), bf16),
                pltpu.VMEM((groups - 3, 64, breadth + 128), f32),
            ),
            flops=10**9,
        )(both, beside, bottom, top, kernel_1, *others, *biases, *inner)

    column, row, twiddle_out, twiddle_home = tables(height, breadth, members_x, members_y)
    column, row = [jnp.asarray(t) for t in column], jnp.asarray(row)
    spectra = call(column_kernel, block)(*gather_y(star), jnp.asarray(twiddle_out), *column)
    factors = call(
        functools.partial(factors_kernel, scale=1.0 / (grid_x * grid_y)), shape((3, grid_x, breadth), f32)
    )()
    columns = call(row_kernel, block, (pltpu.VMEM((grid_x, 2 * breadth), f32),))(
        *gather_x(spectra), factors, row, *column
    )
    part = shape((height, breadth), f32)
    return tuple(call(home_kernel, (part, part))(*gather_y(columns), jnp.asarray(twiddle_home), star))


def solution(mesh):
    return jax.shard_map(
        on_device,
        mesh=mesh,
        in_specs=(P("gx", "gy"), P("gx", "gy"), P(), P(), P(), P(), P(), P()),
        out_specs=(P("gx", "gy"), P("gx", "gy")),
        check_vma=False,
    )
```

```python
import functools
import math

import jax
import jax.numpy as jnp
import ml_dtypes
import numpy as np
from jax import lax
from jax.experimental import pallas as pl
from jax.experimental.pallas import tpu as pltpu
from jax.sharding import PartitionSpec as P

step_ratio = 0.4
stencil_base = (-0.0625, 0.5625, 0.5625, -0.0625)
f32 = jnp.float32
bf16 = jnp.bfloat16

vmem_limit = 48 * 1024 * 1024


def split(value):
    high = value.astype(bf16)
    return high, (value - high.astype(f32)).astype(bf16)


def split_table(table):
    high = table.astype(ml_dtypes.bfloat16)
    low = (table - high.astype(np.float64)).astype(ml_dtypes.bfloat16)
    return high, low


def dot(a, b):
    return jnp.dot(a, b, preferred_element_type=f32)


def product_3(value, high, low):
    rows = value.shape[0]
    first, second = split(value)
    both = dot(jnp.concatenate([first, second], axis=0), high)
    return both[:rows] + both[rows:] + dot(first, low)


def parity(shape):
    rows = lax.broadcasted_iota(jnp.int32, shape, 0)
    return jnp.where(rows < shape[0] // 2, 1.0, -1.0).astype(f32)


def swap(value):
    half = value.shape[0] // 2
    return jnp.concatenate([value[half:], value[:half]], axis=0)


def columns_kernel(both_ref, order_ref, last_ref, first_ref, strip):
    cells, breadth = both_ref.shape
    strip[cells:, :] = jnp.zeros((128 - cells, 128), f32)
    for side, out in ((0, first_ref), (breadth - 128, last_ref)):
        strip[:cells, :] = both_ref[:, side : side + 128]
        turned = strip[...].T
        out[...] = turned[0:8] if side == 0 else turned[120:128]


def rows_kernel(both_ref, right_ref, left_ref, order_ref, last_ref, first_ref, beside_ref, strip):
    height, breadth = both_ref.shape[0] // 2, both_ref.shape[1]
    strip[...] = jnp.zeros_like(strip)
    strip[0:4, :] = right_ref[0:4, :]
    strip[124:128, :] = left_ref[4:8, :]
    beside_ref[...] = strip[...].T[: 2 * height]
    for q in range(2):
        start, end, own = height * q, height * (q + 1), slice(4 * q, 4 * q + 4)
        last_ref[own, :breadth] = both_ref[end - 4 : end, :]
        last_ref[own, breadth:] = beside_ref[end - 4 : end, :]
        first_ref[own, :breadth] = both_ref[start : start + 4, :]
        first_ref[own, breadth:] = beside_ref[start : start + 4, :]


def first_weights_kernel(taps_ref, biases_ref, k1_ref, c1_ref, c2_ref, c3_ref, *, rows):
    groups, depth, _ = k1_ref.shape
    wide = [jnp.concatenate([taps_ref[i]] * 4, axis=1) for i in range(9)]
    c1_ref[...] = jnp.concatenate([biases_ref[:, :64]] * 4, axis=1)
    c2_ref[...] = jnp.concatenate([biases_ref[:, 64:128]] * 4, axis=1)
    place = lax.broadcasted_iota(jnp.int32, (64, 16), 0) // 4
    channel = 8 * (place // 8) + 4 * (place % 2) + (place // 2) % 4
    hit = channel == lax.broadcasted_iota(jnp.int32, (64, 16), 1)
    c3_ref[...] = jnp.sum(jnp.where(hit, biases_ref[:, 128:144], 0.0), axis=1, keepdims=True)
    spread = []
    for d in range(3):
        parts = [
            jnp.broadcast_to(wide[3 * d + s][q : q + 1, :], (rows, 256))
            for s in range(3)
            for q in range(2)
        ]
        parts.append(jnp.zeros((depth - 6 * rows, 256), f32))
        spread.append(jnp.concatenate(parts, axis=0))
    row = lax.broadcasted_iota(jnp.int32, (rows, 256), 0) - lax.broadcasted_iota(jnp.int32, (rows, 256), 1) // 64
    row = jnp.where(row < 0, row + rows, row)
    row = jnp.concatenate([row] * 6 + [jnp.full((depth - 6 * rows, 256), -1, jnp.int32)], axis=0)
    for r in range(groups):
        near = [row == (4 * r + d - 1) % rows for d in range(3)]
        block = jnp.where(near[0], spread[0], jnp.where(near[1], spread[1], jnp.where(near[2], spread[2], 0.0)))
        k1_ref[r] = block.astype(bf16)


def other_weights_kernel(packed_ref, k2_ref, even_ref, odd_ref, order_ref):
    order_ref[...] = jnp.zeros(order_ref.shape, f32)
    slots = {-1: 5, 0: 0, 1: 1, 2: 2, 3: 3, 4: 6}
    blank = jnp.zeros((64, 64), f32)
    for c in range(3):
        taps = [packed_ref[64 * (3 * d + c) : 64 * (3 * d + c) + 64, :].astype(f32) for d in range(3)]
        two = [(taps[0], blank), (taps[1], taps[0]), (taps[2], taps[1]), (blank, taps[2])]
        two = [jnp.concatenate(pair, axis=0).T.astype(bf16) for pair in two]
        for slot, source in enumerate((1, 2, 3, 0)):
            k2_ref[64 * slot : 64 * slot + 64, 128 * c : 128 * c + 128] = two[source]

    taps = [
        [packed_ref[576 + 16 * (3 * d + c) : 592 + 16 * (3 * d + c), :].astype(f32) for d in range(3)]
        for c in range(3)
    ]
    blank = jnp.zeros((16, 64), f32)
    filler = jnp.zeros((64, 256), bf16)
    parts = [filler] * 8
    for k, slot in slots.items():
        pieces = [taps[c][k - t + 1] if 0 <= k - t + 1 < 3 else blank for c in range(3) for t in range(4)]
        pieces += [blank] * 4
        parts[slot] = jnp.concatenate(pieces, axis=0).T.astype(bf16)
    raw = jnp.concatenate(parts, axis=0)
    source = lax.broadcasted_iota(jnp.int32, (256, 256), 0)
    target = lax.broadcasted_iota(jnp.int32, (256, 256), 1)
    inner = target % 64
    place = inner // 4
    channel = 8 * (place // 8) + 4 * (place % 2) + (place // 2) % 4
    lane = 16 * (inner % 4) + channel
    part = target // 64
    column_even = jnp.where(part == 3, -1, 64 * part + lane)
    column_odd = jnp.where(
        part == 2, -1, jnp.where(part == 3, 128 + lane, jnp.where(part == 0, 64 + lane, lane))
    )
    even_ref[...] = dot(raw, jnp.where(source == column_even, 1.0, 0.0).astype(bf16)).astype(bf16)
    odd_ref[...] = dot(raw, jnp.where(source == column_odd, 1.0, 0.0).astype(bf16)).astype(bf16)


def fill(field, both_ref, beside_ref, height, breadth):
    for q in range(2):
        field[q, 8 : 8 + height, :breadth] = both_ref[height * q : height * (q + 1), :]
        field[q, 8 : 8 + height, breadth:] = beside_ref[height * q : height * (q + 1), :]


def patches_of(field, rows, depth):
    lanes = field.shape[2]
    whole = jnp.concatenate([field[0, 8 : 8 + rows], field[1, 8 : 8 + rows]], axis=0)
    pieces = [pltpu.roll(whole, 1, 1), whole, pltpu.roll(whole, lanes - 1, 1)]
    pieces.append(jnp.zeros((depth - 6 * rows, lanes), f32))
    turned = jnp.concatenate(pieces, axis=0).T
    return jnp.concatenate([turned[: lanes - 120], turned[lanes - 8 :]], axis=0).astype(bf16)


def layer_1(patches, weights_ref, bias_ref, r):
    return jnp.maximum(dot(patches, weights_ref[r]) + bias_ref[...], 0.0).astype(bf16)


def with_neighbours(before, own, after, weights_ref):
    beside = jnp.concatenate([before[:, 128:], after[:, :128]], axis=1)
    return dot(own[...], weights_ref[:256]) + dot(beside, weights_ref[256:])


def layer_2(before, own, after, weights_ref, bias_ref):
    span = own.shape[0]
    lower = lax.broadcasted_iota(jnp.int32, (span, 128), 1) < 64
    left, right = own[:, :128], own[:, 128:]
    results = []
    for pair, below, above in ((left, right, before[:, 128:]), (right, after[:, :128], left)):
        total = dot(jnp.concatenate([pair, jnp.where(lower, below, above)], axis=1), weights_ref[...])
        total = pltpu.roll(total[:, :128], 1, 0) + total[:, 128:256] + pltpu.roll(total[:, 256:], span - 1, 0)
        results.append(jnp.maximum(total + bias_ref[:, :128], 0.0).astype(bf16))
    return jnp.concatenate(results, axis=1)


def layer_3(second, groups, r, weights_ref):
    total = with_neighbours(second((r - 1) % groups), second(r), second((r + 1) % groups), weights_ref)
    left_part = total[:, :128]
    return (
        pltpu.roll(left_part, 1, 0)
        + pltpu.roll(left_part, 64, 1)
        + pltpu.roll(total[:, 128:], total.shape[0] - 1, 0)
    )


def coefficients(second, groups, even, odd, even_ref, odd_ref):
    block = layer_3(second, groups, even, even_ref)
    if odd is not None:
        lower = lax.broadcasted_iota(jnp.int32, block.shape, 1) < 64
        block = jnp.where(lower, block, layer_3(second, groups, odd, odd_ref))
    span = block.shape[0]
    filler = jnp.zeros((112, 128), f32)
    return jnp.concatenate([block[: span - 8], filler, block[span - 8 :]], axis=0).T


def inner_kernel(
    both_ref, beside_ref, w1_ref, w2_ref, even_ref, odd_ref, b1_ref, b2_ref, first_ref, second_ref, coeff_ref, field
):
    height, breadth = both_ref.shape[0] // 2, both_ref.shape[1]
    rows = height + 8
    groups = rows // 4
    field[...] = jnp.zeros_like(field)
    fill(field, both_ref, beside_ref, height, breadth)
    patches = patches_of(field, rows, w1_ref.shape[1])
    for r in range(1, groups - 3):
        first_ref[r - 1] = layer_1(patches, w1_ref, b1_ref, r)
        if r >= 3:
            second_ref[r - 3] = layer_2(
                first_ref.at[r - 3], first_ref.at[r - 2], first_ref.at[r - 1], w2_ref, b2_ref
            )
    block = coefficients(lambda r: second_ref.at[r - 2], groups, 3, 4, even_ref, odd_ref)
    coeff_ref[0] = block[:64]
    coeff_ref[1] = block[64:]


def advance_kernel(
    both_ref, beside_ref, bot_ref, top_ref, w1_ref, w2_ref, even_ref, odd_ref, b1_ref, b2_ref, b3_ref,
    first_ref, second_ref, coeff_ref, star_ref, field, outer_first, outer_second, outer_coeff,
):
    height, breadth = both_ref.shape[0] // 2, both_ref.shape[1]
    rows = height + 8
    groups = rows // 4
    lanes = breadth + 128
    fill(field, both_ref, beside_ref, height, breadth)
    for q in range(2):
        field[q, 8 + height : 12 + height, :] = bot_ref[4 * q : 4 * q + 4, :]
        field[q, 12 + height : 16 + height, :] = top_ref[4 * q : 4 * q + 4, :]
        field[q, 0:8, :] = field[q, rows : rows + 8, :]
        field[q, 8 + rows : 16 + rows, :] = field[q, 8:16, :]
    patches = patches_of(field, rows, w1_ref.shape[1])

    ends = (groups - 3, groups - 2, groups - 1, 0, 1, groups - 4)

    def first(r):
        return outer_first.at[ends.index(r)] if r in ends[:4] else first_ref.at[r - 1]

    def second(r):
        return outer_second.at[ends.index(r)] if r in ends else second_ref.at[r - 2]

    held = {3: coeff_ref.at[0], 4: coeff_ref.at[1]}

    def do_first(r):
        outer_first[ends.index(r)] = layer_1(patches, w1_ref, b1_ref, r)

    def do_second(r):
        outer_second[ends.index(r)] = layer_2(
            first((r - 1) % groups), first(r), first((r + 1) % groups), w2_ref, b2_ref
        )

    def do_coefficients(even, odd):
        block = coefficients(second, groups, even, odd, even_ref, odd_ref)
        for r, part in ((even, block[:64]), (odd, block[64:])):
            if r is not None:
                place = len(held)
                outer_coeff[place - 2] = part
                held[r] = outer_coeff.at[place - 2]

    offsets = b3_ref[...]
    sub = lax.broadcasted_iota(jnp.int32, (8, breadth), 0) % 4

    def stacked(r, shift, qs=(0, 1)):
        start = 8 + 4 * r + shift
        return jnp.concatenate([field[q, start : start + 4, :] for q in qs], axis=0)

    def flows(r, previous):
        weights = held[r][...] + offsets
        weights = [weights[8 * i : 8 * i + 8] for i in range(8)]
        centre = stacked(r, 0)

        def stencil(d):
            four = weights[4 * d : 4 * d + 4]
            mean = (four[0] + four[1] + four[2] + four[3]) * 0.25
            return [base + w - mean for base, w in zip(stencil_base, four)]

        east = stencil(0)
        flow_x = (
            east[0] * stacked(r, -1) + east[1] * centre + east[2] * stacked(r, 1) + east[3] * stacked(r, 2)
        )
        flow_x = flow_x * (0.5 * (stacked(r, 0, (0, 0)) + stacked(r, 1, (0, 0))))
        flow_x = flow_x[:, :breadth]
        if previous is not None:
            north = stencil(1)
            flow_y = (
                north[0] * pltpu.roll(centre, 1, 1)
                + north[1] * centre
                + north[2] * pltpu.roll(centre, lanes - 1, 1)
                + north[3] * pltpu.roll(centre, lanes - 2, 1)
            )
            carrier = stacked(r, 0, (1, 1))
            flow_y = flow_y * (0.5 * (carrier + pltpu.roll(carrier, lanes - 1, 1)))
            change_y = (flow_y - pltpu.roll(flow_y, 1, 1))[:, :breadth]
            above = jnp.where(sub == 0, pltpu.roll(previous, 5, 0), pltpu.roll(flow_x, 1, 0))
            star = centre[:, :breadth] - step_ratio * (flow_x - above + change_y)
            star_ref[4 * r : 4 * r + 4, :] = star[:4]
            star_ref[height + 4 * r : height + 4 * r + 4, :] = star[4:]
        return flow_x

    for r in ends[:4]:
        do_first(r)
    for r in ends[1:5]:
        do_second(r)
    do_coefficients(groups - 1, None)
    do_coefficients(0, 1)
    do_second(groups - 4)
    previous = flows(groups - 1, None)
    previous = flows(0, previous)
    previous = flows(1, previous)
    inner = list(range(5, groups - 4))
    do_coefficients(2, inner[0])
    do_second(groups - 3)
    for r in range(2, 5):
        previous = flows(r, previous)
    do_coefficients(groups - 4, groups - 3)
    for r in range(5, groups - 2):
        previous = flows(r, previous)


def own_twiddle(ref):
    own = ref[lax.axis_index("gy")]
    half = own.shape[0] // 2
    return own[:half], own[half:]


def column_kernel(*refs):
    *blocks, twiddle_ref, high_ref, low_ref, out_ref = refs
    rows, breadth = out_ref.shape
    cosine, sine = own_twiddle(twiddle_ref)
    sign = parity((rows, breadth))
    mixed = None
    for k, ref in enumerate(blocks):
        block = ref[...] * sign
        term = block * cosine[k : k + 1, :] + swap(block) * (sign * sine[k : k + 1, :])
        mixed = term if mixed is None else mixed + term
    spectra = product_3(mixed, high_ref[...], low_ref[...])
    out_ref[...] = spectra[:, :breadth] + sign * swap(spectra[:, breadth:])


def factors_kernel(out_ref, *, scale):
    _, length, breadth = out_ref.shape
    index = lax.broadcasted_iota(jnp.int32, (length, breadth), 0)
    wave_x = jnp.where(index >= length // 2, index - length, index).astype(f32) * (2.0 * math.pi / length)
    members_y = lax.axis_size("gy")
    grid_y = members_y * breadth
    number_y = lax.axis_index("gy") + members_y * lax.broadcasted_iota(jnp.int32, (1, breadth), 1)
    wave_y = jnp.where(number_y >= grid_y // 2, number_y - grid_y, number_y).astype(f32) * (2.0 * math.pi / grid_y)
    edge_y = number_y == grid_y // 2
    edge_x = index == length // 2
    total = wave_x * wave_x + wave_y * wave_y
    zero = total == 0.0
    inverse = scale / jnp.where(zero, 1.0, total)
    same = (0.5 * inverse) * (wave_y * wave_y - wave_x * wave_x)
    cross = jnp.where(edge_x != edge_y, 0.0, -inverse * wave_x * wave_y)
    out_ref[0] = jnp.where(zero, 0.5 * scale, same)
    out_ref[1] = jnp.where(zero, -0.5 * scale, same)
    out_ref[2] = cross


def row_kernel(*refs):
    *blocks, factors_ref, table_ref, high_ref, low_ref, out_ref, gathered = refs
    rows, breadth = out_ref.shape
    height = rows // 2
    length = len(blocks) * height
    own_index = lax.axis_index("gx")
    for k, ref in enumerate(blocks):
        start = pl.multiple_of((own_index ^ k) * height, height)
        gathered[pl.ds(start, height), :breadth] = ref[:height, :]
        gathered[pl.ds(start, height), breadth:] = ref[height:, :]
    data = gathered[...]
    data, data_low = split(data)
    both = dot(table_ref[...], data)
    spectra = both[: 2 * length] + both[2 * length :] + dot(table_ref[: 2 * length], data_low)
    real_part = spectra[:length, :breadth] + spectra[length:, breadth:]
    imag_part = spectra[:length, breadth:] - spectra[length:, :breadth]
    same_real, same_imag, cross = factors_ref[0], factors_ref[1], factors_ref[2]
    kept_real = same_real * real_part - cross * imag_part
    kept_imag = same_imag * imag_part + cross * real_part
    kept, kept_low = split(jnp.concatenate([kept_real, kept_imag], axis=1))
    start = pl.multiple_of(own_index * height, height)

    table = jnp.concatenate(
        [table_ref[pl.ds(pl.multiple_of(part * length + start, height), height), :] for part in range(4)], axis=0
    )
    both = dot(table, kept)
    home = both[: 2 * height] + both[2 * height :] + dot(table[: 2 * height], kept_low)
    home = jnp.concatenate(
        [
            home[:height, :breadth] - home[height:, breadth:],
            home[:height, breadth:] + home[height:, :breadth],
        ],
        axis=0,
    )
    columns = product_3(home, high_ref[...], low_ref[...])
    out_ref[...] = columns[:, :breadth] - parity((rows, breadth)) * swap(columns[:, breadth:])


def home_kernel(*refs):
    *blocks, twiddle_ref, star_ref, u_ref, v_ref = refs
    rows, breadth = star_ref.shape
    cosine, sine = own_twiddle(twiddle_ref)
    sign = parity((rows, breadth))
    result = 0.5 * star_ref[...]
    for k, ref in enumerate(blocks):
        block = ref[...]
        result = result + block * cosine[k : k + 1, :] - swap(block) * (sign * sine[k : k + 1, :])
    u_ref[...] = result[: rows // 2]
    v_ref[...] = result[rows // 2 :]


def call(kernel, shapes, scratch=(), flops=10**7):
    return pl.pallas_call(
        kernel,
        out_shape=shapes,
        scratch_shapes=list(scratch),
        compiler_params=pltpu.CompilerParams(vmem_limit_bytes=vmem_limit),
        cost_estimate=pl.CostEstimate(flops=flops, bytes_accessed=2**20, transcendentals=0),
    )


@functools.lru_cache(None)
def tables(height, breadth, members_x, members_y):
    turn = 2.0 * math.pi
    j = np.arange(breadth)
    phase = turn * (np.outer(j, j) % breadth) / breadth
    column = split_table(np.concatenate([np.cos(phase), np.sin(phase)], axis=1))
    length = height * members_x
    k = np.arange(length)
    phase = turn * (np.outer(k, k) % length) / length
    row = np.concatenate(split_table(np.concatenate([np.cos(phase), np.sin(phase)], axis=0)), axis=0)
    g = np.arange(members_y)[:, None, None]
    partner = g ^ np.arange(members_y)[None, :, None]
    whole = breadth * members_y
    out = turn * ((partner * breadth + j) * g % whole) / whole
    home = turn * ((g * breadth + j) * partner % whole) / whole
    twiddle_out, twiddle_home = [
        np.concatenate([np.cos(phase), np.sin(phase)], axis=1).astype(np.float32) for phase in (out, home)
    ]
    return column, row, twiddle_out, twiddle_home


def partner(block, axis, k):
    return lax.ppermute(block, axis, [(i, i ^ k) for i in range(lax.axis_size(axis))])


def gather_y(block):
    return [block] + [partner(block, "gy", k) for k in range(1, lax.axis_size("gy"))]


def gather_x(block):
    own = [block] + [partner(block, "gx", k) for k in range(2, lax.axis_size("gx"), 2)]
    return [other for held in own for other in (held, partner(held, "gx", 1))]


def on_device(u_field, v_field, w_first, b_first, w_second, b_second, w_third, b_third):
    height, breadth = u_field.shape
    members_x, members_y = lax.axis_size("gx"), lax.axis_size("gy")
    grid_x, grid_y = height * members_x, breadth * members_y
    rows = height + 8
    groups = rows // 4
    span = breadth + 16
    shape = jax.ShapeDtypeStruct

    def shifted(value, axis, distance):
        peers = lax.axis_size(axis)
        return lax.ppermute(value, axis, [(i, (i + distance) % peers) for i in range(peers)])

    with jax.named_scope("weights"):
        taps = w_first.transpose(0, 2, 1).astype(f32)
        biases = jnp.concatenate([b_first, b_second, b_third])[None]
        kernel_1, *biases = call(
            functools.partial(first_weights_kernel, rows=rows),
            (
                shape((groups, -(-6 * rows // 128) * 128, 256), bf16),
                shape((1, 256), f32),
                shape((1, 256), f32),
                shape((64, 1), f32),
            ),
        )(taps, biases)

    with jax.named_scope("columns_around"):
        both = jnp.stack([u_field, v_field]).reshape(2 * height, breadth)
        edge = shape((8, 128), f32)
        last, first = call(columns_kernel, (edge, edge), (pltpu.VMEM((128, 128), f32),))(
            both, biases[2]
        )
        left, right = shifted(last, "gy", 1), shifted(first, "gy", -1)

    with jax.named_scope("weights"):
        packed = jnp.concatenate([w_second.reshape(576, 64), w_third.reshape(144, 64)], axis=0)
        *others, order = call(
            other_weights_kernel,
            (shape((256, 384), bf16), shape((512, 256), bf16), shape((512, 256), bf16), shape((8, 128), f32)),
        )(packed)

    with jax.named_scope("rows_around"):
        edge = shape((8, breadth + 128), f32)
        last, first, beside = call(
            rows_kernel, (edge, edge, shape((2 * height, 128), f32)), (pltpu.VMEM((128, 128), f32),)
        )(both, right, left, order)
        top, bottom = shifted(last, "gx", 1), shifted(first, "gx", -1)

    block = shape((2 * height, breadth), f32)
    padded = pltpu.VMEM((2, rows + 16, breadth + 128), f32)
    with jax.named_scope("advance"):
        inner = call(
            inner_kernel,
            (
                shape((groups - 4, span, 256), bf16),
                shape((groups - 6, span, 256), bf16),
                shape((2, 64, breadth + 128), f32),
            ),
            (padded,),
            flops=5 * 10**8,
        )(both, beside, kernel_1, *others, *biases[:2])
        star = call(
            advance_kernel,
            block,
            (
                padded,
                pltpu.VMEM((4, span, 256), bf16),
                pltpu.VMEM((6, span, 256), bf16),
                pltpu.VMEM((groups - 3, 64, breadth + 128), f32),
            ),
            flops=10**9,
        )(both, beside, bottom, top, kernel_1, *others, *biases, *inner)

    column, row, twiddle_out, twiddle_home = tables(height, breadth, members_x, members_y)
    column, row = [jnp.asarray(t) for t in column], jnp.asarray(row)
    spectra = call(column_kernel, block)(*gather_y(star), jnp.asarray(twiddle_out), *column)
    factors = call(
        functools.partial(factors_kernel, scale=1.0 / (grid_x * grid_y)), shape((3, grid_x, breadth), f32)
    )()
    columns = call(row_kernel, block, (pltpu.VMEM((grid_x, 2 * breadth), f32),))(
        *gather_x(spectra), factors, row, *column
    )
    part = shape((height, breadth), f32)
    return tuple(call(home_kernel, (part, part))(*gather_y(columns), jnp.asarray(twiddle_home), star))


def solution(mesh):
    return jax.shard_map(
        on_device,
        mesh=mesh,
        in_specs=(P("gx", "gy"), P("gx", "gy"), P(), P(), P(), P(), P(), P()),
        out_specs=(P("gx", "gy"), P("gx", "gy")),
        check_vma=False,
    )
```

```python
import functools
import math

import jax
import jax.numpy as jnp
import ml_dtypes
import numpy as np
from jax import lax
from jax.experimental import pallas as pl
from jax.experimental.pallas import tpu as pltpu
from jax.sharding import PartitionSpec as P

step_ratio = 0.4
stencil_base = (-0.0625, 0.5625, 0.5625, -0.0625)
f32 = jnp.float32
bf16 = jnp.bfloat16

vmem_limit = 48 * 1024 * 1024


def split(value):
    high = value.astype(bf16)
    return high, (value - high.astype(f32)).astype(bf16)


def split_table(table):
    high = table.astype(ml_dtypes.bfloat16)
    low = (table - high.astype(np.float64)).astype(ml_dtypes.bfloat16)
    return high, low


def dot(a, b):
    return jnp.dot(a, b, preferred_element_type=f32)


def product_3(value, high, low):
    rows = value.shape[0]
    first, second = split(value)
    both = dot(jnp.concatenate([first, second], axis=0), high)
    return both[:rows] + both[rows:] + dot(first, low)


def parity(shape):
    rows = lax.broadcasted_iota(jnp.int32, shape, 0)
    return jnp.where(rows < shape[0] // 2, 1.0, -1.0).astype(f32)


def swap(value):
    half = value.shape[0] // 2
    return jnp.concatenate([value[half:], value[:half]], axis=0)


def by_parity(axis, for_even, for_odd):
    return jnp.where(lax.axis_index(axis) % 2 == 0, for_even, for_odd)


def columns_kernel(both_ref, near_ref, far_ref, strip):
    cells, breadth = both_ref.shape
    strip[cells:, :] = jnp.zeros((128 - cells, 128), f32)
    strip[:cells, :] = both_ref[:, :128]
    first = strip[...].T[0:8]
    strip[:cells, :] = both_ref[:, breadth - 128 :]
    last = strip[...].T[120:128]
    near_ref[...] = by_parity("gy", last, first)
    far_ref[...] = by_parity("gy", first, last)


def rows_kernel(both_ref, from_near_ref, from_far_ref, order_ref, order_too_ref, near_ref, far_ref, beside_ref, strip):
    height, breadth = both_ref.shape[0] // 2, both_ref.shape[1]
    from_near, from_far = from_near_ref[...], from_far_ref[...]
    strip[...] = jnp.zeros_like(strip)
    strip[0:4, :] = by_parity("gy", from_near, from_far)[0:4]
    strip[124:128, :] = by_parity("gy", from_far, from_near)[4:8]
    beside = strip[...].T[: 2 * height]
    beside_ref[...] = beside
    whole = jnp.concatenate([both_ref[...], beside], axis=1)
    last = jnp.concatenate([whole[height - 4 : height], whole[2 * height - 4 :]], axis=0)
    first = jnp.concatenate([whole[:4], whole[height : height + 4]], axis=0)
    near_ref[...] = by_parity("gx", last, first)
    far_ref[...] = by_parity("gx", first, last)


def first_weights_kernel(taps_ref, biases_ref, k1_ref, c1_ref, c2_ref, c3_ref, *, rows):
    groups, depth, _ = k1_ref.shape
    wide = [jnp.concatenate([taps_ref[i]] * 4, axis=1) for i in range(9)]
    c1_ref[...] = jnp.concatenate([biases_ref[:, :64]] * 4, axis=1)
    c2_ref[...] = jnp.concatenate([biases_ref[:, 64:128]] * 4, axis=1)
    place = lax.broadcasted_iota(jnp.int32, (64, 16), 0) // 4
    channel = 8 * (place // 8) + 4 * (place % 2) + (place // 2) % 4
    hit = channel == lax.broadcasted_iota(jnp.int32, (64, 16), 1)
    c3_ref[...] = jnp.sum(jnp.where(hit, biases_ref[:, 128:144], 0.0), axis=1, keepdims=True)
    spread = []
    for d in range(3):
        parts = [
            jnp.broadcast_to(wide[3 * d + s][q : q + 1, :], (rows, 256))
            for s in range(3)
            for q in range(2)
        ]
        parts.append(jnp.zeros((depth - 6 * rows, 256), f32))
        spread.append(jnp.concatenate(parts, axis=0))
    row = lax.broadcasted_iota(jnp.int32, (rows, 256), 0) - lax.broadcasted_iota(jnp.int32, (rows, 256), 1) // 64
    row = jnp.where(row < 0, row + rows, row)
    row = jnp.concatenate([row] * 6 + [jnp.full((depth - 6 * rows, 256), -1, jnp.int32)], axis=0)
    for r in range(groups):
        near = [row == (4 * r + d - 1) % rows for d in range(3)]
        block = jnp.where(near[0], spread[0], jnp.where(near[1], spread[1], jnp.where(near[2], spread[2], 0.0)))
        k1_ref[r] = block.astype(bf16)


def other_weights_kernel(packed_ref, k2_ref, even_ref, odd_ref, order_ref):
    order_ref[...] = jnp.zeros(order_ref.shape, f32)
    slots = {-1: 5, 0: 0, 1: 1, 2: 2, 3: 3, 4: 6}
    blank = jnp.zeros((64, 64), f32)
    for c in range(3):
        taps = [packed_ref[64 * (3 * d + c) : 64 * (3 * d + c) + 64, :].astype(f32) for d in range(3)]
        two = [(taps[0], blank), (taps[1], taps[0]), (taps[2], taps[1]), (blank, taps[2])]
        two = [jnp.concatenate(pair, axis=0).T.astype(bf16) for pair in two]
        for slot, source in enumerate((1, 2, 3, 0)):
            k2_ref[64 * slot : 64 * slot + 64, 128 * c : 128 * c + 128] = two[source]

    taps = [
        [packed_ref[576 + 16 * (3 * d + c) : 592 + 16 * (3 * d + c), :].astype(f32) for d in range(3)]
        for c in range(3)
    ]
    blank = jnp.zeros((16, 64), f32)
    filler = jnp.zeros((64, 256), bf16)
    parts = [filler] * 8
    for k, slot in slots.items():
        pieces = [taps[c][k - t + 1] if 0 <= k - t + 1 < 3 else blank for c in range(3) for t in range(4)]
        pieces += [blank] * 4
        parts[slot] = jnp.concatenate(pieces, axis=0).T.astype(bf16)
    raw = jnp.concatenate(parts, axis=0)
    source = lax.broadcasted_iota(jnp.int32, (256, 256), 0)
    target = lax.broadcasted_iota(jnp.int32, (256, 256), 1)
    inner = target % 64
    place = inner // 4
    channel = 8 * (place // 8) + 4 * (place % 2) + (place // 2) % 4
    lane = 16 * (inner % 4) + channel
    part = target // 64
    column_even = jnp.where(part == 3, -1, 64 * part + lane)
    column_odd = jnp.where(
        part == 2, -1, jnp.where(part == 3, 128 + lane, jnp.where(part == 0, 64 + lane, lane))
    )
    even_ref[...] = dot(raw, jnp.where(source == column_even, 1.0, 0.0).astype(bf16)).astype(bf16)
    odd_ref[...] = dot(raw, jnp.where(source == column_odd, 1.0, 0.0).astype(bf16)).astype(bf16)


def fill(field, both_ref, beside_ref, height, breadth):
    for q in range(2):
        field[q, 8 : 8 + height, :breadth] = both_ref[height * q : height * (q + 1), :]
        field[q, 8 : 8 + height, breadth:] = beside_ref[height * q : height * (q + 1), :]


def patches_of(field, rows, depth):
    lanes = field.shape[2]
    whole = jnp.concatenate([field[0, 8 : 8 + rows], field[1, 8 : 8 + rows]], axis=0)
    pieces = [pltpu.roll(whole, 1, 1), whole, pltpu.roll(whole, lanes - 1, 1)]
    pieces.append(jnp.zeros((depth - 6 * rows, lanes), f32))
    turned = jnp.concatenate(pieces, axis=0).T
    return jnp.concatenate([turned[: lanes - 120], turned[lanes - 8 :]], axis=0).astype(bf16)


def layer_1(patches, weights_ref, bias_ref, r):
    return jnp.maximum(dot(patches, weights_ref[r]) + bias_ref[...], 0.0).astype(bf16)


def with_neighbours(before, own, after, weights_ref):
    beside = jnp.concatenate([before[:, 128:], after[:, :128]], axis=1)
    return dot(own[...], weights_ref[:256]) + dot(beside, weights_ref[256:])


def layer_2(before, own, after, weights_ref, bias_ref):
    span = own.shape[0]
    lower = lax.broadcasted_iota(jnp.int32, (span, 128), 1) < 64
    left, right = own[:, :128], own[:, 128:]
    results = []
    for pair, below, above in ((left, right, before[:, 128:]), (right, after[:, :128], left)):
        total = dot(jnp.concatenate([pair, jnp.where(lower, below, above)], axis=1), weights_ref[...])
        total = pltpu.roll(total[:, :128], 1, 0) + total[:, 128:256] + pltpu.roll(total[:, 256:], span - 1, 0)
        results.append(jnp.maximum(total + bias_ref[:, :128], 0.0).astype(bf16))
    return jnp.concatenate(results, axis=1)


def layer_3(second, groups, r, weights_ref):
    total = with_neighbours(second((r - 1) % groups), second(r), second((r + 1) % groups), weights_ref)
    left_part = total[:, :128]
    return (
        pltpu.roll(left_part, 1, 0)
        + pltpu.roll(left_part, 64, 1)
        + pltpu.roll(total[:, 128:], total.shape[0] - 1, 0)
    )


def coefficients(second, groups, even, odd, even_ref, odd_ref):
    block = layer_3(second, groups, even, even_ref)
    if odd is not None:
        lower = lax.broadcasted_iota(jnp.int32, block.shape, 1) < 64
        block = jnp.where(lower, block, layer_3(second, groups, odd, odd_ref))
    span = block.shape[0]
    filler = jnp.zeros((112, 128), f32)
    return jnp.concatenate([block[: span - 8], filler, block[span - 8 :]], axis=0).T


def inner_kernel(
    both_ref, beside_ref, w1_ref, w2_ref, even_ref, odd_ref, b1_ref, b2_ref, first_ref, second_ref, coeff_ref, field
):
    height, breadth = both_ref.shape[0] // 2, both_ref.shape[1]
    rows = height + 8
    groups = rows // 4
    field[...] = jnp.zeros_like(field)
    fill(field, both_ref, beside_ref, height, breadth)
    patches = patches_of(field, rows, w1_ref.shape[1])
    for r in range(1, groups - 3):
        first_ref[r - 1] = layer_1(patches, w1_ref, b1_ref, r)
        if r >= 3:
            second_ref[r - 3] = layer_2(
                first_ref.at[r - 3], first_ref.at[r - 2], first_ref.at[r - 1], w2_ref, b2_ref
            )
    block = coefficients(lambda r: second_ref.at[r - 2], groups, 3, 4, even_ref, odd_ref)
    coeff_ref[0] = block[:64]
    coeff_ref[1] = block[64:]


def advance_kernel(
    both_ref, beside_ref, from_near_ref, from_far_ref, w1_ref, w2_ref, even_ref, odd_ref, b1_ref, b2_ref, b3_ref,
    first_ref, second_ref, coeff_ref, star_ref, field, outer_first, outer_second, outer_coeff,
):
    height, breadth = both_ref.shape[0] // 2, both_ref.shape[1]
    rows = height + 8
    groups = rows // 4
    lanes = breadth + 128
    fill(field, both_ref, beside_ref, height, breadth)
    from_near, from_far = from_near_ref[...], from_far_ref[...]
    below, above = by_parity("gx", from_near, from_far), by_parity("gx", from_far, from_near)
    for q in range(2):
        field[q, 8 + height : 12 + height, :] = below[4 * q : 4 * q + 4]
        field[q, 12 + height : 16 + height, :] = above[4 * q : 4 * q + 4]
        field[q, 0:8, :] = field[q, rows : rows + 8, :]
        field[q, 8 + rows : 16 + rows, :] = field[q, 8:16, :]
    patches = patches_of(field, rows, w1_ref.shape[1])

    ends = (groups - 3, groups - 2, groups - 1, 0, 1, groups - 4)

    def first(r):
        return outer_first.at[ends.index(r)] if r in ends[:4] else first_ref.at[r - 1]

    def second(r):
        return outer_second.at[ends.index(r)] if r in ends else second_ref.at[r - 2]

    held = {3: coeff_ref.at[0], 4: coeff_ref.at[1]}

    def do_first(r):
        outer_first[ends.index(r)] = layer_1(patches, w1_ref, b1_ref, r)

    def do_second(r):
        outer_second[ends.index(r)] = layer_2(
            first((r - 1) % groups), first(r), first((r + 1) % groups), w2_ref, b2_ref
        )

    def do_coefficients(even, odd):
        block = coefficients(second, groups, even, odd, even_ref, odd_ref)
        for r, part in ((even, block[:64]), (odd, block[64:])):
            if r is not None:
                place = len(held)
                outer_coeff[place - 2] = part
                held[r] = outer_coeff.at[place - 2]

    offsets = b3_ref[...]
    sub = lax.broadcasted_iota(jnp.int32, (8, breadth), 0) % 4

    def stacked(r, shift, qs=(0, 1)):
        start = 8 + 4 * r + shift
        return jnp.concatenate([field[q, start : start + 4, :] for q in qs], axis=0)

    def flows(r, previous):
        weights = held[r][...] + offsets
        weights = [weights[8 * i : 8 * i + 8] for i in range(8)]
        centre = stacked(r, 0)

        def stencil(d):
            four = weights[4 * d : 4 * d + 4]
            mean = (four[0] + four[1] + four[2] + four[3]) * 0.25
            return [base + w - mean for base, w in zip(stencil_base, four)]

        east = stencil(0)
        flow_x = (
            east[0] * stacked(r, -1) + east[1] * centre + east[2] * stacked(r, 1) + east[3] * stacked(r, 2)
        )
        flow_x = flow_x * (0.5 * (stacked(r, 0, (0, 0)) + stacked(r, 1, (0, 0))))
        flow_x = flow_x[:, :breadth]
        if previous is not None:
            north = stencil(1)
            flow_y = (
                north[0] * pltpu.roll(centre, 1, 1)
                + north[1] * centre
                + north[2] * pltpu.roll(centre, lanes - 1, 1)
                + north[3] * pltpu.roll(centre, lanes - 2, 1)
            )
            carrier = stacked(r, 0, (1, 1))
            flow_y = flow_y * (0.5 * (carrier + pltpu.roll(carrier, lanes - 1, 1)))
            change_y = (flow_y - pltpu.roll(flow_y, 1, 1))[:, :breadth]
            above = jnp.where(sub == 0, pltpu.roll(previous, 5, 0), pltpu.roll(flow_x, 1, 0))
            star = centre[:, :breadth] - step_ratio * (flow_x - above + change_y)
            star_ref[4 * r : 4 * r + 4, :] = star[:4]
            star_ref[height + 4 * r : height + 4 * r + 4, :] = star[4:]
        return flow_x

    for r in ends[:4]:
        do_first(r)
    for r in ends[1:5]:
        do_second(r)
    do_coefficients(groups - 1, None)
    do_coefficients(0, 1)
    do_second(groups - 4)
    previous = flows(groups - 1, None)
    previous = flows(0, previous)
    previous = flows(1, previous)
    inner = list(range(5, groups - 4))
    do_coefficients(2, inner[0])
    do_second(groups - 3)
    for r in range(2, 5):
        previous = flows(r, previous)
    do_coefficients(groups - 4, groups - 3)
    for r in range(5, groups - 2):
        previous = flows(r, previous)


def own_twiddle(ref):
    own = ref[lax.axis_index("gy")]
    half = own.shape[0] // 2
    return own[:half], own[half:]


def column_kernel(*refs):
    *blocks, twiddle_ref, high_ref, low_ref, out_ref = refs
    rows, breadth = out_ref.shape
    cosine, sine = own_twiddle(twiddle_ref)
    sign = parity((rows, breadth))
    mixed = None
    for k, ref in enumerate(blocks):
        block = ref[...] * sign
        term = block * cosine[k : k + 1, :] + swap(block) * (sign * sine[k : k + 1, :])
        mixed = term if mixed is None else mixed + term
    spectra = product_3(mixed, high_ref[...], low_ref[...])
    out_ref[...] = spectra[:, :breadth] + sign * swap(spectra[:, breadth:])


def factors_kernel(out_ref, *, scale):
    _, length, breadth = out_ref.shape
    index = lax.broadcasted_iota(jnp.int32, (length, breadth), 0)
    wave_x = jnp.where(index >= length // 2, index - length, index).astype(f32) * (2.0 * math.pi / length)
    members_y = lax.axis_size("gy")
    grid_y = members_y * breadth
    number_y = lax.axis_index("gy") + members_y * lax.broadcasted_iota(jnp.int32, (1, breadth), 1)
    wave_y = jnp.where(number_y >= grid_y // 2, number_y - grid_y, number_y).astype(f32) * (2.0 * math.pi / grid_y)
    edge_y = number_y == grid_y // 2
    edge_x = index == length // 2
    total = wave_x * wave_x + wave_y * wave_y
    zero = total == 0.0
    inverse = scale / jnp.where(zero, 1.0, total)
    same = (0.5 * inverse) * (wave_y * wave_y - wave_x * wave_x)
    cross = jnp.where(edge_x != edge_y, 0.0, -inverse * wave_x * wave_y)
    out_ref[0] = jnp.where(zero, 0.5 * scale, same)
    out_ref[1] = jnp.where(zero, -0.5 * scale, same)
    out_ref[2] = cross


def row_kernel(*refs):
    *blocks, factors_ref, table_ref, high_ref, low_ref, out_ref, gathered = refs
    rows, breadth = out_ref.shape
    height = rows // 2
    length = len(blocks) * height
    own_index = lax.axis_index("gx")
    for k, ref in enumerate(blocks):
        start = pl.multiple_of((own_index ^ k) * height, height)
        gathered[pl.ds(start, height), :breadth] = ref[:height, :]
        gathered[pl.ds(start, height), breadth:] = ref[height:, :]
    data = gathered[...]
    data, data_low = split(data)
    both = dot(table_ref[...], data)
    spectra = both[: 2 * length] + both[2 * length :] + dot(table_ref[: 2 * length], data_low)
    real_part = spectra[:length, :breadth] + spectra[length:, breadth:]
    imag_part = spectra[:length, breadth:] - spectra[length:, :breadth]
    same_real, same_imag, cross = factors_ref[0], factors_ref[1], factors_ref[2]
    kept_real = same_real * real_part - cross * imag_part
    kept_imag = same_imag * imag_part + cross * real_part
    kept, kept_low = split(jnp.concatenate([kept_real, kept_imag], axis=1))
    start = pl.multiple_of(own_index * height, height)

    table = jnp.concatenate(
        [table_ref[pl.ds(pl.multiple_of(part * length + start, height), height), :] for part in range(4)], axis=0
    )
    both = dot(table, kept)
    home = both[: 2 * height] + both[2 * height :] + dot(table[: 2 * height], kept_low)
    home = jnp.concatenate(
        [
            home[:height, :breadth] - home[height:, breadth:],
            home[:height, breadth:] + home[height:, :breadth],
        ],
        axis=0,
    )
    columns = product_3(home, high_ref[...], low_ref[...])
    out_ref[...] = columns[:, :breadth] - parity((rows, breadth)) * swap(columns[:, breadth:])


def home_kernel(*refs):
    *blocks, twiddle_ref, star_ref, u_ref, v_ref = refs
    rows, breadth = star_ref.shape
    cosine, sine = own_twiddle(twiddle_ref)
    sign = parity((rows, breadth))
    result = 0.5 * star_ref[...]
    for k, ref in enumerate(blocks):
        block = ref[...]
        result = result + block * cosine[k : k + 1, :] - swap(block) * (sign * sine[k : k + 1, :])
    u_ref[...] = result[: rows // 2]
    v_ref[...] = result[rows // 2 :]


def call(kernel, shapes, scratch=(), flops=10**7):
    return pl.pallas_call(
        kernel,
        out_shape=shapes,
        scratch_shapes=list(scratch),
        compiler_params=pltpu.CompilerParams(vmem_limit_bytes=vmem_limit),
        cost_estimate=pl.CostEstimate(flops=flops, bytes_accessed=2**20, transcendentals=0),
    )


@functools.lru_cache(None)
def tables(height, breadth, members_x, members_y):
    turn = 2.0 * math.pi
    j = np.arange(breadth)
    phase = turn * (np.outer(j, j) % breadth) / breadth
    column = split_table(np.concatenate([np.cos(phase), np.sin(phase)], axis=1))
    length = height * members_x
    k = np.arange(length)
    phase = turn * (np.outer(k, k) % length) / length
    row = np.concatenate(split_table(np.concatenate([np.cos(phase), np.sin(phase)], axis=0)), axis=0)
    g = np.arange(members_y)[:, None, None]
    partner = g ^ np.arange(members_y)[None, :, None]
    whole = breadth * members_y
    out = turn * ((partner * breadth + j) * g % whole) / whole
    home = turn * ((g * breadth + j) * partner % whole) / whole
    twiddle_out, twiddle_home = [
        np.concatenate([np.cos(phase), np.sin(phase)], axis=1).astype(np.float32) for phase in (out, home)
    ]
    return column, row, twiddle_out, twiddle_home


def partner(block, axis, k):
    return lax.ppermute(block, axis, [(i, i ^ k) for i in range(lax.axis_size(axis))])


def gather_y(block):
    return [block] + [partner(block, "gy", k) for k in range(1, lax.axis_size("gy"))]


def gather_x(block):
    own = [block] + [partner(block, "gx", k) for k in range(2, lax.axis_size("gx"), 2)]
    return [other for held in own for other in (held, partner(held, "gx", 1))]


def on_device(u_field, v_field, w_first, b_first, w_second, b_second, w_third, b_third):
    height, breadth = u_field.shape
    members_x, members_y = lax.axis_size("gx"), lax.axis_size("gy")
    grid_x, grid_y = height * members_x, breadth * members_y
    rows = height + 8
    groups = rows // 4
    span = breadth + 16
    shape = jax.ShapeDtypeStruct

    def swapped(near, far, axis):
        peers = lax.axis_size(axis)
        after, before = lambda i: (i + 1) % peers, lambda i: (i - 1) % peers
        pairs = [(i, before(i) if i % 2 else after(i)) for i in range(peers)]
        other_pairs = [(i, after(i) if i % 2 else before(i)) for i in range(peers)]
        return lax.ppermute(near, axis, pairs), lax.ppermute(far, axis, other_pairs)

    with jax.named_scope("columns_around"):
        both = jnp.stack([u_field, v_field]).reshape(2 * height, breadth)
        edge = shape((8, 128), f32)
        near, far = call(columns_kernel, (edge, edge), (pltpu.VMEM((128, 128), f32),))(both)
        near, far = swapped(near, far, "gy")

    with jax.named_scope("weights"):
        taps = w_first.transpose(0, 2, 1).astype(f32)
        biases = jnp.concatenate([b_first, b_second, b_third])[None]
        kernel_1, *biases = call(
            functools.partial(first_weights_kernel, rows=rows),
            (
                shape((groups, -(-6 * rows // 128) * 128, 256), bf16),
                shape((1, 256), f32),
                shape((1, 256), f32),
                shape((64, 1), f32),
            ),
        )(taps, biases)
        packed = jnp.concatenate([w_second.reshape(576, 64), w_third.reshape(144, 64)], axis=0)
        *others, order = call(
            other_weights_kernel,
            (shape((256, 384), bf16), shape((512, 256), bf16), shape((512, 256), bf16), shape((8, 128), f32)),
        )(packed)

    with jax.named_scope("rows_around"):
        edge = shape((8, breadth + 128), f32)
        near, far, beside = call(
            rows_kernel, (edge, edge, shape((2 * height, 128), f32)), (pltpu.VMEM((128, 128), f32),)
        )(both, near, far, biases[2], order)
        near, far = swapped(near, far, "gx")

    block = shape((2 * height, breadth), f32)
    padded = pltpu.VMEM((2, rows + 16, breadth + 128), f32)
    with jax.named_scope("advance"):
        inner = call(
            inner_kernel,
            (
                shape((groups - 4, span, 256), bf16),
                shape((groups - 6, span, 256), bf16),
                shape((2, 64, breadth + 128), f32),
            ),
            (padded,),
            flops=5 * 10**8,
        )(both, beside, kernel_1, *others, *biases[:2])
        star = call(
            advance_kernel,
            block,
            (
                padded,
                pltpu.VMEM((4, span, 256), bf16),
                pltpu.VMEM((6, span, 256), bf16),
                pltpu.VMEM((groups - 3, 64, breadth + 128), f32),
            ),
            flops=10**9,
        )(both, beside, near, far, kernel_1, *others, *biases, *inner)

    column, row, twiddle_out, twiddle_home = tables(height, breadth, members_x, members_y)
    column, row = [jnp.asarray(t) for t in column], jnp.asarray(row)
    spectra = call(column_kernel, block)(*gather_y(star), jnp.asarray(twiddle_out), *column)
    factors = call(
        functools.partial(factors_kernel, scale=1.0 / (grid_x * grid_y)), shape((3, grid_x, breadth), f32)
    )()
    columns = call(row_kernel, block, (pltpu.VMEM((grid_x, 2 * breadth), f32),))(
        *gather_x(spectra), factors, row, *column
    )
    part = shape((height, breadth), f32)
    return tuple(call(home_kernel, (part, part))(*gather_y(columns), jnp.asarray(twiddle_home), star))


def solution(mesh):
    return jax.shard_map(
        on_device,
        mesh=mesh,
        in_specs=(P("gx", "gy"), P("gx", "gy"), P(), P(), P(), P(), P(), P()),
        out_specs=(P("gx", "gy"), P("gx", "gy")),
        check_vma=False,
    )
```

```python
import functools
import math

import jax
import jax.numpy as jnp
import ml_dtypes
import numpy as np
from jax import lax
from jax.experimental import pallas as pl
from jax.experimental.pallas import tpu as pltpu
from jax.sharding import PartitionSpec as P

step_ratio = 0.4
stencil_base = (-0.0625, 0.5625, 0.5625, -0.0625)
f32 = jnp.float32
bf16 = jnp.bfloat16

vmem_limit = 48 * 1024 * 1024


def split(value):
    high = value.astype(bf16)
    return high, (value - high.astype(f32)).astype(bf16)


def split_table(table):
    high = table.astype(ml_dtypes.bfloat16)
    low = (table - high.astype(np.float64)).astype(ml_dtypes.bfloat16)
    return high, low


def dot(a, b):
    return jnp.dot(a, b, preferred_element_type=f32)


def product_3(value, high, low):
    rows = value.shape[0]
    first, second = split(value)
    both = dot(jnp.concatenate([first, second], axis=0), high)
    return both[:rows] + both[rows:] + dot(first, low)


def parity(shape):
    rows = lax.broadcasted_iota(jnp.int32, shape, 0)
    return jnp.where(rows < shape[0] // 2, 1.0, -1.0).astype(f32)


def swap(value):
    half = value.shape[0] // 2
    return jnp.concatenate([value[half:], value[:half]], axis=0)


def by_parity(axis, for_even, for_odd):
    return jnp.where(lax.axis_index(axis) % 2 == 0, for_even, for_odd)


def columns_kernel(both_ref, near_ref, far_ref, strip):
    cells, breadth = both_ref.shape
    strip[cells:, :] = jnp.zeros((128 - cells, 128), f32)
    strip[:cells, :] = both_ref[:, :128]
    first = strip[...].T[0:8]
    strip[:cells, :] = both_ref[:, breadth - 128 :]
    last = strip[...].T[120:128]
    near_ref[...] = by_parity("gy", last, first)
    far_ref[...] = by_parity("gy", first, last)


def rows_kernel(both_ref, from_near_ref, from_far_ref, order_ref, order_too_ref, near_ref, far_ref, beside_ref, strip):
    height, breadth = both_ref.shape[0] // 2, both_ref.shape[1]
    from_near, from_far = from_near_ref[...], from_far_ref[...]
    strip[...] = jnp.zeros_like(strip)
    strip[0:4, :] = by_parity("gy", from_near, from_far)[0:4]
    strip[124:128, :] = by_parity("gy", from_far, from_near)[4:8]
    beside = strip[...].T[: 2 * height]
    beside_ref[...] = beside
    whole = jnp.concatenate([both_ref[...], beside], axis=1)
    last = jnp.concatenate([whole[height - 4 : height], whole[2 * height - 4 :]], axis=0)
    first = jnp.concatenate([whole[:4], whole[height : height + 4]], axis=0)
    near_ref[...] = by_parity("gx", last, first)
    far_ref[...] = by_parity("gx", first, last)


def first_weights_kernel(taps_ref, biases_ref, k1_ref, c1_ref, c2_ref, c3_ref, *, rows):
    groups, depth, _ = k1_ref.shape
    wide = [jnp.concatenate([taps_ref[i]] * 4, axis=1) for i in range(9)]
    c1_ref[...] = jnp.concatenate([biases_ref[:, :64]] * 4, axis=1)
    c2_ref[...] = jnp.concatenate([biases_ref[:, 64:128]] * 4, axis=1)
    place = lax.broadcasted_iota(jnp.int32, (64, 16), 0) // 4
    channel = 8 * (place // 8) + 4 * (place % 2) + (place // 2) % 4
    hit = channel == lax.broadcasted_iota(jnp.int32, (64, 16), 1)
    c3_ref[...] = jnp.sum(jnp.where(hit, biases_ref[:, 128:144], 0.0), axis=1, keepdims=True)
    spread = []
    for d in range(3):
        parts = [
            jnp.broadcast_to(wide[3 * d + s][q : q + 1, :], (rows, 256))
            for s in range(3)
            for q in range(2)
        ]
        parts.append(jnp.zeros((depth - 6 * rows, 256), f32))
        spread.append(jnp.concatenate(parts, axis=0))
    row = lax.broadcasted_iota(jnp.int32, (rows, 256), 0) - lax.broadcasted_iota(jnp.int32, (rows, 256), 1) // 64
    row = jnp.where(row < 0, row + rows, row)
    row = jnp.concatenate([row] * 6 + [jnp.full((depth - 6 * rows, 256), -1, jnp.int32)], axis=0)
    for r in range(groups):
        near = [row == (4 * r + d - 1) % rows for d in range(3)]
        block = jnp.where(near[0], spread[0], jnp.where(near[1], spread[1], jnp.where(near[2], spread[2], 0.0)))
        k1_ref[r] = block.astype(bf16)


def other_weights_kernel(packed_ref, k2_ref, even_ref, odd_ref):
    slots = {-1: 5, 0: 0, 1: 1, 2: 2, 3: 3, 4: 6}
    blank = jnp.zeros((64, 64), f32)
    for c in range(3):
        taps = [packed_ref[64 * (3 * d + c) : 64 * (3 * d + c) + 64, :].astype(f32) for d in range(3)]
        two = [(taps[0], blank), (taps[1], taps[0]), (taps[2], taps[1]), (blank, taps[2])]
        two = [jnp.concatenate(pair, axis=0).T.astype(bf16) for pair in two]
        for slot, source in enumerate((1, 2, 3, 0)):
            k2_ref[64 * slot : 64 * slot + 64, 128 * c : 128 * c + 128] = two[source]

    taps = [
        [packed_ref[576 + 16 * (3 * d + c) : 592 + 16 * (3 * d + c), :].astype(f32) for d in range(3)]
        for c in range(3)
    ]
    blank = jnp.zeros((16, 64), f32)
    filler = jnp.zeros((64, 256), bf16)
    parts = [filler] * 8
    for k, slot in slots.items():
        pieces = [taps[c][k - t + 1] if 0 <= k - t + 1 < 3 else blank for c in range(3) for t in range(4)]
        pieces += [blank] * 4
        parts[slot] = jnp.concatenate(pieces, axis=0).T.astype(bf16)
    raw = jnp.concatenate(parts, axis=0)
    source = lax.broadcasted_iota(jnp.int32, (256, 256), 0)
    target = lax.broadcasted_iota(jnp.int32, (256, 256), 1)
    inner = target % 64
    place = inner // 4
    channel = 8 * (place // 8) + 4 * (place % 2) + (place // 2) % 4
    lane = 16 * (inner % 4) + channel
    part = target // 64
    column_even = jnp.where(part == 3, -1, 64 * part + lane)
    column_odd = jnp.where(
        part == 2, -1, jnp.where(part == 3, 128 + lane, jnp.where(part == 0, 64 + lane, lane))
    )
    even_ref[...] = dot(raw, jnp.where(source == column_even, 1.0, 0.0).astype(bf16)).astype(bf16)
    odd_ref[...] = dot(raw, jnp.where(source == column_odd, 1.0, 0.0).astype(bf16)).astype(bf16)


def fill(field, both_ref, beside_ref, height, breadth):
    for q in range(2):
        field[q, 8 : 8 + height, :breadth] = both_ref[height * q : height * (q + 1), :]
        field[q, 8 : 8 + height, breadth:] = beside_ref[height * q : height * (q + 1), :]


def patches_of(field, rows, depth):
    lanes = field.shape[2]
    whole = jnp.concatenate([field[0, 8 : 8 + rows], field[1, 8 : 8 + rows]], axis=0)
    pieces = [pltpu.roll(whole, 1, 1), whole, pltpu.roll(whole, lanes - 1, 1)]
    pieces.append(jnp.zeros((depth - 6 * rows, lanes), f32))
    turned = jnp.concatenate(pieces, axis=0).T
    return jnp.concatenate([turned[: lanes - 120], turned[lanes - 8 :]], axis=0).astype(bf16)


def layer_1(patches, weights_ref, bias_ref, r):
    return jnp.maximum(dot(patches, weights_ref[r]) + bias_ref[...], 0.0).astype(bf16)


def with_neighbours(before, own, after, weights_ref):
    beside = jnp.concatenate([before[:, 128:], after[:, :128]], axis=1)
    return dot(own[...], weights_ref[:256]) + dot(beside, weights_ref[256:])


def layer_2(before, own, after, weights_ref, bias_ref):
    span = own.shape[0]
    lower = lax.broadcasted_iota(jnp.int32, (span, 128), 1) < 64
    left, right = own[:, :128], own[:, 128:]
    results = []
    for pair, below, above in ((left, right, before[:, 128:]), (right, after[:, :128], left)):
        total = dot(jnp.concatenate([pair, jnp.where(lower, below, above)], axis=1), weights_ref[...])
        total = pltpu.roll(total[:, :128], 1, 0) + total[:, 128:256] + pltpu.roll(total[:, 256:], span - 1, 0)
        results.append(jnp.maximum(total + bias_ref[:, :128], 0.0).astype(bf16))
    return jnp.concatenate(results, axis=1)


def layer_3(second, groups, r, weights_ref):
    total = with_neighbours(second((r - 1) % groups), second(r), second((r + 1) % groups), weights_ref)
    left_part = total[:, :128]
    return (
        pltpu.roll(left_part, 1, 0)
        + pltpu.roll(left_part, 64, 1)
        + pltpu.roll(total[:, 128:], total.shape[0] - 1, 0)
    )


def coefficients(second, groups, even, odd, even_ref, odd_ref):
    block = layer_3(second, groups, even, even_ref)
    if odd is not None:
        lower = lax.broadcasted_iota(jnp.int32, block.shape, 1) < 64
        block = jnp.where(lower, block, layer_3(second, groups, odd, odd_ref))
    span = block.shape[0]
    filler = jnp.zeros((112, 128), f32)
    return jnp.concatenate([block[: span - 8], filler, block[span - 8 :]], axis=0).T


def inner_kernel(
    both_ref, beside_ref, w1_ref, w2_ref, even_ref, odd_ref, b1_ref, b2_ref, first_ref, second_ref, coeff_ref, field
):
    height, breadth = both_ref.shape[0] // 2, both_ref.shape[1]
    rows = height + 8
    groups = rows // 4
    field[...] = jnp.zeros_like(field)
    fill(field, both_ref, beside_ref, height, breadth)
    patches = patches_of(field, rows, w1_ref.shape[1])
    for r in range(1, groups - 3):
        first_ref[r - 1] = layer_1(patches, w1_ref, b1_ref, r)
        if r >= 3:
            second_ref[r - 3] = layer_2(
                first_ref.at[r - 3], first_ref.at[r - 2], first_ref.at[r - 1], w2_ref, b2_ref
            )
    block = coefficients(lambda r: second_ref.at[r - 2], groups, 3, 4, even_ref, odd_ref)
    coeff_ref[0] = block[:64]
    coeff_ref[1] = block[64:]


def advance_kernel(
    both_ref, beside_ref, from_near_ref, from_far_ref, w1_ref, w2_ref, even_ref, odd_ref, b1_ref, b2_ref, b3_ref,
    first_ref, second_ref, coeff_ref, star_ref, field, outer_first, outer_second, outer_coeff,
):
    height, breadth = both_ref.shape[0] // 2, both_ref.shape[1]
    rows = height + 8
    groups = rows // 4
    lanes = breadth + 128
    fill(field, both_ref, beside_ref, height, breadth)
    from_near, from_far = from_near_ref[...], from_far_ref[...]
    below, above = by_parity("gx", from_near, from_far), by_parity("gx", from_far, from_near)
    for q in range(2):
        field[q, 8 + height : 12 + height, :] = below[4 * q : 4 * q + 4]
        field[q, 12 + height : 16 + height, :] = above[4 * q : 4 * q + 4]
        field[q, 0:8, :] = field[q, rows : rows + 8, :]
        field[q, 8 + rows : 16 + rows, :] = field[q, 8:16, :]
    patches = patches_of(field, rows, w1_ref.shape[1])

    ends = (groups - 3, groups - 2, groups - 1, 0, 1, groups - 4)

    def first(r):
        return outer_first.at[ends.index(r)] if r in ends[:4] else first_ref.at[r - 1]

    def second(r):
        return outer_second.at[ends.index(r)] if r in ends else second_ref.at[r - 2]

    held = {3: coeff_ref.at[0], 4: coeff_ref.at[1]}

    def do_first(r):
        outer_first[ends.index(r)] = layer_1(patches, w1_ref, b1_ref, r)

    def do_second(r):
        outer_second[ends.index(r)] = layer_2(
            first((r - 1) % groups), first(r), first((r + 1) % groups), w2_ref, b2_ref
        )

    def do_coefficients(even, odd):
        block = coefficients(second, groups, even, odd, even_ref, odd_ref)
        for r, part in ((even, block[:64]), (odd, block[64:])):
            if r is not None:
                place = len(held)
                outer_coeff[place - 2] = part
                held[r] = outer_coeff.at[place - 2]

    offsets = b3_ref[...]
    sub = lax.broadcasted_iota(jnp.int32, (8, breadth), 0) % 4

    def stacked(r, shift, qs=(0, 1)):
        start = 8 + 4 * r + shift
        return jnp.concatenate([field[q, start : start + 4, :] for q in qs], axis=0)

    def flows(r, previous):
        weights = held[r][...] + offsets
        weights = [weights[8 * i : 8 * i + 8] for i in range(8)]
        centre = stacked(r, 0)

        def stencil(d):
            four = weights[4 * d : 4 * d + 4]
            mean = (four[0] + four[1] + four[2] + four[3]) * 0.25
            return [base + w - mean for base, w in zip(stencil_base, four)]

        east = stencil(0)
        flow_x = (
            east[0] * stacked(r, -1) + east[1] * centre + east[2] * stacked(r, 1) + east[3] * stacked(r, 2)
        )
        flow_x = flow_x * (0.5 * (stacked(r, 0, (0, 0)) + stacked(r, 1, (0, 0))))
        flow_x = flow_x[:, :breadth]
        if previous is not None:
            north = stencil(1)
            flow_y = (
                north[0] * pltpu.roll(centre, 1, 1)
                + north[1] * centre
                + north[2] * pltpu.roll(centre, lanes - 1, 1)
                + north[3] * pltpu.roll(centre, lanes - 2, 1)
            )
            carrier = stacked(r, 0, (1, 1))
            flow_y = flow_y * (0.5 * (carrier + pltpu.roll(carrier, lanes - 1, 1)))
            change_y = (flow_y - pltpu.roll(flow_y, 1, 1))[:, :breadth]
            above = jnp.where(sub == 0, pltpu.roll(previous, 5, 0), pltpu.roll(flow_x, 1, 0))
            star = centre[:, :breadth] - step_ratio * (flow_x - above + change_y)
            star_ref[4 * r : 4 * r + 4, :] = star[:4]
            star_ref[height + 4 * r : height + 4 * r + 4, :] = star[4:]
        return flow_x

    for r in ends[:4]:
        do_first(r)
    for r in ends[1:5]:
        do_second(r)
    do_coefficients(groups - 1, None)
    do_coefficients(0, 1)
    do_second(groups - 4)
    previous = flows(groups - 1, None)
    previous = flows(0, previous)
    previous = flows(1, previous)
    inner = list(range(5, groups - 4))
    do_coefficients(2, inner[0])
    do_second(groups - 3)
    for r in range(2, 5):
        previous = flows(r, previous)
    do_coefficients(groups - 4, groups - 3)
    for r in range(5, groups - 2):
        previous = flows(r, previous)


def own_twiddle(ref):
    own = ref[lax.axis_index("gy")]
    half = own.shape[0] // 2
    return own[:half], own[half:]


def column_kernel(*refs):
    *blocks, twiddle_ref, high_ref, low_ref, out_ref = refs
    rows, breadth = out_ref.shape
    cosine, sine = own_twiddle(twiddle_ref)
    sign = parity((rows, breadth))
    mixed = None
    for k, ref in enumerate(blocks):
        block = ref[...] * sign
        term = block * cosine[k : k + 1, :] + swap(block) * (sign * sine[k : k + 1, :])
        mixed = term if mixed is None else mixed + term
    spectra = product_3(mixed, high_ref[...], low_ref[...])
    out_ref[...] = spectra[:, :breadth] + sign * swap(spectra[:, breadth:])


def factors_kernel(out_ref, *, scale):
    _, length, breadth = out_ref.shape
    index = lax.broadcasted_iota(jnp.int32, (length, breadth), 0)
    wave_x = jnp.where(index >= length // 2, index - length, index).astype(f32) * (2.0 * math.pi / length)
    members_y = lax.axis_size("gy")
    grid_y = members_y * breadth
    number_y = lax.axis_index("gy") + members_y * lax.broadcasted_iota(jnp.int32, (1, breadth), 1)
    wave_y = jnp.where(number_y >= grid_y // 2, number_y - grid_y, number_y).astype(f32) * (2.0 * math.pi / grid_y)
    edge_y = number_y == grid_y // 2
    edge_x = index == length // 2
    total = wave_x * wave_x + wave_y * wave_y
    zero = total == 0.0
    inverse = scale / jnp.where(zero, 1.0, total)
    same = (0.5 * inverse) * (wave_y * wave_y - wave_x * wave_x)
    cross = jnp.where(edge_x != edge_y, 0.0, -inverse * wave_x * wave_y)
    out_ref[0] = jnp.where(zero, 0.5 * scale, same)
    out_ref[1] = jnp.where(zero, -0.5 * scale, same)
    out_ref[2] = cross


def row_kernel(*refs):
    *blocks, factors_ref, table_ref, high_ref, low_ref, out_ref, gathered = refs
    rows, breadth = out_ref.shape
    height = rows // 2
    length = len(blocks) * height
    own_index = lax.axis_index("gx")
    for k, ref in enumerate(blocks):
        start = pl.multiple_of((own_index ^ k) * height, height)
        gathered[pl.ds(start, height), :breadth] = ref[:height, :]
        gathered[pl.ds(start, height), breadth:] = ref[height:, :]
    data = gathered[...]
    data, data_low = split(data)
    both = dot(table_ref[...], data)
    spectra = both[: 2 * length] + both[2 * length :] + dot(table_ref[: 2 * length], data_low)
    real_part = spectra[:length, :breadth] + spectra[length:, breadth:]
    imag_part = spectra[:length, breadth:] - spectra[length:, :breadth]
    same_real, same_imag, cross = factors_ref[0], factors_ref[1], factors_ref[2]
    kept_real = same_real * real_part - cross * imag_part
    kept_imag = same_imag * imag_part + cross * real_part
    kept, kept_low = split(jnp.concatenate([kept_real, kept_imag], axis=1))
    start = pl.multiple_of(own_index * height, height)

    table = jnp.concatenate(
        [table_ref[pl.ds(pl.multiple_of(part * length + start, height), height), :] for part in range(4)], axis=0
    )
    both = dot(table, kept)
    home = both[: 2 * height] + both[2 * height :] + dot(table[: 2 * height], kept_low)
    home = jnp.concatenate(
        [
            home[:height, :breadth] - home[height:, breadth:],
            home[:height, breadth:] + home[height:, :breadth],
        ],
        axis=0,
    )
    columns = product_3(home, high_ref[...], low_ref[...])
    out_ref[...] = columns[:, :breadth] - parity((rows, breadth)) * swap(columns[:, breadth:])


def home_kernel(*refs):
    *blocks, twiddle_ref, star_ref, u_ref, v_ref = refs
    rows, breadth = star_ref.shape
    cosine, sine = own_twiddle(twiddle_ref)
    sign = parity((rows, breadth))
    result = 0.5 * star_ref[...]
    for k, ref in enumerate(blocks):
        block = ref[...]
        result = result + block * cosine[k : k + 1, :] - swap(block) * (sign * sine[k : k + 1, :])
    u_ref[...] = result[: rows // 2]
    v_ref[...] = result[rows // 2 :]


def call(kernel, shapes, scratch=(), flops=10**7):
    return pl.pallas_call(
        kernel,
        out_shape=shapes,
        scratch_shapes=list(scratch),
        compiler_params=pltpu.CompilerParams(vmem_limit_bytes=vmem_limit),
        cost_estimate=pl.CostEstimate(flops=flops, bytes_accessed=2**20, transcendentals=0),
    )


@functools.lru_cache(None)
def tables(height, breadth, members_x, members_y):
    turn = 2.0 * math.pi
    j = np.arange(breadth)
    phase = turn * (np.outer(j, j) % breadth) / breadth
    column = split_table(np.concatenate([np.cos(phase), np.sin(phase)], axis=1))
    length = height * members_x
    k = np.arange(length)
    phase = turn * (np.outer(k, k) % length) / length
    row = np.concatenate(split_table(np.concatenate([np.cos(phase), np.sin(phase)], axis=0)), axis=0)
    g = np.arange(members_y)[:, None, None]
    partner = g ^ np.arange(members_y)[None, :, None]
    whole = breadth * members_y
    out = turn * ((partner * breadth + j) * g % whole) / whole
    home = turn * ((g * breadth + j) * partner % whole) / whole
    twiddle_out, twiddle_home = [
        np.concatenate([np.cos(phase), np.sin(phase)], axis=1).astype(np.float32) for phase in (out, home)
    ]
    return column, row, twiddle_out, twiddle_home


def partner(block, axis, k):
    return lax.ppermute(block, axis, [(i, i ^ k) for i in range(lax.axis_size(axis))])


def gather_y(block):
    return [block] + [partner(block, "gy", k) for k in range(1, lax.axis_size("gy"))]


def gather_x(block):
    own = [block] + [partner(block, "gx", k) for k in range(2, lax.axis_size("gx"), 2)]
    return [other for held in own for other in (held, partner(held, "gx", 1))]


def on_device(u_field, v_field, w_first, b_first, w_second, b_second, w_third, b_third):
    height, breadth = u_field.shape
    members_x, members_y = lax.axis_size("gx"), lax.axis_size("gy")
    grid_x, grid_y = height * members_x, breadth * members_y
    rows = height + 8
    groups = rows // 4
    span = breadth + 16
    shape = jax.ShapeDtypeStruct

    def swapped(near, far, axis):
        peers = lax.axis_size(axis)
        after, before = lambda i: (i + 1) % peers, lambda i: (i - 1) % peers
        pairs = [(i, before(i) if i % 2 else after(i)) for i in range(peers)]
        other_pairs = [(i, after(i) if i % 2 else before(i)) for i in range(peers)]
        return lax.ppermute(near, axis, pairs), lax.ppermute(far, axis, other_pairs)

    with jax.named_scope("columns_around"):
        both = jnp.stack([u_field, v_field]).reshape(2 * height, breadth)
        edge = shape((8, 128), f32)
        near, far = call(columns_kernel, (edge, edge), (pltpu.VMEM((128, 128), f32),))(both)
        near, far = swapped(near, far, "gy")

    with jax.named_scope("weights"):
        taps = w_first.transpose(0, 2, 1).astype(f32)
        biases = jnp.concatenate([b_first, b_second, b_third])[None]
        kernel_1, *biases = call(
            functools.partial(first_weights_kernel, rows=rows),
            (
                shape((groups, -(-6 * rows // 128) * 128, 256), bf16),
                shape((1, 256), f32),
                shape((1, 256), f32),
                shape((64, 1), f32),
            ),
        )(taps, biases)
        packed = jnp.concatenate([w_second.reshape(576, 64), w_third.reshape(144, 64)], axis=0)
        others = call(
            other_weights_kernel,
            (shape((256, 384), bf16), shape((512, 256), bf16), shape((512, 256), bf16)),
        )(packed)

    with jax.named_scope("rows_around"):
        edge = shape((8, breadth + 128), f32)
        near, far, beside = call(
            rows_kernel, (edge, edge, shape((2 * height, 128), f32)), (pltpu.VMEM((128, 128), f32),)
        )(both, near, far, biases[2], packed)
        near, far = swapped(near, far, "gx")

    block = shape((2 * height, breadth), f32)
    padded = pltpu.VMEM((2, rows + 16, breadth + 128), f32)
    with jax.named_scope("advance"):
        inner = call(
            inner_kernel,
            (
                shape((groups - 4, span, 256), bf16),
                shape((groups - 6, span, 256), bf16),
                shape((2, 64, breadth + 128), f32),
            ),
            (padded,),
            flops=5 * 10**8,
        )(both, beside, kernel_1, *others, *biases[:2])
        star = call(
            advance_kernel,
            block,
            (
                padded,
                pltpu.VMEM((4, span, 256), bf16),
                pltpu.VMEM((6, span, 256), bf16),
                pltpu.VMEM((groups - 3, 64, breadth + 128), f32),
            ),
            flops=10**9,
        )(both, beside, near, far, kernel_1, *others, *biases, *inner)

    column, row, twiddle_out, twiddle_home = tables(height, breadth, members_x, members_y)
    column, row = [jnp.asarray(t) for t in column], jnp.asarray(row)
    spectra = call(column_kernel, block)(*gather_y(star), jnp.asarray(twiddle_out), *column)
    factors = call(
        functools.partial(factors_kernel, scale=1.0 / (grid_x * grid_y)), shape((3, grid_x, breadth), f32)
    )()
    columns = call(row_kernel, block, (pltpu.VMEM((grid_x, 2 * breadth), f32),))(
        *gather_x(spectra), factors, row, *column
    )
    part = shape((height, breadth), f32)
    return tuple(call(home_kernel, (part, part))(*gather_y(columns), jnp.asarray(twiddle_home), star))


def solution(mesh):
    return jax.shard_map(
        on_device,
        mesh=mesh,
        in_specs=(P("gx", "gy"), P("gx", "gy"), P(), P(), P(), P(), P(), P()),
        out_specs=(P("gx", "gy"), P("gx", "gy")),
        check_vma=False,
    )
```

```python
import functools
import math

import jax
import jax.numpy as jnp
import ml_dtypes
import numpy as np
from jax import lax
from jax.experimental import pallas as pl
from jax.experimental.pallas import tpu as pltpu
from jax.sharding import PartitionSpec as P

step_ratio = 0.4
stencil_base = (-0.0625, 0.5625, 0.5625, -0.0625)
f32 = jnp.float32
bf16 = jnp.bfloat16

vmem_limit = 48 * 1024 * 1024


def split(value):
    high = value.astype(bf16)
    return high, (value - high.astype(f32)).astype(bf16)


def split_table(table):
    high = table.astype(ml_dtypes.bfloat16)
    low = (table - high.astype(np.float64)).astype(ml_dtypes.bfloat16)
    return high, low


def dot(a, b):
    return jnp.dot(a, b, preferred_element_type=f32)


def product_3(value, high, low):
    rows = value.shape[0]
    first, second = split(value)
    both = dot(jnp.concatenate([first, second], axis=0), high)
    return both[:rows] + both[rows:] + dot(first, low)


def parity(shape):
    rows = lax.broadcasted_iota(jnp.int32, shape, 0)
    return jnp.where(rows < shape[0] // 2, 1.0, -1.0).astype(f32)


def swap(value):
    half = value.shape[0] // 2
    return jnp.concatenate([value[half:], value[:half]], axis=0)


def by_parity(axis, for_even, for_odd):
    return jnp.where(lax.axis_index(axis) % 2 == 0, for_even, for_odd)


def columns_kernel(both_ref, near_ref, far_ref, strip):
    cells, breadth = both_ref.shape
    strip[cells:, :] = jnp.zeros((128 - cells, 128), f32)
    strip[:cells, :] = both_ref[:, :128]
    first = strip[...].T[0:8]
    strip[:cells, :] = both_ref[:, breadth - 128 :]
    last = strip[...].T[120:128]
    near_ref[...] = by_parity("gy", last, first)
    far_ref[...] = by_parity("gy", first, last)


def rows_kernel(both_ref, from_near_ref, from_far_ref, order_ref, order_too_ref, near_ref, far_ref, beside_ref, strip):
    height, breadth = both_ref.shape[0] // 2, both_ref.shape[1]
    from_near, from_far = from_near_ref[...], from_far_ref[...]
    strip[...] = jnp.zeros_like(strip)
    strip[0:4, :] = by_parity("gy", from_near, from_far)[0:4]
    strip[124:128, :] = by_parity("gy", from_far, from_near)[4:8]
    beside = strip[...].T[: 2 * height]
    beside_ref[...] = beside
    whole = jnp.concatenate([both_ref[...], beside], axis=1)
    last = jnp.concatenate([whole[height - 4 : height], whole[2 * height - 4 :]], axis=0)
    first = jnp.concatenate([whole[:4], whole[height : height + 4]], axis=0)
    near_ref[...] = by_parity("gx", last, first)
    far_ref[...] = by_parity("gx", first, last)


def first_weights_kernel(taps_ref, biases_ref, k1_ref, c1_ref, c2_ref, c3_ref, *, rows):
    groups, depth, _ = k1_ref.shape
    wide = [jnp.concatenate([taps_ref[i]] * 4, axis=1) for i in range(9)]
    c1_ref[...] = jnp.concatenate([biases_ref[:, :64]] * 4, axis=1)
    c2_ref[...] = jnp.concatenate([biases_ref[:, 64:128]] * 4, axis=1)
    place = lax.broadcasted_iota(jnp.int32, (64, 16), 0) // 4
    channel = 8 * (place // 8) + 4 * (place % 2) + (place // 2) % 4
    hit = channel == lax.broadcasted_iota(jnp.int32, (64, 16), 1)
    c3_ref[...] = jnp.sum(jnp.where(hit, biases_ref[:, 128:144], 0.0), axis=1, keepdims=True)
    spread = []
    for d in range(3):
        parts = [
            jnp.broadcast_to(wide[3 * d + s][q : q + 1, :], (rows, 256))
            for s in range(3)
            for q in range(2)
        ]
        parts.append(jnp.zeros((depth - 6 * rows, 256), f32))
        spread.append(jnp.concatenate(parts, axis=0))
    row = lax.broadcasted_iota(jnp.int32, (rows, 256), 0) - lax.broadcasted_iota(jnp.int32, (rows, 256), 1) // 64
    row = jnp.where(row < 0, row + rows, row)
    row = jnp.concatenate([row] * 6 + [jnp.full((depth - 6 * rows, 256), -1, jnp.int32)], axis=0)
    for r in range(groups):
        near = [row == (4 * r + d - 1) % rows for d in range(3)]
        block = jnp.where(near[0], spread[0], jnp.where(near[1], spread[1], jnp.where(near[2], spread[2], 0.0)))
        k1_ref[r] = block.astype(bf16)


def other_weights_kernel(packed_ref, order_ref, k2_ref, even_ref, odd_ref):
    slots = {-1: 5, 0: 0, 1: 1, 2: 2, 3: 3, 4: 6}
    blank = jnp.zeros((64, 64), f32)
    for c in range(3):
        taps = [packed_ref[64 * (3 * d + c) : 64 * (3 * d + c) + 64, :].astype(f32) for d in range(3)]
        two = [(taps[0], blank), (taps[1], taps[0]), (taps[2], taps[1]), (blank, taps[2])]
        two = [jnp.concatenate(pair, axis=0).T.astype(bf16) for pair in two]
        for slot, source in enumerate((1, 2, 3, 0)):
            k2_ref[64 * slot : 64 * slot + 64, 128 * c : 128 * c + 128] = two[source]

    taps = [
        [packed_ref[576 + 16 * (3 * d + c) : 592 + 16 * (3 * d + c), :].astype(f32) for d in range(3)]
        for c in range(3)
    ]
    blank = jnp.zeros((16, 64), f32)
    filler = jnp.zeros((64, 256), bf16)
    parts = [filler] * 8
    for k, slot in slots.items():
        pieces = [taps[c][k - t + 1] if 0 <= k - t + 1 < 3 else blank for c in range(3) for t in range(4)]
        pieces += [blank] * 4
        parts[slot] = jnp.concatenate(pieces, axis=0).T.astype(bf16)
    raw = jnp.concatenate(parts, axis=0)
    source = lax.broadcasted_iota(jnp.int32, (256, 256), 0)
    target = lax.broadcasted_iota(jnp.int32, (256, 256), 1)
    inner = target % 64
    place = inner // 4
    channel = 8 * (place // 8) + 4 * (place % 2) + (place // 2) % 4
    lane = 16 * (inner % 4) + channel
    part = target // 64
    column_even = jnp.where(part == 3, -1, 64 * part + lane)
    column_odd = jnp.where(
        part == 2, -1, jnp.where(part == 3, 128 + lane, jnp.where(part == 0, 64 + lane, lane))
    )
    even_ref[...] = dot(raw, jnp.where(source == column_even, 1.0, 0.0).astype(bf16)).astype(bf16)
    odd_ref[...] = dot(raw, jnp.where(source == column_odd, 1.0, 0.0).astype(bf16)).astype(bf16)


def fill(field, both_ref, beside_ref, height, breadth):
    for q in range(2):
        field[q, 8 : 8 + height, :breadth] = both_ref[height * q : height * (q + 1), :]
        field[q, 8 : 8 + height, breadth:] = beside_ref[height * q : height * (q + 1), :]


def patches_of(field, rows, depth):
    lanes = field.shape[2]
    whole = jnp.concatenate([field[0, 8 : 8 + rows], field[1, 8 : 8 + rows]], axis=0)
    pieces = [pltpu.roll(whole, 1, 1), whole, pltpu.roll(whole, lanes - 1, 1)]
    pieces.append(jnp.zeros((depth - 6 * rows, lanes), f32))
    turned = jnp.concatenate(pieces, axis=0).T
    return jnp.concatenate([turned[: lanes - 120], turned[lanes - 8 :]], axis=0).astype(bf16)


def layer_1(patches, weights_ref, bias_ref, r):
    return jnp.maximum(dot(patches, weights_ref[r]) + bias_ref[...], 0.0).astype(bf16)


def with_neighbours(before, own, after, weights_ref):
    beside = jnp.concatenate([before[:, 128:], after[:, :128]], axis=1)
    return dot(own[...], weights_ref[:256]) + dot(beside, weights_ref[256:])


def layer_2(before, own, after, weights_ref, bias_ref):
    span = own.shape[0]
    lower = lax.broadcasted_iota(jnp.int32, (span, 128), 1) < 64
    left, right = own[:, :128], own[:, 128:]
    results = []
    for pair, below, above in ((left, right, before[:, 128:]), (right, after[:, :128], left)):
        total = dot(jnp.concatenate([pair, jnp.where(lower, below, above)], axis=1), weights_ref[...])
        total = pltpu.roll(total[:, :128], 1, 0) + total[:, 128:256] + pltpu.roll(total[:, 256:], span - 1, 0)
        results.append(jnp.maximum(total + bias_ref[:, :128], 0.0).astype(bf16))
    return jnp.concatenate(results, axis=1)


def layer_3(second, groups, r, weights_ref):
    total = with_neighbours(second((r - 1) % groups), second(r), second((r + 1) % groups), weights_ref)
    left_part = total[:, :128]
    return (
        pltpu.roll(left_part, 1, 0)
        + pltpu.roll(left_part, 64, 1)
        + pltpu.roll(total[:, 128:], total.shape[0] - 1, 0)
    )


def coefficients(second, groups, even, odd, even_ref, odd_ref):
    block = layer_3(second, groups, even, even_ref)
    if odd is not None:
        lower = lax.broadcasted_iota(jnp.int32, block.shape, 1) < 64
        block = jnp.where(lower, block, layer_3(second, groups, odd, odd_ref))
    span = block.shape[0]
    filler = jnp.zeros((112, 128), f32)
    return jnp.concatenate([block[: span - 8], filler, block[span - 8 :]], axis=0).T


def inner_kernel(
    both_ref, beside_ref, w1_ref, w2_ref, even_ref, odd_ref, b1_ref, b2_ref, first_ref, second_ref, coeff_ref, field
):
    height, breadth = both_ref.shape[0] // 2, both_ref.shape[1]
    rows = height + 8
    groups = rows // 4
    field[...] = jnp.zeros_like(field)
    fill(field, both_ref, beside_ref, height, breadth)
    patches = patches_of(field, rows, w1_ref.shape[1])
    for r in range(1, groups - 3):
        first_ref[r - 1] = layer_1(patches, w1_ref, b1_ref, r)
        if r >= 3:
            second_ref[r - 3] = layer_2(
                first_ref.at[r - 3], first_ref.at[r - 2], first_ref.at[r - 1], w2_ref, b2_ref
            )
    block = coefficients(lambda r: second_ref.at[r - 2], groups, 3, 4, even_ref, odd_ref)
    coeff_ref[0] = block[:64]
    coeff_ref[1] = block[64:]


def advance_kernel(
    both_ref, beside_ref, from_near_ref, from_far_ref, w1_ref, w2_ref, even_ref, odd_ref, b1_ref, b2_ref, b3_ref,
    first_ref, second_ref, coeff_ref, star_ref, field, outer_first, outer_second, outer_coeff,
):
    height, breadth = both_ref.shape[0] // 2, both_ref.shape[1]
    rows = height + 8
    groups = rows // 4
    lanes = breadth + 128
    fill(field, both_ref, beside_ref, height, breadth)
    from_near, from_far = from_near_ref[...], from_far_ref[...]
    below, above = by_parity("gx", from_near, from_far), by_parity("gx", from_far, from_near)
    for q in range(2):
        field[q, 8 + height : 12 + height, :] = below[4 * q : 4 * q + 4]
        field[q, 12 + height : 16 + height, :] = above[4 * q : 4 * q + 4]
        field[q, 0:8, :] = field[q, rows : rows + 8, :]
        field[q, 8 + rows : 16 + rows, :] = field[q, 8:16, :]
    patches = patches_of(field, rows, w1_ref.shape[1])

    ends = (groups - 3, groups - 2, groups - 1, 0, 1, groups - 4)

    def first(r):
        return outer_first.at[ends.index(r)] if r in ends[:4] else first_ref.at[r - 1]

    def second(r):
        return outer_second.at[ends.index(r)] if r in ends else second_ref.at[r - 2]

    held = {3: coeff_ref.at[0], 4: coeff_ref.at[1]}

    def do_first(r):
        outer_first[ends.index(r)] = layer_1(patches, w1_ref, b1_ref, r)

    def do_second(r):
        outer_second[ends.index(r)] = layer_2(
            first((r - 1) % groups), first(r), first((r + 1) % groups), w2_ref, b2_ref
        )

    def do_coefficients(even, odd):
        block = coefficients(second, groups, even, odd, even_ref, odd_ref)
        for r, part in ((even, block[:64]), (odd, block[64:])):
            if r is not None:
                place = len(held)
                outer_coeff[place - 2] = part
                held[r] = outer_coeff.at[place - 2]

    offsets = b3_ref[...]
    sub = lax.broadcasted_iota(jnp.int32, (8, breadth), 0) % 4

    def stacked(r, shift, qs=(0, 1)):
        start = 8 + 4 * r + shift
        return jnp.concatenate([field[q, start : start + 4, :] for q in qs], axis=0)

    def flows(r, previous):
        weights = held[r][...] + offsets
        weights = [weights[8 * i : 8 * i + 8] for i in range(8)]
        centre = stacked(r, 0)

        def stencil(d):
            four = weights[4 * d : 4 * d + 4]
            mean = (four[0] + four[1] + four[2] + four[3]) * 0.25
            return [base + w - mean for base, w in zip(stencil_base, four)]

        east = stencil(0)
        flow_x = (
            east[0] * stacked(r, -1) + east[1] * centre + east[2] * stacked(r, 1) + east[3] * stacked(r, 2)
        )
        flow_x = flow_x * (0.5 * (stacked(r, 0, (0, 0)) + stacked(r, 1, (0, 0))))
        flow_x = flow_x[:, :breadth]
        if previous is not None:
            north = stencil(1)
            flow_y = (
                north[0] * pltpu.roll(centre, 1, 1)
                + north[1] * centre
                + north[2] * pltpu.roll(centre, lanes - 1, 1)
                + north[3] * pltpu.roll(centre, lanes - 2, 1)
            )
            carrier = stacked(r, 0, (1, 1))
            flow_y = flow_y * (0.5 * (carrier + pltpu.roll(carrier, lanes - 1, 1)))
            change_y = (flow_y - pltpu.roll(flow_y, 1, 1))[:, :breadth]
            above = jnp.where(sub == 0, pltpu.roll(previous, 5, 0), pltpu.roll(flow_x, 1, 0))
            star = centre[:, :breadth] - step_ratio * (flow_x - above + change_y)
            star_ref[4 * r : 4 * r + 4, :] = star[:4]
            star_ref[height + 4 * r : height + 4 * r + 4, :] = star[4:]
        return flow_x

    for r in ends[:4]:
        do_first(r)
    for r in ends[1:5]:
        do_second(r)
    do_coefficients(groups - 1, None)
    do_coefficients(0, 1)
    do_second(groups - 4)
    previous = flows(groups - 1, None)
    previous = flows(0, previous)
    previous = flows(1, previous)
    inner = list(range(5, groups - 4))
    do_coefficients(2, inner[0])
    do_second(groups - 3)
    for r in range(2, 5):
        previous = flows(r, previous)
    do_coefficients(groups - 4, groups - 3)
    for r in range(5, groups - 2):
        previous = flows(r, previous)


def own_twiddle(ref):
    own = ref[lax.axis_index("gy")]
    half = own.shape[0] // 2
    return own[:half], own[half:]


def column_kernel(*refs):
    *blocks, twiddle_ref, high_ref, low_ref, out_ref = refs
    rows, breadth = out_ref.shape
    cosine, sine = own_twiddle(twiddle_ref)
    sign = parity((rows, breadth))
    mixed = None
    for k, ref in enumerate(blocks):
        block = ref[...] * sign
        term = block * cosine[k : k + 1, :] + swap(block) * (sign * sine[k : k + 1, :])
        mixed = term if mixed is None else mixed + term
    spectra = product_3(mixed, high_ref[...], low_ref[...])
    out_ref[...] = spectra[:, :breadth] + sign * swap(spectra[:, breadth:])


def factors_kernel(out_ref, *, scale):
    _, length, breadth = out_ref.shape
    index = lax.broadcasted_iota(jnp.int32, (length, breadth), 0)
    wave_x = jnp.where(index >= length // 2, index - length, index).astype(f32) * (2.0 * math.pi / length)
    members_y = lax.axis_size("gy")
    grid_y = members_y * breadth
    number_y = lax.axis_index("gy") + members_y * lax.broadcasted_iota(jnp.int32, (1, breadth), 1)
    wave_y = jnp.where(number_y >= grid_y // 2, number_y - grid_y, number_y).astype(f32) * (2.0 * math.pi / grid_y)
    edge_y = number_y == grid_y // 2
    edge_x = index == length // 2
    total = wave_x * wave_x + wave_y * wave_y
    zero = total == 0.0
    inverse = scale / jnp.where(zero, 1.0, total)
    same = (0.5 * inverse) * (wave_y * wave_y - wave_x * wave_x)
    cross = jnp.where(edge_x != edge_y, 0.0, -inverse * wave_x * wave_y)
    out_ref[0] = jnp.where(zero, 0.5 * scale, same)
    out_ref[1] = jnp.where(zero, -0.5 * scale, same)
    out_ref[2] = cross


def row_kernel(*refs):
    *blocks, factors_ref, table_ref, high_ref, low_ref, out_ref, gathered = refs
    rows, breadth = out_ref.shape
    height = rows // 2
    length = len(blocks) * height
    own_index = lax.axis_index("gx")
    for k, ref in enumerate(blocks):
        start = pl.multiple_of((own_index ^ k) * height, height)
        gathered[pl.ds(start, height), :breadth] = ref[:height, :]
        gathered[pl.ds(start, height), breadth:] = ref[height:, :]
    data = gathered[...]
    data, data_low = split(data)
    both = dot(table_ref[...], data)
    spectra = both[: 2 * length] + both[2 * length :] + dot(table_ref[: 2 * length], data_low)
    real_part = spectra[:length, :breadth] + spectra[length:, breadth:]
    imag_part = spectra[:length, breadth:] - spectra[length:, :breadth]
    same_real, same_imag, cross = factors_ref[0], factors_ref[1], factors_ref[2]
    kept_real = same_real * real_part - cross * imag_part
    kept_imag = same_imag * imag_part + cross * real_part
    kept, kept_low = split(jnp.concatenate([kept_real, kept_imag], axis=1))
    start = pl.multiple_of(own_index * height, height)

    table = jnp.concatenate(
        [table_ref[pl.ds(pl.multiple_of(part * length + start, height), height), :] for part in range(4)], axis=0
    )
    both = dot(table, kept)
    home = both[: 2 * height] + both[2 * height :] + dot(table[: 2 * height], kept_low)
    home = jnp.concatenate(
        [
            home[:height, :breadth] - home[height:, breadth:],
            home[:height, breadth:] + home[height:, :breadth],
        ],
        axis=0,
    )
    columns = product_3(home, high_ref[...], low_ref[...])
    out_ref[...] = columns[:, :breadth] - parity((rows, breadth)) * swap(columns[:, breadth:])


def home_kernel(*refs):
    *blocks, twiddle_ref, star_ref, u_ref, v_ref = refs
    rows, breadth = star_ref.shape
    cosine, sine = own_twiddle(twiddle_ref)
    sign = parity((rows, breadth))
    result = 0.5 * star_ref[...]
    for k, ref in enumerate(blocks):
        block = ref[...]
        result = result + block * cosine[k : k + 1, :] - swap(block) * (sign * sine[k : k + 1, :])
    u_ref[...] = result[: rows // 2]
    v_ref[...] = result[rows // 2 :]


def call(kernel, shapes, scratch=(), flops=10**7):
    return pl.pallas_call(
        kernel,
        out_shape=shapes,
        scratch_shapes=list(scratch),
        compiler_params=pltpu.CompilerParams(vmem_limit_bytes=vmem_limit),
        cost_estimate=pl.CostEstimate(flops=flops, bytes_accessed=2**20, transcendentals=0),
    )


@functools.lru_cache(None)
def tables(height, breadth, members_x, members_y):
    turn = 2.0 * math.pi
    j = np.arange(breadth)
    phase = turn * (np.outer(j, j) % breadth) / breadth
    column = split_table(np.concatenate([np.cos(phase), np.sin(phase)], axis=1))
    length = height * members_x
    k = np.arange(length)
    phase = turn * (np.outer(k, k) % length) / length
    row = np.concatenate(split_table(np.concatenate([np.cos(phase), np.sin(phase)], axis=0)), axis=0)
    g = np.arange(members_y)[:, None, None]
    partner = g ^ np.arange(members_y)[None, :, None]
    whole = breadth * members_y
    out = turn * ((partner * breadth + j) * g % whole) / whole
    home = turn * ((g * breadth + j) * partner % whole) / whole
    twiddle_out, twiddle_home = [
        np.concatenate([np.cos(phase), np.sin(phase)], axis=1).astype(np.float32) for phase in (out, home)
    ]
    return column, row, twiddle_out, twiddle_home


def partner(block, axis, k):
    return lax.ppermute(block, axis, [(i, i ^ k) for i in range(lax.axis_size(axis))])


def gather_y(block):
    return [block] + [partner(block, "gy", k) for k in range(1, lax.axis_size("gy"))]


def gather_x(block):
    own = [block] + [partner(block, "gx", k) for k in range(2, lax.axis_size("gx"), 2)]
    return [other for held in own for other in (held, partner(held, "gx", 1))]


def on_device(u_field, v_field, w_first, b_first, w_second, b_second, w_third, b_third):
    height, breadth = u_field.shape
    members_x, members_y = lax.axis_size("gx"), lax.axis_size("gy")
    grid_x, grid_y = height * members_x, breadth * members_y
    rows = height + 8
    groups = rows // 4
    span = breadth + 16
    shape = jax.ShapeDtypeStruct

    def swapped(near, far, axis):
        peers = lax.axis_size(axis)
        after, before = lambda i: (i + 1) % peers, lambda i: (i - 1) % peers
        pairs = [(i, before(i) if i % 2 else after(i)) for i in range(peers)]
        other_pairs = [(i, after(i) if i % 2 else before(i)) for i in range(peers)]
        return lax.ppermute(near, axis, pairs), lax.ppermute(far, axis, other_pairs)

    with jax.named_scope("columns_around"):
        both = jnp.stack([u_field, v_field]).reshape(2 * height, breadth)
        edge = shape((8, 128), f32)
        near, far = call(columns_kernel, (edge, edge), (pltpu.VMEM((128, 128), f32),))(both)
        near, far = swapped(near, far, "gy")

    with jax.named_scope("weights"):
        taps = w_first.transpose(0, 2, 1).astype(f32)
        biases = jnp.concatenate([b_first, b_second, b_third])[None]
        kernel_1, *biases = call(
            functools.partial(first_weights_kernel, rows=rows),
            (
                shape((groups, -(-6 * rows // 128) * 128, 256), bf16),
                shape((1, 256), f32),
                shape((1, 256), f32),
                shape((64, 1), f32),
            ),
        )(taps, biases)
        packed = jnp.concatenate([w_second.reshape(576, 64), w_third.reshape(144, 64)], axis=0)

    with jax.named_scope("rows_around"):
        edge = shape((8, breadth + 128), f32)
        near, far, beside = call(
            rows_kernel, (edge, edge, shape((2 * height, 128), f32)), (pltpu.VMEM((128, 128), f32),)
        )(both, near, far, biases[2], packed)
        near, far = swapped(near, far, "gx")

    with jax.named_scope("weights"):
        others = call(
            other_weights_kernel,
            (shape((256, 384), bf16), shape((512, 256), bf16), shape((512, 256), bf16)),
        )(packed, beside)

    block = shape((2 * height, breadth), f32)
    padded = pltpu.VMEM((2, rows + 16, breadth + 128), f32)
    with jax.named_scope("advance"):
        inner = call(
            inner_kernel,
            (
                shape((groups - 4, span, 256), bf16),
                shape((groups - 6, span, 256), bf16),
                shape((2, 64, breadth + 128), f32),
            ),
            (padded,),
            flops=5 * 10**8,
        )(both, beside, kernel_1, *others, *biases[:2])
        star = call(
            advance_kernel,
            block,
            (
                padded,
                pltpu.VMEM((4, span, 256), bf16),
                pltpu.VMEM((6, span, 256), bf16),
                pltpu.VMEM((groups - 3, 64, breadth + 128), f32),
            ),
            flops=10**9,
        )(both, beside, near, far, kernel_1, *others, *biases, *inner)

    column, row, twiddle_out, twiddle_home = tables(height, breadth, members_x, members_y)
    column, row = [jnp.asarray(t) for t in column], jnp.asarray(row)
    spectra = call(column_kernel, block)(*gather_y(star), jnp.asarray(twiddle_out), *column)
    factors = call(
        functools.partial(factors_kernel, scale=1.0 / (grid_x * grid_y)), shape((3, grid_x, breadth), f32)
    )()
    columns = call(row_kernel, block, (pltpu.VMEM((grid_x, 2 * breadth), f32),))(
        *gather_x(spectra), factors, row, *column
    )
    part = shape((height, breadth), f32)
    return tuple(call(home_kernel, (part, part))(*gather_y(columns), jnp.asarray(twiddle_home), star))


def solution(mesh):
    return jax.shard_map(
        on_device,
        mesh=mesh,
        in_specs=(P("gx", "gy"), P("gx", "gy"), P(), P(), P(), P(), P(), P()),
        out_specs=(P("gx", "gy"), P("gx", "gy")),
        check_vma=False,
    )
```

```python
import functools
import math

import jax
import jax.numpy as jnp
import ml_dtypes
import numpy as np
from jax import lax
from jax.experimental import pallas as pl
from jax.experimental.pallas import tpu as pltpu
from jax.sharding import PartitionSpec as P

step_ratio = 0.4
stencil_base = (-0.0625, 0.5625, 0.5625, -0.0625)
f32 = jnp.float32
bf16 = jnp.bfloat16

vmem_limit = 48 * 1024 * 1024


def split(value):
    high = value.astype(bf16)
    return high, (value - high.astype(f32)).astype(bf16)


def split_table(table):
    high = table.astype(ml_dtypes.bfloat16)
    low = (table - high.astype(np.float64)).astype(ml_dtypes.bfloat16)
    return high, low


def dot(a, b):
    return jnp.dot(a, b, preferred_element_type=f32)


def product_3(value, high, low):
    rows = value.shape[0]
    first, second = split(value)
    both = dot(jnp.concatenate([first, second], axis=0), high)
    return both[:rows] + both[rows:] + dot(first, low)


def parity(shape):
    rows = lax.broadcasted_iota(jnp.int32, shape, 0)
    return jnp.where(rows < shape[0] // 2, 1.0, -1.0).astype(f32)


def swap(value):
    half = value.shape[0] // 2
    return jnp.concatenate([value[half:], value[:half]], axis=0)


def by_parity(axis, for_even, for_odd):
    return jnp.where(lax.axis_index(axis) % 2 == 0, for_even, for_odd)


def columns_kernel(both_ref, near_ref, far_ref, strip):
    cells, breadth = both_ref.shape
    strip[cells:, :] = jnp.zeros((128 - cells, 128), f32)
    strip[:cells, :] = both_ref[:, :128]
    first = strip[...].T[0:8]
    strip[:cells, :] = both_ref[:, breadth - 128 :]
    last = strip[...].T[120:128]
    near_ref[...] = by_parity("gy", last, first)
    far_ref[...] = by_parity("gy", first, last)


def rows_kernel(both_ref, from_near_ref, from_far_ref, order_ref, order_too_ref, near_ref, far_ref, beside_ref, strip):
    height, breadth = both_ref.shape[0] // 2, both_ref.shape[1]
    from_near, from_far = from_near_ref[...], from_far_ref[...]
    strip[...] = jnp.zeros_like(strip)
    strip[0:4, :] = by_parity("gy", from_near, from_far)[0:4]
    strip[124:128, :] = by_parity("gy", from_far, from_near)[4:8]
    beside = strip[...].T[: 2 * height]
    beside_ref[...] = beside
    whole = jnp.concatenate([both_ref[...], beside], axis=1)
    last = jnp.concatenate([whole[height - 4 : height], whole[2 * height - 4 :]], axis=0)
    first = jnp.concatenate([whole[:4], whole[height : height + 4]], axis=0)
    near_ref[...] = by_parity("gx", last, first)
    far_ref[...] = by_parity("gx", first, last)


def first_weights_kernel(taps_ref, biases_ref, k1_ref, c1_ref, c2_ref, c3_ref, *, rows):
    groups, depth, _ = k1_ref.shape
    wide = [jnp.concatenate([taps_ref[i]] * 4, axis=1) for i in range(9)]
    c1_ref[...] = jnp.concatenate([biases_ref[:, :64]] * 4, axis=1)
    c2_ref[...] = jnp.concatenate([biases_ref[:, 64:128]] * 4, axis=1)
    place = lax.broadcasted_iota(jnp.int32, (64, 16), 0) // 4
    channel = 8 * (place // 8) + 4 * (place % 2) + (place // 2) % 4
    hit = channel == lax.broadcasted_iota(jnp.int32, (64, 16), 1)
    c3_ref[...] = jnp.sum(jnp.where(hit, biases_ref[:, 128:144], 0.0), axis=1, keepdims=True)
    spread = []
    for d in range(3):
        parts = [
            jnp.broadcast_to(wide[3 * d + s][q : q + 1, :], (rows, 256))
            for s in range(3)
            for q in range(2)
        ]
        parts.append(jnp.zeros((depth - 6 * rows, 256), f32))
        spread.append(jnp.concatenate(parts, axis=0))
    row = lax.broadcasted_iota(jnp.int32, (rows, 256), 0) - lax.broadcasted_iota(jnp.int32, (rows, 256), 1) // 64
    row = jnp.where(row < 0, row + rows, row)
    row = jnp.concatenate([row] * 6 + [jnp.full((depth - 6 * rows, 256), -1, jnp.int32)], axis=0)
    for r in range(groups):
        near = [row == (4 * r + d - 1) % rows for d in range(3)]
        block = jnp.where(near[0], spread[0], jnp.where(near[1], spread[1], jnp.where(near[2], spread[2], 0.0)))
        k1_ref[r] = block.astype(bf16)


def other_weights_kernel(packed_ref, k2_ref, even_ref, odd_ref):
    slots = {-1: 5, 0: 0, 1: 1, 2: 2, 3: 3, 4: 6}
    blank = jnp.zeros((64, 64), f32)
    for c in range(3):
        taps = [packed_ref[64 * (3 * d + c) : 64 * (3 * d + c) + 64, :].astype(f32) for d in range(3)]
        two = [(taps[0], blank), (taps[1], taps[0]), (taps[2], taps[1]), (blank, taps[2])]
        two = [jnp.concatenate(pair, axis=0).T.astype(bf16) for pair in two]
        for slot, source in enumerate((1, 2, 3, 0)):
            k2_ref[64 * slot : 64 * slot + 64, 128 * c : 128 * c + 128] = two[source]

    taps = [
        [packed_ref[576 + 16 * (3 * d + c) : 592 + 16 * (3 * d + c), :].astype(f32) for d in range(3)]
        for c in range(3)
    ]
    blank = jnp.zeros((16, 64), f32)
    filler = jnp.zeros((64, 256), bf16)
    parts = [filler] * 8
    for k, slot in slots.items():
        pieces = [taps[c][k - t + 1] if 0 <= k - t + 1 < 3 else blank for c in range(3) for t in range(4)]
        pieces += [blank] * 4
        parts[slot] = jnp.concatenate(pieces, axis=0).T.astype(bf16)
    raw = jnp.concatenate(parts, axis=0)
    source = lax.broadcasted_iota(jnp.int32, (256, 256), 0)
    target = lax.broadcasted_iota(jnp.int32, (256, 256), 1)
    inner = target % 64
    place = inner // 4
    channel = 8 * (place // 8) + 4 * (place % 2) + (place // 2) % 4
    lane = 16 * (inner % 4) + channel
    part = target // 64
    column_even = jnp.where(part == 3, -1, 64 * part + lane)
    column_odd = jnp.where(
        part == 2, -1, jnp.where(part == 3, 128 + lane, jnp.where(part == 0, 64 + lane, lane))
    )
    even_ref[...] = dot(raw, jnp.where(source == column_even, 1.0, 0.0).astype(bf16)).astype(bf16)
    odd_ref[...] = dot(raw, jnp.where(source == column_odd, 1.0, 0.0).astype(bf16)).astype(bf16)


def fill(field, both_ref, beside_ref, height, breadth):
    for q in range(2):
        field[q, 8 : 8 + height, :breadth] = both_ref[height * q : height * (q + 1), :]
        field[q, 8 : 8 + height, breadth:] = beside_ref[height * q : height * (q + 1), :]


def patches_of(field, rows, depth):
    lanes = field.shape[2]
    whole = jnp.concatenate([field[0, 8 : 8 + rows], field[1, 8 : 8 + rows]], axis=0)
    pieces = [pltpu.roll(whole, 1, 1), whole, pltpu.roll(whole, lanes - 1, 1)]
    pieces.append(jnp.zeros((depth - 6 * rows, lanes), f32))
    turned = jnp.concatenate(pieces, axis=0).T
    return jnp.concatenate([turned[: lanes - 120], turned[lanes - 8 :]], axis=0).astype(bf16)


def layer_1(patches, weights_ref, bias_ref, r):
    return jnp.maximum(dot(patches, weights_ref[r]) + bias_ref[...], 0.0).astype(bf16)


def with_neighbours(before, own, after, weights_ref):
    beside = jnp.concatenate([before[:, 128:], after[:, :128]], axis=1)
    return dot(own[...], weights_ref[:256]) + dot(beside, weights_ref[256:])


def layer_2(before, own, after, weights_ref, bias_ref):
    span = own.shape[0]
    lower = lax.broadcasted_iota(jnp.int32, (span, 128), 1) < 64
    left, right = own[:, :128], own[:, 128:]
    results = []
    for pair, below, above in ((left, right, before[:, 128:]), (right, after[:, :128], left)):
        total = dot(jnp.concatenate([pair, jnp.where(lower, below, above)], axis=1), weights_ref[...])
        total = pltpu.roll(total[:, :128], 1, 0) + total[:, 128:256] + pltpu.roll(total[:, 256:], span - 1, 0)
        results.append(jnp.maximum(total + bias_ref[:, :128], 0.0).astype(bf16))
    return jnp.concatenate(results, axis=1)


def layer_3(second, groups, r, weights_ref):
    total = with_neighbours(second((r - 1) % groups), second(r), second((r + 1) % groups), weights_ref)
    left_part = total[:, :128]
    return (
        pltpu.roll(left_part, 1, 0)
        + pltpu.roll(left_part, 64, 1)
        + pltpu.roll(total[:, 128:], total.shape[0] - 1, 0)
    )


def coefficients(second, groups, even, odd, even_ref, odd_ref):
    block = layer_3(second, groups, even, even_ref)
    if odd is not None:
        lower = lax.broadcasted_iota(jnp.int32, block.shape, 1) < 64
        block = jnp.where(lower, block, layer_3(second, groups, odd, odd_ref))
    span = block.shape[0]
    filler = jnp.zeros((112, 128), f32)
    return jnp.concatenate([block[: span - 8], filler, block[span - 8 :]], axis=0).T


def inner_kernel(
    both_ref, beside_ref, w1_ref, w2_ref, even_ref, odd_ref, b1_ref, b2_ref, first_ref, second_ref, coeff_ref, field
):
    height, breadth = both_ref.shape[0] // 2, both_ref.shape[1]
    rows = height + 8
    groups = rows // 4
    field[...] = jnp.zeros_like(field)
    fill(field, both_ref, beside_ref, height, breadth)
    patches = patches_of(field, rows, w1_ref.shape[1])
    for r in range(1, groups - 3):
        first_ref[r - 1] = layer_1(patches, w1_ref, b1_ref, r)
        if r >= 3:
            second_ref[r - 3] = layer_2(
                first_ref.at[r - 3], first_ref.at[r - 2], first_ref.at[r - 1], w2_ref, b2_ref
            )
    block = coefficients(lambda r: second_ref.at[r - 2], groups, 3, 4, even_ref, odd_ref)
    coeff_ref[0] = block[:64]
    coeff_ref[1] = block[64:]


def advance_kernel(
    both_ref, beside_ref, from_near_ref, from_far_ref, w1_ref, w2_ref, even_ref, odd_ref, b1_ref, b2_ref, b3_ref,
    first_ref, second_ref, coeff_ref, star_ref, field, outer_first, outer_second, outer_coeff,
):
    height, breadth = both_ref.shape[0] // 2, both_ref.shape[1]
    rows = height + 8
    groups = rows // 4
    lanes = breadth + 128
    fill(field, both_ref, beside_ref, height, breadth)
    from_near, from_far = from_near_ref[...], from_far_ref[...]
    below, above = by_parity("gx", from_near, from_far), by_parity("gx", from_far, from_near)
    for q in range(2):
        field[q, 8 + height : 12 + height, :] = below[4 * q : 4 * q + 4]
        field[q, 12 + height : 16 + height, :] = above[4 * q : 4 * q + 4]
        field[q, 0:8, :] = field[q, rows : rows + 8, :]
        field[q, 8 + rows : 16 + rows, :] = field[q, 8:16, :]
    patches = patches_of(field, rows, w1_ref.shape[1])

    ends = (groups - 3, groups - 2, groups - 1, 0, 1, groups - 4)

    def first(r):
        return outer_first.at[ends.index(r)] if r in ends[:4] else first_ref.at[r - 1]

    def second(r):
        return outer_second.at[ends.index(r)] if r in ends else second_ref.at[r - 2]

    held = {3: coeff_ref.at[0], 4: coeff_ref.at[1]}

    def do_first(r):
        outer_first[ends.index(r)] = layer_1(patches, w1_ref, b1_ref, r)

    def do_second(r):
        outer_second[ends.index(r)] = layer_2(
            first((r - 1) % groups), first(r), first((r + 1) % groups), w2_ref, b2_ref
        )

    def do_coefficients(even, odd):
        block = coefficients(second, groups, even, odd, even_ref, odd_ref)
        for r, part in ((even, block[:64]), (odd, block[64:])):
            if r is not None:
                place = len(held)
                outer_coeff[place - 2] = part
                held[r] = outer_coeff.at[place - 2]

    offsets = b3_ref[...]
    sub = lax.broadcasted_iota(jnp.int32, (8, breadth), 0) % 4

    def stacked(r, shift, qs=(0, 1)):
        start = 8 + 4 * r + shift
        return jnp.concatenate([field[q, start : start + 4, :] for q in qs], axis=0)

    def flows(r, previous):
        weights = held[r][...] + offsets
        weights = [weights[8 * i : 8 * i + 8] for i in range(8)]
        centre = stacked(r, 0)

        def stencil(d):
            four = weights[4 * d : 4 * d + 4]
            mean = (four[0] + four[1] + four[2] + four[3]) * 0.25
            return [base + w - mean for base, w in zip(stencil_base, four)]

        east = stencil(0)
        flow_x = (
            east[0] * stacked(r, -1) + east[1] * centre + east[2] * stacked(r, 1) + east[3] * stacked(r, 2)
        )
        flow_x = flow_x * (0.5 * (stacked(r, 0, (0, 0)) + stacked(r, 1, (0, 0))))
        flow_x = flow_x[:, :breadth]
        if previous is not None:
            north = stencil(1)
            flow_y = (
                north[0] * pltpu.roll(centre, 1, 1)
                + north[1] * centre
                + north[2] * pltpu.roll(centre, lanes - 1, 1)
                + north[3] * pltpu.roll(centre, lanes - 2, 1)
            )
            carrier = stacked(r, 0, (1, 1))
            flow_y = flow_y * (0.5 * (carrier + pltpu.roll(carrier, lanes - 1, 1)))
            change_y = (flow_y - pltpu.roll(flow_y, 1, 1))[:, :breadth]
            above = jnp.where(sub == 0, pltpu.roll(previous, 5, 0), pltpu.roll(flow_x, 1, 0))
            star = centre[:, :breadth] - step_ratio * (flow_x - above + change_y)
            star_ref[4 * r : 4 * r + 4, :] = star[:4]
            star_ref[height + 4 * r : height + 4 * r + 4, :] = star[4:]
        return flow_x

    for r in ends[:4]:
        do_first(r)
    for r in ends[1:5]:
        do_second(r)
    do_coefficients(groups - 1, None)
    do_coefficients(0, 1)
    do_second(groups - 4)
    previous = flows(groups - 1, None)
    previous = flows(0, previous)
    previous = flows(1, previous)
    inner = list(range(5, groups - 4))
    do_coefficients(2, inner[0])
    do_second(groups - 3)
    for r in range(2, 5):
        previous = flows(r, previous)
    do_coefficients(groups - 4, groups - 3)
    for r in range(5, groups - 2):
        previous = flows(r, previous)


def own_twiddle(ref):
    own = ref[lax.axis_index("gy")]
    half = own.shape[0] // 2
    return own[:half], own[half:]


def column_kernel(*refs):
    *blocks, twiddle_ref, high_ref, low_ref, out_ref = refs
    rows, breadth = out_ref.shape
    cosine, sine = own_twiddle(twiddle_ref)
    sign = parity((rows, breadth))
    mixed = None
    for k, ref in enumerate(blocks):
        block = ref[...] * sign
        term = block * cosine[k : k + 1, :] + swap(block) * (sign * sine[k : k + 1, :])
        mixed = term if mixed is None else mixed + term
    spectra = product_3(mixed, high_ref[...], low_ref[...])
    out_ref[...] = spectra[:, :breadth] + sign * swap(spectra[:, breadth:])


def factors_kernel(out_ref, *, scale):
    _, length, breadth = out_ref.shape
    index = lax.broadcasted_iota(jnp.int32, (length, breadth), 0)
    wave_x = jnp.where(index >= length // 2, index - length, index).astype(f32) * (2.0 * math.pi / length)
    members_y = lax.axis_size("gy")
    grid_y = members_y * breadth
    number_y = lax.axis_index("gy") + members_y * lax.broadcasted_iota(jnp.int32, (1, breadth), 1)
    wave_y = jnp.where(number_y >= grid_y // 2, number_y - grid_y, number_y).astype(f32) * (2.0 * math.pi / grid_y)
    edge_y = number_y == grid_y // 2
    edge_x = index == length // 2
    total = wave_x * wave_x + wave_y * wave_y
    zero = total == 0.0
    inverse = scale / jnp.where(zero, 1.0, total)
    same = (0.5 * inverse) * (wave_y * wave_y - wave_x * wave_x)
    cross = jnp.where(edge_x != edge_y, 0.0, -inverse * wave_x * wave_y)
    out_ref[0] = jnp.where(zero, 0.5 * scale, same)
    out_ref[1] = jnp.where(zero, -0.5 * scale, same)
    out_ref[2] = cross


def row_kernel(*refs):
    *blocks, factors_ref, table_ref, high_ref, low_ref, out_ref, gathered = refs
    rows, breadth = out_ref.shape
    height = rows // 2
    length = len(blocks) * height
    own_index = lax.axis_index("gx")
    for k, ref in enumerate(blocks):
        start = pl.multiple_of((own_index ^ k) * height, height)
        gathered[pl.ds(start, height), :breadth] = ref[:height, :]
        gathered[pl.ds(start, height), breadth:] = ref[height:, :]
    data = gathered[...]
    data, data_low = split(data)
    both = dot(table_ref[...], data)
    spectra = both[: 2 * length] + both[2 * length :] + dot(table_ref[: 2 * length], data_low)
    real_part = spectra[:length, :breadth] + spectra[length:, breadth:]
    imag_part = spectra[:length, breadth:] - spectra[length:, :breadth]
    same_real, same_imag, cross = factors_ref[0], factors_ref[1], factors_ref[2]
    kept_real = same_real * real_part - cross * imag_part
    kept_imag = same_imag * imag_part + cross * real_part
    kept, kept_low = split(jnp.concatenate([kept_real, kept_imag], axis=1))
    start = pl.multiple_of(own_index * height, height)

    table = jnp.concatenate(
        [table_ref[pl.ds(pl.multiple_of(part * length + start, height), height), :] for part in range(4)], axis=0
    )
    both = dot(table, kept)
    home = both[: 2 * height] + both[2 * height :] + dot(table[: 2 * height], kept_low)
    home = jnp.concatenate(
        [
            home[:height, :breadth] - home[height:, breadth:],
            home[:height, breadth:] + home[height:, :breadth],
        ],
        axis=0,
    )
    columns = product_3(home, high_ref[...], low_ref[...])
    out_ref[...] = columns[:, :breadth] - parity((rows, breadth)) * swap(columns[:, breadth:])


def home_kernel(*refs):
    *blocks, twiddle_ref, star_ref, u_ref, v_ref = refs
    rows, breadth = star_ref.shape
    cosine, sine = own_twiddle(twiddle_ref)
    sign = parity((rows, breadth))
    result = 0.5 * star_ref[...]
    for k, ref in enumerate(blocks):
        block = ref[...]
        result = result + block * cosine[k : k + 1, :] - swap(block) * (sign * sine[k : k + 1, :])
    u_ref[...] = result[: rows // 2]
    v_ref[...] = result[rows // 2 :]


def call(kernel, shapes, scratch=(), flops=10**7):
    return pl.pallas_call(
        kernel,
        out_shape=shapes,
        scratch_shapes=list(scratch),
        compiler_params=pltpu.CompilerParams(vmem_limit_bytes=vmem_limit),
        cost_estimate=pl.CostEstimate(flops=flops, bytes_accessed=2**20, transcendentals=0),
    )


@functools.lru_cache(None)
def tables(height, breadth, members_x, members_y):
    turn = 2.0 * math.pi
    j = np.arange(breadth)
    phase = turn * (np.outer(j, j) % breadth) / breadth
    column = split_table(np.concatenate([np.cos(phase), np.sin(phase)], axis=1))
    length = height * members_x
    k = np.arange(length)
    phase = turn * (np.outer(k, k) % length) / length
    row = np.concatenate(split_table(np.concatenate([np.cos(phase), np.sin(phase)], axis=0)), axis=0)
    g = np.arange(members_y)[:, None, None]
    partner = g ^ np.arange(members_y)[None, :, None]
    whole = breadth * members_y
    out = turn * ((partner * breadth + j) * g % whole) / whole
    home = turn * ((g * breadth + j) * partner % whole) / whole
    twiddle_out, twiddle_home = [
        np.concatenate([np.cos(phase), np.sin(phase)], axis=1).astype(np.float32) for phase in (out, home)
    ]
    return column, row, twiddle_out, twiddle_home


def partner(block, axis, k):
    return lax.ppermute(block, axis, [(i, i ^ k) for i in range(lax.axis_size(axis))])


def gather_y(block):
    return [block] + [partner(block, "gy", k) for k in range(1, lax.axis_size("gy"))]


def gather_x(block):
    far_first = [partner(block, "gx", k) for k in reversed(range(2, lax.axis_size("gx"), 2))]
    own = [block] + far_first[::-1]
    return [other for held in own for other in (held, partner(held, "gx", 1))]


def on_device(u_field, v_field, w_first, b_first, w_second, b_second, w_third, b_third):
    height, breadth = u_field.shape
    members_x, members_y = lax.axis_size("gx"), lax.axis_size("gy")
    grid_x, grid_y = height * members_x, breadth * members_y
    rows = height + 8
    groups = rows // 4
    span = breadth + 16
    shape = jax.ShapeDtypeStruct

    def swapped(near, far, axis):
        peers = lax.axis_size(axis)
        after, before = lambda i: (i + 1) % peers, lambda i: (i - 1) % peers
        pairs = [(i, before(i) if i % 2 else after(i)) for i in range(peers)]
        other_pairs = [(i, after(i) if i % 2 else before(i)) for i in range(peers)]
        return lax.ppermute(near, axis, pairs), lax.ppermute(far, axis, other_pairs)

    with jax.named_scope("columns_around"):
        both = jnp.stack([u_field, v_field]).reshape(2 * height, breadth)
        edge = shape((8, 128), f32)
        near, far = call(columns_kernel, (edge, edge), (pltpu.VMEM((128, 128), f32),))(both)
        near, far = swapped(near, far, "gy")

    with jax.named_scope("weights"):
        taps = w_first.transpose(0, 2, 1).astype(f32)
        biases = jnp.concatenate([b_first, b_second, b_third])[None]
        kernel_1, *biases = call(
            functools.partial(first_weights_kernel, rows=rows),
            (
                shape((groups, -(-6 * rows // 128) * 128, 256), bf16),
                shape((1, 256), f32),
                shape((1, 256), f32),
                shape((64, 1), f32),
            ),
        )(taps, biases)
        packed = jnp.concatenate([w_second.reshape(576, 64), w_third.reshape(144, 64)], axis=0)
        others = call(
            other_weights_kernel,
            (shape((256, 384), bf16), shape((512, 256), bf16), shape((512, 256), bf16)),
        )(packed)

    with jax.named_scope("rows_around"):
        edge = shape((8, breadth + 128), f32)
        near, far, beside = call(
            rows_kernel, (edge, edge, shape((2 * height, 128), f32)), (pltpu.VMEM((128, 128), f32),)
        )(both, near, far, biases[2], packed)
        near, far = swapped(near, far, "gx")

    block = shape((2 * height, breadth), f32)
    padded = pltpu.VMEM((2, rows + 16, breadth + 128), f32)
    with jax.named_scope("advance"):
        inner = call(
            inner_kernel,
            (
                shape((groups - 4, span, 256), bf16),
                shape((groups - 6, span, 256), bf16),
                shape((2, 64, breadth + 128), f32),
            ),
            (padded,),
            flops=5 * 10**8,
        )(both, beside, kernel_1, *others, *biases[:2])
        star = call(
            advance_kernel,
            block,
            (
                padded,
                pltpu.VMEM((4, span, 256), bf16),
                pltpu.VMEM((6, span, 256), bf16),
                pltpu.VMEM((groups - 3, 64, breadth + 128), f32),
            ),
            flops=10**9,
        )(both, beside, near, far, kernel_1, *others, *biases, *inner)

    column, row, twiddle_out, twiddle_home = tables(height, breadth, members_x, members_y)
    column, row = [jnp.asarray(t) for t in column], jnp.asarray(row)
    spectra = call(column_kernel, block)(*gather_y(star), jnp.asarray(twiddle_out), *column)
    factors = call(
        functools.partial(factors_kernel, scale=1.0 / (grid_x * grid_y)), shape((3, grid_x, breadth), f32)
    )()
    columns = call(row_kernel, block, (pltpu.VMEM((grid_x, 2 * breadth), f32),))(
        *gather_x(spectra), factors, row, *column
    )
    part = shape((height, breadth), f32)
    return tuple(call(home_kernel, (part, part))(*gather_y(columns), jnp.asarray(twiddle_home), star))


def solution(mesh):
    return jax.shard_map(
        on_device,
        mesh=mesh,
        in_specs=(P("gx", "gy"), P("gx", "gy"), P(), P(), P(), P(), P(), P()),
        out_specs=(P("gx", "gy"), P("gx", "gy")),
        check_vma=False,
    )
```
